32 devices in a mesh: ctx: 8 (over z, x), tp: 4 (over y, core).
Axes of the slice: x: 2, y: 2, z: 4, core: 2. Of those that a mesh axis runs over, the one named last changes fastest.
Arguments:
- residual: bfloat16 [2048, 8192], P('ctx', 'tp'), may hold values from -40 to 40
- query_in: bfloat16 [2048, 8192], P('ctx', 'tp'), may hold values from -6 to 6
- key_in: bfloat16 [2048, 8192], P('ctx', 'tp'), may hold values from -6 to 6
- value_in: bfloat16 [2048, 8192], P('ctx', 'tp'), may hold values from -6 to 6
- short_filter: float32 [3, 7, 8192], P(None, None, 'tp'), may hold values from -2 to 2
- residues: float32 [16, 8192], P(None, 'tp'), may hold values from -0.32 to 0.32
- decay_rate: float32 [16, 8192], P(None, 'tp'), may hold values from 9.765625e-05 to 0.05
- skip_gain: float32 [8192], P('tp'), may hold values from 0.5 to 1.5
- norm_gain: float32 [8192], P('tp'), may hold values from 0.5 to 1.5
- cotangent: bfloat16 [2048, 8192], P('ctx', 'tp'), may hold values from -6 to 6
Outputs:
- normed: bfloat16 [2048, 8192], P('ctx', 'tp')
- grad_residual: bfloat16 [2048, 8192], P('ctx', 'tp')
- grad_query: bfloat16 [2048, 8192], P('ctx', 'tp')
- grad_key: bfloat16 [2048, 8192], P('ctx', 'tp')
- grad_value: bfloat16 [2048, 8192], P('ctx', 'tp')
- grad_short: float32 [3, 7, 8192], P(None, None, 'tp')
- grad_residues: float32 [16, 8192], P(None, 'tp')
- grad_rate: float32 [16, 8192], P(None, 'tp')
- grad_skip: float32 [8192], P('tp')
- grad_norm_gain: float32 [8192], P('tp')
The draws below stay inside these ranges and needn't reach their ends.
All inputs are finite; a program needn't handle non-finite values.
Results may differ from the reference program's by a relative error of at most 0.002.
Values may be sent and summed in bfloat16 or wider, within the bound.
No kernel may reach another device: no remote copies, remote signals or barrier semaphores. Data moves between devices by JAX's collectives and lax.ppermute only.
A program may use at most 128 MiB of HBM per device.

```python
import math
import jax
import jax.numpy as jnp
from jax import lax

D = 8192
M = 16
KS = 7
TOK_DEV = 256
SEQ = 2048


def modal_pair(key):
    pick_key = jax.random.fold_in(key, 101)
    place_key = jax.random.fold_in(key, 202)
    sign_key = jax.random.fold_in(key, 303)
    slow_share = 0.5
    is_slow = jax.random.uniform(pick_key, (M, D)) < slow_share
    position = jax.random.uniform(place_key, (M, D))
    slow_low = math.log(0.2 / SEQ)
    slow_high = math.log(2.0 / SEQ)
    fast_high = math.log(0.05)
    log_rate = jnp.where(is_slow, slow_low + position * (slow_high - slow_low), slow_high + position * (fast_high - slow_high))
    rates = jnp.exp(log_rate)
    signs = jnp.clip(jax.random.normal(sign_key, (M, D)), -4.0, 4.0)
    return (rates, signs * jnp.sqrt(2.0 * rates) * 0.25)


def draw_decay_rate(key, part):
    return modal_pair(key)[0]


def draw_residues(key, part):
    return modal_pair(key)[1]


def draw_residual(key, part):
    noise_key = jax.random.fold_in(key, 404)
    row_key = jax.random.fold_in(key, 505)
    noise_values = jnp.clip(jax.random.normal(noise_key, (SEQ, D)), -4.0, 4.0)
    row_scale = jnp.exp(jax.random.uniform(row_key, (SEQ, 1)) * math.log(10.0))
    column_scale = jnp.exp(jnp.arange(D).astype(jnp.float32) / D * math.log(10.0))
    return (0.1 * noise_values * row_scale * column_scale[None, :]).astype(jnp.bfloat16)


def shard_levels(rng, dims, split, least, high):
    factor_of, own = 1.0, jax.random.fold_in(rng, 6)
    for axis_at, blocks in split:
        heights = jnp.exp(jax.random.uniform(jax.random.fold_in(own, axis_at), (blocks,), jnp.float32, least / len(split), high / len(split)))
        factor_of = factor_of * jnp.repeat(heights, dims[axis_at] // blocks).reshape([-1 if axis == axis_at else 1 for axis in range(len(dims))])
    return factor_of


def gaussian(own_key, dims, scale, bound, cuts=(), kind=jnp.bfloat16):
    values = scale * jax.random.normal(own_key, dims, jnp.float32)
    if cuts:
        values = values * shard_levels(own_key, dims, cuts, -0.22, 0.18)
    return jnp.clip(values, -bound, bound).astype(kind)


def setup_inputs(seed: int = 0) -> dict:
    streams_of = jax.random.split(jax.random.key(seed), 11)
    residual = draw_residual(jax.random.fold_in(streams_of[10], 71), 0)
    query_in = gaussian(streams_of[1], (SEQ, D), 1.0, 6.0, ((0, 8), (1, 4)))
    key_in = gaussian(streams_of[2], (SEQ, D), 1.0, 6.0, ((0, 8), (1, 4)))
    value_in = gaussian(streams_of[3], (SEQ, D), 1.0, 6.0, ((0, 8), (1, 4)))
    short_filter = gaussian(streams_of[4], (3, KS, D), KS ** -0.5, 2.0, ((2, 4),), jnp.float32)
    residues = draw_residues(jax.random.fold_in(streams_of[10], 71), 0)
    decay_rate = draw_decay_rate(jax.random.fold_in(streams_of[10], 71), 0)
    skip_gain = jnp.clip(0.5 + 1.0 * jax.random.uniform(streams_of[7], (D,), jnp.float32) ** shard_levels(streams_of[7], (D,), ((0, 4),), -0.2, 0.2), 0.5, 1.5)
    norm_gain = jnp.clip(1.0 + 0.1 * jax.random.normal(streams_of[8], (D,), jnp.float32), 0.5, 1.5)
    cotangent = gaussian(streams_of[9], (SEQ, D), 1.0, 6.0, ((0, 8), (1, 4)))
    return {"residual": residual, "query_in": query_in, "key_in": key_in, "value_in": value_in, "short_filter": short_filter, "residues": residues, "decay_rate": decay_rate, "skip_gain": skip_gain, "norm_gain": norm_gain, "cotangent": cotangent}


exact_mode = lax.Precision.HIGHEST

def make_tables(decay_rate, residues, block_len):
    lag_values = jnp.arange(block_len).astype(jnp.float32)
    powers = jnp.exp(-decay_rate[None, :, :] * lag_values[:, None, None])
    kernel = jnp.einsum('kmc,mc->kc', powers, residues, precision=exact_mode)
    offsets = jnp.arange(block_len)
    shifter = (offsets[:, None, None] - offsets[None, :, None] == offsets[None, None, :]).astype(jnp.float32)
    toeplitz = jnp.einsum('tsk,kc->tsc', shifter, kernel, precision=exact_mode)
    return (lag_values, powers, shifter, toeplitz)

def short_conv(extended, taps, row_count):
    tap_count = taps.shape[0]
    result = taps[0] * extended[tap_count - 1:tap_count - 1 + row_count]
    for offset in range(1, tap_count):
        result = result + taps[offset] * extended[tap_count - 1 - offset:tap_count - 1 - offset + row_count]
    return result

def conv_back(extended_grad, taps, row_count):
    tap_count = taps.shape[0]
    result = taps[0] * extended_grad[0:row_count]
    for offset in range(1, tap_count):
        result = result + taps[offset] * extended_grad[offset:offset + row_count]
    return result

def filter_grad(grad_feat, padded, tap_count, row_count):
    margin = tap_count - 1
    columns = [lax.optimization_barrier(jnp.sum(grad_feat * padded[margin - offset:margin - offset + row_count], axis=0)) for offset in range(tap_count)]
    return jnp.stack(columns)

def output_pass(u_blocks, state_x, state_p, decay_rate, residues, skip_gain, tables, track):
    lag_values, powers, shifter, toeplitz = tables
    block_len = powers.shape[0]
    ahead_pow = powers * jnp.exp(-decay_rate)[None]
    behind = powers[::-1]
    behind_lag = behind * lag_values[::-1][:, None, None]
    fading = jnp.exp(-decay_rate * block_len)

    def advance(running, u_block):
        state_x, state_p = running
        inside = jnp.einsum('tsc,sc->tc', toeplitz, u_block, precision=exact_mode)
        carried = jnp.einsum('tmc,mc->tc', ahead_pow, residues * state_x, precision=exact_mode)
        result = inside + carried + skip_gain * u_block
        gathered = jnp.einsum('smc,sc->mc', behind, u_block, precision=exact_mode)
        if track:
            weighted = jnp.einsum('smc,sc->mc', behind_lag, u_block, precision=exact_mode)
            state_p = fading * state_p - block_len * fading * state_x - weighted
        state_x = fading * state_x + gathered
        return ((state_x, state_p), result)
    (state_x, state_p), results = lax.scan(advance, (state_x, state_p), u_blocks)
    return (results, state_x, state_p)

def gradient_pass(u_blocks, dz_blocks, state_x, state_p, decay_rate, tables):
    lag_values, powers, shifter, toeplitz = tables
    block_len = powers.shape[0]
    ahead_pow = powers * jnp.exp(-decay_rate)[None]
    ahead_lag = ahead_pow * (lag_values + 1.0)[:, None, None]
    powers_lag = powers * lag_values[:, None, None]
    behind = powers[::-1]
    behind_lag = behind * lag_values[::-1][:, None, None]
    fading = jnp.exp(-decay_rate * block_len)

    def advance(running, pair):
        state_x, state_p, sum_res, sum_rate = running
        u_block, dz_block = pair
        products = dz_block[:, None, :] * u_block[None, :, :]
        lagged = jnp.einsum('tsk,tsc->kc', shifter, products, precision=exact_mode)
        nearby = jnp.einsum('tmc,tc->mc', ahead_pow, dz_block, precision=exact_mode)
        nearby_lag = jnp.einsum('tmc,tc->mc', ahead_lag, dz_block, precision=exact_mode)
        sum_res = sum_res + jnp.einsum('kc,kmc->mc', lagged, powers, precision=exact_mode) + nearby * state_x
        sum_rate = sum_rate - jnp.einsum('kc,kmc->mc', lagged, powers_lag, precision=exact_mode) - nearby_lag * state_x + nearby * state_p
        gathered = jnp.einsum('smc,sc->mc', behind, u_block, precision=exact_mode)
        weighted = jnp.einsum('smc,sc->mc', behind_lag, u_block, precision=exact_mode)
        state_p = fading * state_p - block_len * fading * state_x - weighted
        state_x = fading * state_x + gathered
        return ((state_x, state_p, sum_res, sum_rate), None)
    zero_sum = jnp.zeros_like(state_x)
    (state_x, state_p, sum_res, sum_rate), _ = lax.scan(advance, (state_x, state_p, zero_sum, zero_sum), (u_blocks, dz_blocks))
    return (sum_res, sum_rate)

def adjoint_pass(dz_blocks, adjoint, decay_rate, residues, tables):
    lag_values, powers, shifter, toeplitz = tables
    block_len = powers.shape[0]
    behind_next = powers[::-1] * jnp.exp(-decay_rate)[None]
    fading = jnp.exp(-decay_rate * block_len)

    def advance(adjoint, dz_block):
        inside = jnp.einsum('tsc,tc->sc', toeplitz, dz_block, precision=exact_mode)
        carried = jnp.einsum('smc,mc->sc', behind_next, residues * adjoint, precision=exact_mode)
        adjoint = jnp.einsum('tmc,tc->mc', powers, dz_block, precision=exact_mode) + fading * adjoint
        return (adjoint, inside + carried)
    adjoint, results = lax.scan(advance, adjoint, dz_blocks, reverse=True)
    return (results, adjoint)

def reference(residual, query_in, key_in, value_in, short_filter, residues, decay_rate, skip_gain, norm_gain, cotangent):
    block_len = min(32, TOK_DEV)
    margin = KS - 1
    streams = (query_in, key_in, value_in)
    padded = [jnp.concatenate([jnp.zeros((margin, D), jnp.float32), stream.astype(jnp.float32)], axis=0) for stream in streams]
    featured = [short_conv(padded[stream_id], short_filter[stream_id], SEQ) for stream_id in range(3)]
    mixed_uv = featured[1] * featured[2]
    tables = make_tables(decay_rate, residues, block_len)
    zero_state = jnp.zeros((M, D), jnp.float32)
    u_blocks = mixed_uv.reshape(SEQ // block_len, block_len, D)
    modal_blocks, _, _ = output_pass(u_blocks, zero_state, zero_state, decay_rate, residues, skip_gain, tables, False)
    modal = modal_blocks.reshape(SEQ, D)
    summed = residual.astype(jnp.float32) + featured[0] * modal
    inv_rms = lax.rsqrt(lax.optimization_barrier(jnp.sum(summed * summed, axis=1)) / D + 1e-05)
    normed = (summed * inv_rms[:, None] * norm_gain).astype(jnp.bfloat16)
    cot_values = cotangent.astype(jnp.float32)
    gain_term = cot_values * norm_gain
    inner_sum = lax.optimization_barrier(jnp.sum(gain_term * summed, axis=1))
    grad_sum = inv_rms[:, None] * gain_term - summed * (inv_rms ** 3 * inner_sum / D)[:, None]
    grad_modal = grad_sum * featured[0]
    grad_front = grad_sum * modal
    dz_blocks = grad_modal.reshape(SEQ // block_len, block_len, D)
    sum_res, sum_rate = gradient_pass(u_blocks, dz_blocks, zero_state, zero_state, decay_rate, tables)
    mixed_blocks, _ = adjoint_pass(dz_blocks, zero_state, decay_rate, residues, tables)
    grad_mixed = mixed_blocks.reshape(SEQ, D) + skip_gain * grad_modal
    grad_feats = (grad_front, grad_mixed * featured[2], grad_mixed * featured[1])
    zero_rows = jnp.zeros((margin, D), jnp.float32)
    grad_streams = [conv_back(jnp.concatenate([grad_feats[stream_id], zero_rows], axis=0), short_filter[stream_id], SEQ).astype(jnp.bfloat16) for stream_id in range(3)]
    grad_short = jnp.stack([filter_grad(grad_feats[stream_id], padded[stream_id], KS, SEQ) for stream_id in range(3)])
    grad_skip = lax.optimization_barrier(jnp.sum(grad_modal * mixed_uv, axis=0))
    grad_gain = lax.optimization_barrier(jnp.sum(cot_values * summed * inv_rms[:, None], axis=0))
    return (normed, grad_sum.astype(jnp.bfloat16), grad_streams[0], grad_streams[1], grad_streams[2], grad_short, sum_res, residues * sum_rate, grad_skip, grad_gain)
```

```python
import functools

import jax
import jax.numpy as jnp
from jax import lax
from jax.experimental import pallas as pl
from jax.experimental.pallas import tpu as pltpu
from jax.sharding import PartitionSpec as P

LANES = 128
SUB = 8
WIDE = SUB * LANES
F32 = jnp.float32
BF16 = jnp.bfloat16
VMEM_LIMIT = 48 * 1024 * 1024


def row(ref, t):
    return ref[pl.ds(pl.multiple_of(t * SUB, SUB), SUB), :]


def put(ref, t, value):
    ref[pl.ds(pl.multiple_of(t * SUB, SUB), SUB), :] = value


def spread(src, dst, first, count):
    def some(i, carry):
        start = pl.multiple_of(i * 16, 16)
        for g in range(SUB):
            piece = src[pl.ds(start, 16), g * LANES : (g + 1) * LANES].astype(F32)
            dst[pl.ds((start + first) * SUB + g, 16, stride=SUB), :] = piece
        return carry

    lax.fori_loop(0, count // 16, some, 0)


def gather_rows(src, dst, count):
    def some(i, carry):
        start = pl.multiple_of(i * 16, 16)
        for g in range(SUB):
            piece = src[pl.ds(start * SUB + g, 16, stride=SUB), :]
            dst[pl.ds(start, 16), g * LANES : (g + 1) * LANES] = piece.astype(dst.dtype)
        return carry

    lax.fori_loop(0, count // 16, some, 0)


def total(values):
    values = list(values)
    while len(values) > 1:
        values = [
            values[i] + values[i + 1] if i + 1 < len(values) else values[i]
            for i in range(0, len(values), 2)
        ]
    return values[0]


def taps_of(filt, stream, taps):
    return [row(filt, stream * taps + j) for j in range(taps)]


def conv_at(window, taps, i):
    margin = len(taps) - 1
    return total([taps[j] * window[margin + i - j] for j in range(margin + 1)])


def features_kernel(
    modes, taps, steps, key, value, filt3, decay, resid, k_ext, v_ext, f1, f2, u, lam, res, filt, x_out
):
    margin = taps - 1
    for g in range(SUB):
        lanes = slice(g * LANES, (g + 1) * LANES)
        lam[pl.ds(g, modes, stride=SUB), :] = decay[:, lanes]
        res[pl.ds(g, modes, stride=SUB), :] = resid[:, lanes]
        for i in range(3):
            filt[pl.ds(i * taps * SUB + g, taps, stride=SUB), :] = filt3[i, :, lanes]
    spread(key, k_ext, SUB, steps)
    spread(value, v_ext, SUB, steps)
    taps1, taps2 = taps_of(filt, 1, taps), taps_of(filt, 2, taps)

    def conv(c, carry):
        t0 = c * SUB
        kw = [row(k_ext, t0 + SUB - margin + i) for i in range(SUB + margin)]
        for i in range(SUB):
            put(f1, t0 + i, conv_at(kw, taps1, i))
        vw = [row(v_ext, t0 + SUB - margin + i) for i in range(SUB + margin)]
        for i in range(SUB):
            second = conv_at(vw, taps2, i)
            put(f2, t0 + i, second)
            put(u, t0 + i, second * row(f1, t0 + i))
        return carry

    lax.fori_loop(1, steps // SUB, conv, 0)
    fade = [jnp.exp(-row(lam, m)) for m in range(modes)]

    def advance(c, x):
        for i in range(SUB):
            now = row(u, c * SUB + i)
            x = tuple(fade[m] * x[m] + now for m in range(modes))
        return x

    x = lax.fori_loop(
        1, steps // SUB, advance, tuple(jnp.zeros((SUB, LANES), F32) for _ in range(modes))
    )
    for m in range(modes):
        put(x_out, m, x[m])


def head_kernel(
    modes, taps, steps, halo, k_head, v_head, filt, lam, x_part, k_in, v_in, f1_in, f2_in, u_in,
    k_ext, v_ext, f1, f2, u, x_out,
):
    del k_in, v_in, f1_in, f2_in, u_in
    margin = taps - 1
    for g in range(SUB):
        lanes = slice(g * LANES, (g + 1) * LANES)
        k_ext[pl.ds(g, SUB, stride=SUB), :] = halo[1, :, lanes].astype(F32)
        v_ext[pl.ds(g, SUB, stride=SUB), :] = halo[2, :, lanes].astype(F32)
    taps1, taps2 = taps_of(filt, 1, taps), taps_of(filt, 2, taps)
    kw = [row(k_ext, SUB - margin + i) for i in range(margin)] + [row(k_head, i) for i in range(SUB)]
    vw = [row(v_ext, SUB - margin + i) for i in range(margin)] + [row(v_head, i) for i in range(SUB)]
    mixed = []
    for i in range(SUB):
        first, second = conv_at(kw, taps1, i), conv_at(vw, taps2, i)
        put(f1, i, first)
        put(f2, i, second)
        put(u, i, first * second)
        mixed.append(first * second)
    for m in range(modes):
        rate = row(lam, m)
        fade = jnp.exp(-rate)
        x = mixed[0]
        for i in range(1, SUB):
            x = fade * x + mixed[i]
        put(x_out, m, row(x_part, m) + jnp.exp(-rate * float(steps - SUB)) * x)


def query_kernel(taps, steps, query, residual, cot, halo, filt, q_ext, f0, res_pos, cot_pos):
    margin = taps - 1
    for g in range(SUB):
        lanes = slice(g * LANES, (g + 1) * LANES)
        q_ext[pl.ds(g, SUB, stride=SUB), :] = halo[0, :, lanes].astype(F32)
    spread(query, q_ext, SUB, steps)
    spread(residual, res_pos, 0, steps)
    spread(cot, cot_pos, 0, steps)
    taps0 = taps_of(filt, 0, taps)

    def conv(c, carry):
        t0 = c * SUB
        qw = [row(q_ext, t0 + SUB - margin + i) for i in range(SUB + margin)]
        for i in range(SUB):
            put(f0, t0 + i, conv_at(qw, taps0, i))
        return carry

    lax.fori_loop(0, steps // SUB, conv, 0)


def own_modal_kernel(modes, steps, u, lam, res, skip, y, p_out):
    gain = skip[...]
    half = modes // 2
    for part in range(2):
        ms = range(part * half, (part + 1) * half)
        fade = [jnp.exp(-row(lam, m)) for m in ms]
        weight = [row(res, m) for m in ms]

        def advance(c, state, part=part, fade=fade, weight=weight):
            x, p = state
            for i in range(SUB):
                t = c * SUB + i
                now = row(u, t)
                x = tuple(f * v + now for f, v in zip(fade, x))
                p = tuple(f * w + v for f, w, v in zip(fade, p, x))
                own = total([w * v for w, v in zip(weight, x)])
                put(y, t, own + (gain * now if part == 0 else row(y, t)))
            return x, p

        zeros = tuple(jnp.zeros((SUB, LANES), F32) for _ in ms)
        _, p = lax.fori_loop(0, steps // SUB, advance, (zeros, zeros))
        for m, v in zip(ms, p):
            put(p_out, m, v)


def summed_kernel(modes, steps, blocks, y, f0, res_pos, cot_pos, x_in, lam, res, gain, modal, summed, sums, squares, inner):
    block = pl.program_id(0)

    @pl.when(block == 0)
    def _():
        squares[...] = jnp.zeros_like(squares)
        inner[...] = jnp.zeros_like(inner)

    fade = [jnp.exp(-row(lam, m)) for m in range(modes)]
    factor = gain[...]

    def advance(c, w):
        for i in range(SUB):
            t = c * SUB + i
            w = tuple(f * v for f, v in zip(fade, w))
            long = row(y, t) + total(w)
            put(modal, t, long)
            now = row(res_pos, t) + row(f0, t) * long
            put(summed, t, now)
            put(squares, t, row(squares, t) + now * now)
            put(inner, t, row(inner, t) + factor * row(cot_pos, t) * now)
        return w

    lax.fori_loop(
        0, steps // SUB, advance, tuple(row(res, m) * row(x_in, m) for m in range(modes))
    )

    @pl.when(block == blocks - 1)
    def _():
        for which, scratch in enumerate((squares, inner)):
            for b in range(steps // LANES):
                part = total(
                    [
                        scratch[pl.ds(b * LANES * SUB + g, LANES, stride=SUB), :]
                        for g in range(SUB)
                    ]
                )
                sums[which : which + 1, b * LANES : (b + 1) * LANES] = jnp.sum(
                    part.T, axis=0, keepdims=True
                )


def grad_modal_kernel(modes, steps, width, sums, summed, cot_pos, f0, modal, lam, gain, scale, gm, a_out, gf0_head):
    @pl.when(pl.program_id(0) == 0)
    def _():
        inv = lax.rsqrt(sums[0:1, :] / width + 1e-05)
        coef = inv * inv * inv * sums[1:2, :] / width
        for which, value in enumerate((inv, coef)):
            for b in range(steps // LANES):
                piece = value[:, b * LANES : (b + 1) * LANES]
                scale[pl.ds(which * steps + b * LANES, LANES), :] = jnp.broadcast_to(
                    piece, (LANES, LANES)
                ).T

    fade = [jnp.exp(-row(lam, m)) for m in range(modes)]
    factor = gain[...]

    def advance(c, a):
        t0 = steps - SUB - c * SUB
        for i in reversed(range(SUB)):
            t = t0 + i
            inv = scale[pl.ds(t, 1), :]
            coef = scale[pl.ds(steps + t, 1), :]
            grad = inv * (factor * row(cot_pos, t)) - coef * row(summed, t)
            now = grad * row(f0, t)
            put(gm, t, now)
            a = tuple(f * v + now for f, v in zip(fade, a))
        return a

    a = lax.fori_loop(
        0, steps // SUB, advance, tuple(jnp.zeros((SUB, LANES), F32) for _ in range(modes))
    )
    for m in range(modes):
        put(a_out, m, fade[m] * a[m])
    for t in range(SUB):
        inv = scale[pl.ds(t, 1), :]
        coef = scale[pl.ds(steps + t, 1), :]
        grad = inv * (factor * row(cot_pos, t)) - coef * row(summed, t)
        put(gf0_head, t, grad * row(modal, t))


def own_adjoint_kernel(modes, steps, gm, u, lam, res, skip, gmx, res_sum, rate_sum, lag_out, skip_out):
    gain = skip[...]
    half = modes // 2
    zero = jnp.zeros((SUB, LANES), F32)
    for part in range(2):
        ms = range(part * half, (part + 1) * half)
        fade = [jnp.exp(-row(lam, m)) for m in ms]
        weight = [row(res, m) for m in ms]

        def advance(c, state, part=part, fade=fade, weight=weight):
            adj, lag, by_res, by_rate, by_skip = state
            t0 = steps - SUB - c * SUB
            for i in reversed(range(SUB)):
                t = t0 + i
                now, mixed = row(gm, t), row(u, t)
                older = tuple(f * v for f, v in zip(fade, adj))
                lag = tuple(f * v + o for f, v, o in zip(fade, lag, older))
                adj = tuple(o + now for o in older)
                by_res = tuple(s + mixed * v for s, v in zip(by_res, adj))
                by_rate = tuple(s + mixed * v for s, v in zip(by_rate, lag))
                own = total([w * v for w, v in zip(weight, adj)])
                if part == 0:
                    put(gmx, t, own + gain * now)
                    by_skip = by_skip + now * mixed
                else:
                    put(gmx, t, own + row(gmx, t))
            return adj, lag, by_res, by_rate, by_skip

        zeros = tuple(zero for _ in ms)
        _, lag, by_res, by_rate, by_skip = lax.fori_loop(
            0, steps // SUB, advance, (zeros, zeros, zeros, zeros, zero)
        )
        for i, m in enumerate(ms):
            put(res_sum, m, by_res[i])
            put(rate_sum, m, by_rate[i])
            put(lag_out, m, fade[i] * lag[i])
        if part == 0:
            skip_out[...] = by_skip


def outputs_kernel(taps, steps, scale, summed, cot_pos, modal, q_ext, gf0_next, filt, gain, normed, grad_res, grad_query, short0, gain_out, work, gf0):
    margin = taps - 1
    factor = gain[...]
    gf0[pl.ds(steps * SUB, SUB * SUB), :] = gf0_next[...]
    taps0 = taps_of(filt, 0, taps)

    def norm(c, acc):
        for i in range(SUB):
            t = c * SUB + i
            inv = scale[pl.ds(t, 1), :]
            here = row(summed, t) * inv
            put(work, t, here * factor)
            acc = acc + row(cot_pos, t) * here
        return acc

    gain_out[...] = lax.fori_loop(0, steps // SUB, norm, jnp.zeros((SUB, LANES), F32))
    gather_rows(work, normed, steps)

    def grads(c, carry):
        for i in range(SUB):
            t = c * SUB + i
            inv = scale[pl.ds(t, 1), :]
            coef = scale[pl.ds(steps + t, 1), :]
            grad = inv * (factor * row(cot_pos, t)) - coef * row(summed, t)
            put(work, t, grad)
            put(gf0, t, grad * row(modal, t))
        return carry

    lax.fori_loop(0, steps // SUB, grads, 0)
    gather_rows(work, grad_res, steps)
    sums = filter_pass(taps, steps, gf0, q_ext)
    for j in range(taps):
        put(short0, j, sums[j])
    back_pass(taps, steps, gf0, taps0, work)
    gather_rows(work, grad_query, steps)


def filter_pass(taps, steps, grad, ext):
    margin = taps - 1

    def some(c, acc):
        t0 = c * SUB
        window = [row(ext, t0 + SUB - margin + i) for i in range(SUB + margin)]
        for i in range(SUB):
            now = row(grad, t0 + i)
            acc = tuple(acc[j] + now * window[margin + i - j] for j in range(taps))
        return acc

    zero = jnp.zeros((SUB, LANES), F32)
    return lax.fori_loop(0, steps // SUB, some, tuple(zero for _ in range(taps)))


def back_pass(taps, steps, grad, weights, out):
    margin = taps - 1

    def some(c, carry):
        t0 = c * SUB
        window = [row(grad, t0 + i) for i in range(SUB + margin)]
        for i in range(SUB):
            put(out, t0 + i, total([weights[j] * window[i + j] for j in range(taps)]))
        return carry

    lax.fori_loop(0, steps // SUB, some, 0)


def mixed_kernel(modes, taps, steps, gmx, f1, f2, k_ext, v_ext, lam, res, alpha, x_in, p_own, lag_own, rate_own, gf1, gf2, sums):
    rates = [row(lam, m) for m in range(modes)]
    fade = [jnp.exp(-r) for r in rates]

    def advance(c, w):
        t0 = steps - SUB - c * SUB
        for i in reversed(range(SUB)):
            t = t0 + i
            grad = row(gmx, t) + total(w)
            put(gf1, t, grad * row(f2, t))
            put(gf2, t, grad * row(f1, t))
            w = tuple(f * v for f, v in zip(fade, w))
        return w

    lax.fori_loop(
        0, steps // SUB, advance, tuple(row(res, m) * row(alpha, m) for m in range(modes))
    )
    for which, (grad, ext) in enumerate(((gf1, k_ext), (gf2, v_ext))):
        parts = filter_pass(taps, steps, grad, ext)
        for j in range(taps):
            put(sums, which * taps + j, parts[j])
    for m in range(modes):
        before, after = row(x_in, m), row(alpha, m)
        across = float(steps) * jnp.exp(-rates[m] * float(steps)) * before * after
        lagged = row(rate_own, m) + before * row(lag_own, m) + after * row(p_own, m) + across
        put(sums, 2 * taps + m, -row(res, m) * lagged)


def back_kernel(taps, steps, gf1, gf2, next_head, filt, grad_key, grad_value, work, ext):
    for which, (grad, out) in enumerate(((gf1, grad_key), (gf2, grad_value))):
        ext[pl.ds(0, steps * SUB), :] = grad[...]
        ext[pl.ds(steps * SUB, SUB * SUB), :] = next_head[which, 0]
        back_pass(taps, steps, ext, taps_of(filt, which + 1, taps), work)
        gather_rows(work, out, steps)


def finish_kernel(modes, taps, late, late_other, early, early_other, short, res, rate, skip, gain, work, work2):
    work[...] = late[...] + late_other[...]
    work2[...] = early[...] + early_other[...]
    for g in range(SUB):
        lanes = slice(g * LANES, (g + 1) * LANES)
        short[0, :, lanes] = work2[pl.ds(g, taps, stride=SUB), :]
        short[1, :, lanes] = work[pl.ds(g, taps, stride=SUB), :]
        short[2, :, lanes] = work[pl.ds(taps * SUB + g, taps, stride=SUB), :]
        rate[:, lanes] = work[pl.ds(2 * taps * SUB + g, modes, stride=SUB), :]
        res[:, lanes] = work2[pl.ds(taps * SUB + g, modes, stride=SUB), :]
    skip[...] = row(work2, taps + modes)
    gain[...] = row(work2, taps + modes + 1)


def shift(value, axis, distance):
    devices = range(lax.axis_size(axis))
    route = [(i - distance, i) for i in devices if i - distance in devices]
    return lax.ppermute(value, axis, route)


def carried_in(own, lam, span, axis, sign):
    count = lax.axis_size(axis)
    reach = min(2, count - 1)
    parts = [shift(own, axis, sign * k) for k in range(1, reach + 1)]
    state = parts[0]
    for k in range(1, reach):
        state = state + jnp.exp(-lam * float(span * k)) * parts[k]
    while reach < count - 1:
        state = state + jnp.exp(-lam * float(span * reach)) * shift(state, axis, sign * reach)
        reach *= 2
    return state


def sum_but_last(value, axis):
    count, step = lax.axis_size(axis), 1
    while True:
        other = lax.ppermute(value, axis, [(i, i ^ step) for i in range(count)])
        step *= 2
        if step >= count:
            return value, other
        value = value + other


def shards(
    residual, query_in, key_in, value_in, short_filter, residues, decay_rate, skip_gain, norm_gain, cotangent
):
    steps, channels = residual.shape
    modes, taps = residues.shape[0], short_filter.shape[1]
    blocks = channels // WIDE
    width = channels * lax.axis_size("tp")
    skip, gain = (v.reshape(blocks * SUB, LANES) for v in (skip_gain, norm_gain))

    def pos(count):
        return jax.ShapeDtypeStruct((blocks * count * SUB, LANES), F32)

    def pos_spec(count):
        return pl.BlockSpec((count * SUB, LANES), lambda h: (h, 0))

    def head_spec(total_steps, start):
        return pl.BlockSpec((SUB * SUB, LANES), lambda h: (h * (total_steps // SUB) + start, 0))

    wide_spec = pl.BlockSpec((steps, WIDE), lambda h: (0, h))
    wide = jax.ShapeDtypeStruct((steps, channels), BF16)
    mode_spec, one_spec, filt_spec = pos_spec(modes), pos_spec(1), pos_spec(3 * taps)
    seq_spec, ext_spec = pos_spec(steps), pos_spec(steps + SUB)
    seq, ext, mode, one = pos(steps), pos(steps + SUB), pos(modes), pos(1)
    halo_spec = pl.BlockSpec((3, SUB, WIDE), lambda h: (0, 0, h))
    param_spec = pl.BlockSpec((modes, WIDE), lambda h: (0, h))
    short_spec = pl.BlockSpec((3, taps, WIDE), lambda h: (0, 0, h))

    def call(body, ins, in_specs, outs, out_specs, ops, name, scratch=(), aliases=None):
        elements = steps * channels
        return pl.pallas_call(
            body,
            grid=(blocks,),
            in_specs=in_specs,
            out_specs=out_specs,
            out_shape=outs,
            scratch_shapes=list(scratch),
            input_output_aliases=aliases or {},
            compiler_params=pltpu.CompilerParams(
                dimension_semantics=("arbitrary",), vmem_limit_bytes=VMEM_LIMIT
            ),
            cost_estimate=pl.CostEstimate(
                flops=ops * elements, bytes_accessed=4 * elements, transcendentals=0
            ),
            name=name,
        )(*ins)

    trailing = jnp.stack([s[steps - SUB :] for s in (query_in, key_in, value_in)])
    halo = shift(trailing, "ctx", 1)

    k_ext, v_ext, f1, f2, u, lam, res, filt, x_part = call(
        functools.partial(features_kernel, modes, taps, steps),
        (key_in, value_in, short_filter, decay_rate, residues),
        [wide_spec, wide_spec, short_spec, param_spec, param_spec],
        [ext, ext, seq, seq, seq, mode, mode, pos(3 * taps), mode],
        [ext_spec, ext_spec, seq_spec, seq_spec, seq_spec, mode_spec, mode_spec, filt_spec, mode_spec],
        64,
        "features",
    )
    any_spec = pl.BlockSpec(memory_space=pl.ANY)
    k_ext, v_ext, f1, f2, u, x_own = call(
        functools.partial(head_kernel, modes, taps, steps),
        (halo, k_ext, v_ext, filt, lam, x_part, k_ext, v_ext, f1, f2, u),
        [halo_spec, head_spec(steps + SUB, 1), head_spec(steps + SUB, 1), filt_spec, mode_spec, mode_spec]
        + [any_spec] * 5,
        [ext, ext, seq, seq, seq, mode],
        [head_spec(steps + SUB, 0)] * 2 + [head_spec(steps, 0)] * 3 + [mode_spec],
        2,
        "head",
        aliases={6: 0, 7: 1, 8: 2, 9: 3, 10: 4},
    )
    x_in = carried_in(x_own, lam, steps, "ctx", 1)
    q_ext, f0, res_pos, cot_pos = call(
        functools.partial(query_kernel, taps, steps),
        (query_in, residual, cotangent, halo, filt),
        [wide_spec, wide_spec, wide_spec, halo_spec, filt_spec],
        [ext, seq, seq, seq],
        [ext_spec, seq_spec, seq_spec, seq_spec],
        30,
        "query",
    )
    y, p_own = call(
        functools.partial(own_modal_kernel, modes, steps),
        (u, lam, res, skip),
        [seq_spec, mode_spec, mode_spec, one_spec],
        [seq, mode],
        [seq_spec, mode_spec],
        96,
        "own_modal",
    )
    modal, summed, sums = call(
        functools.partial(summed_kernel, modes, steps, blocks),
        (y, f0, res_pos, cot_pos, x_in, lam, res, gain),
        [seq_spec] * 4 + [mode_spec] * 3 + [one_spec],
        [seq, seq, jax.ShapeDtypeStruct((2, steps), F32)],
        [seq_spec, seq_spec, pl.BlockSpec((2, steps), lambda h: (0, 0))],
        40,
        "summed",
        scratch=[pltpu.VMEM((steps * SUB, LANES), F32)] * 2,
    )
    sums = lax.psum(sums, "tp")
    scale, gm, a_own, gf0_head = call(
        functools.partial(grad_modal_kernel, modes, steps, width),
        (sums, summed, cot_pos, f0, modal, lam, gain),
        [pl.BlockSpec((2, steps), lambda h: (0, 0)), seq_spec, seq_spec, seq_spec, head_spec(steps, 0), mode_spec, one_spec],
        [jax.ShapeDtypeStruct((2 * steps, LANES), F32), seq, mode, pos(SUB)],
        [pl.BlockSpec((2 * steps, LANES), lambda h: (0, 0)), seq_spec, mode_spec, pos_spec(SUB)],
        40,
        "grad_modal",
    )
    alpha = carried_in(a_own, lam, steps, "ctx", -1)
    gf0_next = shift(gf0_head, "ctx", -1)
    gmx, res_sum, rate_own, lag_own, skip_sum = call(
        functools.partial(own_adjoint_kernel, modes, steps),
        (gm, u, lam, res, skip),
        [seq_spec, seq_spec, mode_spec, mode_spec, one_spec],
        [seq, mode, mode, mode, one],
        [seq_spec, mode_spec, mode_spec, mode_spec, one_spec],
        160,
        "own_adjoint",
    )
    scale_spec = pl.BlockSpec((2 * steps, LANES), lambda h: (0, 0))
    normed, grad_residual, grad_query, short0, gain_sum = call(
        functools.partial(outputs_kernel, taps, steps),
        (scale, summed, cot_pos, modal, q_ext, gf0_next, filt, gain),
        [scale_spec, seq_spec, seq_spec, seq_spec, ext_spec, pos_spec(SUB), filt_spec, one_spec],
        [wide, wide, wide, pos(taps), one],
        [wide_spec, wide_spec, wide_spec, pos_spec(taps), one_spec],
        50,
        "outputs",
        scratch=[
            pltpu.VMEM((steps * SUB, LANES), F32),
            pltpu.VMEM(((steps + SUB) * SUB, LANES), F32),
        ],
    )
    early_rows = taps + modes + 2
    early = jnp.concatenate(
        [
            v.reshape(blocks, -1, LANES)
            for v in (short0, res_sum + x_in * a_own, skip_sum, gain_sum)
        ],
        axis=1,
    ).reshape(-1, LANES)
    early, early_other = sum_but_last(early, "ctx")
    late_rows = 2 * taps + modes
    gf1, gf2, late = call(
        functools.partial(mixed_kernel, modes, taps, steps),
        (gmx, f1, f2, k_ext, v_ext, lam, res, alpha, x_in, p_own, lag_own, rate_own),
        [seq_spec] * 3 + [ext_spec] * 2 + [mode_spec] * 7,
        [seq, seq, pos(late_rows)],
        [seq_spec, seq_spec, pos_spec(late_rows)],
        64,
        "mixed",
    )
    late, late_other = sum_but_last(late, "ctx")
    heads = jnp.stack([v.reshape(blocks, steps * SUB, LANES)[:, : SUB * SUB] for v in (gf1, gf2)])
    next_head = shift(heads, "ctx", -1)
    grad_key, grad_value = call(
        functools.partial(back_kernel, taps, steps),
        (gf1, gf2, next_head, filt),
        [seq_spec, seq_spec, pl.BlockSpec((2, 1, SUB * SUB, LANES), lambda h: (0, h, 0, 0)), filt_spec],
        [wide, wide],
        [wide_spec, wide_spec],
        28,
        "back",
        scratch=[
            pltpu.VMEM((steps * SUB, LANES), F32),
            pltpu.VMEM(((steps + SUB) * SUB, LANES), F32),
        ],
    )
    late_spec, early_spec = pos_spec(late_rows), pos_spec(early_rows)
    grad_short, grad_residues, grad_rate, grad_skip, grad_gain = call(
        functools.partial(finish_kernel, modes, taps),
        (late, late_other, early, early_other),
        [late_spec, late_spec, early_spec, early_spec],
        [
            jax.ShapeDtypeStruct(short_filter.shape, F32),
            jax.ShapeDtypeStruct(residues.shape, F32),
            jax.ShapeDtypeStruct(residues.shape, F32),
            one,
            one,
        ],
        [short_spec, param_spec, param_spec, one_spec, one_spec],
        1,
        "finish",
        scratch=[
            pltpu.VMEM((late_rows * SUB, LANES), F32),
            pltpu.VMEM((early_rows * SUB, LANES), F32),
        ],
    )
    return (
        normed,
        grad_residual,
        grad_query,
        grad_key,
        grad_value,
        grad_short,
        grad_residues,
        grad_rate,
        grad_skip.reshape(channels),
        grad_gain.reshape(channels),
    )


def solution(mesh):
    both, modes, vector = P("ctx", "tp"), P(None, "tp"), P("tp")
    return jax.shard_map(
        shards,
        mesh=mesh,
        in_specs=(both, both, both, both, P(None, None, "tp"), modes, modes, vector, vector, both),
        out_specs=(both,) * 5 + (P(None, None, "tp"), modes, modes, vector, vector),
        check_vma=False,
    )
```

```python
import functools

import jax
import jax.numpy as jnp
from jax import lax
from jax.experimental import pallas as pl
from jax.experimental.pallas import tpu as pltpu
from jax.sharding import PartitionSpec as P

LANES = 128
SUB = 8
WIDE = SUB * LANES
F32 = jnp.float32
BF16 = jnp.bfloat16
VMEM_LIMIT = 10 * 1024 * 1024


def row(ref, t):
    return ref[pl.ds(pl.multiple_of(t * SUB, SUB), SUB), :]


def put(ref, t, value):
    ref[pl.ds(pl.multiple_of(t * SUB, SUB), SUB), :] = value


def spread(src, dst, first, count):
    def some(i, carry):
        start = pl.multiple_of(i * 16, 16)
        for g in range(SUB):
            piece = src[pl.ds(start, 16), g * LANES : (g + 1) * LANES].astype(F32)
            dst[pl.ds((start + first) * SUB + g, 16, stride=SUB), :] = piece
        return carry

    lax.fori_loop(0, count // 16, some, 0)


def gather_rows(src, dst, count):
    def some(i, carry):
        start = pl.multiple_of(i * 16, 16)
        for g in range(SUB):
            piece = src[pl.ds(start * SUB + g, 16, stride=SUB), :]
            dst[pl.ds(start, 16), g * LANES : (g + 1) * LANES] = piece.astype(dst.dtype)
        return carry

    lax.fori_loop(0, count // 16, some, 0)


def total(values):
    values = list(values)
    while len(values) > 1:
        values = [
            values[i] + values[i + 1] if i + 1 < len(values) else values[i]
            for i in range(0, len(values), 2)
        ]
    return values[0]


def taps_of(filt, stream, taps):
    return [row(filt, stream * taps + j) for j in range(taps)]


def conv_at(window, taps, i):
    margin = len(taps) - 1
    return total([taps[j] * window[margin + i - j] for j in range(margin + 1)])


def features_kernel(
    modes, taps, steps, key, value, filt3, decay, resid, k_ext, v_ext, f1, f2, u, lam, res, filt, x_out
):
    margin = taps - 1
    for g in range(SUB):
        lanes = slice(g * LANES, (g + 1) * LANES)
        lam[pl.ds(g, modes, stride=SUB), :] = decay[:, lanes]
        res[pl.ds(g, modes, stride=SUB), :] = resid[:, lanes]
        for i in range(3):
            filt[pl.ds(i * taps * SUB + g, taps, stride=SUB), :] = filt3[i, :, lanes]
    spread(key, k_ext, SUB, steps)
    spread(value, v_ext, SUB, steps)
    taps1, taps2 = taps_of(filt, 1, taps), taps_of(filt, 2, taps)

    def conv(c, carry):
        t0 = c * SUB
        kw = [row(k_ext, t0 + SUB - margin + i) for i in range(SUB + margin)]
        for i in range(SUB):
            put(f1, t0 + i, conv_at(kw, taps1, i))
        vw = [row(v_ext, t0 + SUB - margin + i) for i in range(SUB + margin)]
        for i in range(SUB):
            second = conv_at(vw, taps2, i)
            put(f2, t0 + i, second)
            put(u, t0 + i, second * row(f1, t0 + i))
        return carry

    lax.fori_loop(1, steps // SUB, conv, 0)
    fade = [jnp.exp(-row(lam, m)) for m in range(modes)]

    def advance(c, x):
        for i in range(SUB):
            now = row(u, c * SUB + i)
            x = tuple(fade[m] * x[m] + now for m in range(modes))
        return x

    x = lax.fori_loop(
        1, steps // SUB, advance, tuple(jnp.zeros((SUB, LANES), F32) for _ in range(modes))
    )
    for m in range(modes):
        put(x_out, m, x[m])


def head_kernel(
    modes, taps, steps, halo, k_head, v_head, filt, lam, x_part, f1_in, f2_in, u_in,
    k_ext, v_ext, f1, f2, u, x_out,
):
    del f1_in, f2_in, u_in
    margin = taps - 1
    for g in range(SUB):
        lanes = slice(g * LANES, (g + 1) * LANES)
        k_ext[pl.ds(g, SUB, stride=SUB), :] = halo[1, :, lanes].astype(F32)
        v_ext[pl.ds(g, SUB, stride=SUB), :] = halo[2, :, lanes].astype(F32)
    taps1, taps2 = taps_of(filt, 1, taps), taps_of(filt, 2, taps)
    kw = [row(k_ext, SUB - margin + i) for i in range(margin)] + [row(k_head, i) for i in range(SUB)]
    vw = [row(v_ext, SUB - margin + i) for i in range(margin)] + [row(v_head, i) for i in range(SUB)]
    mixed = []
    for i in range(SUB):
        first, second = conv_at(kw, taps1, i), conv_at(vw, taps2, i)
        put(f1, i, first)
        put(f2, i, second)
        put(u, i, first * second)
        mixed.append(first * second)
    for m in range(modes):
        rate = row(lam, m)
        fade = jnp.exp(-rate)
        x = mixed[0]
        for i in range(1, SUB):
            x = fade * x + mixed[i]
        put(x_out, m, row(x_part, m) + jnp.exp(-rate * float(steps - SUB)) * x)


def query_kernel(taps, steps, query, residual, cot, halo, filt, q_ext, f0, res_pos, cot_pos):
    margin = taps - 1
    for g in range(SUB):
        lanes = slice(g * LANES, (g + 1) * LANES)
        q_ext[pl.ds(g, SUB, stride=SUB), :] = halo[0, :, lanes].astype(F32)
    spread(query, q_ext, SUB, steps)
    spread(residual, res_pos, 0, steps)
    spread(cot, cot_pos, 0, steps)
    taps0 = taps_of(filt, 0, taps)

    def conv(c, carry):
        t0 = c * SUB
        qw = [row(q_ext, t0 + SUB - margin + i) for i in range(SUB + margin)]
        for i in range(SUB):
            put(f0, t0 + i, conv_at(qw, taps0, i))
        return carry

    lax.fori_loop(0, steps // SUB, conv, 0)


def own_modal_kernel(modes, steps, u, lam, res, skip, y, p_out):
    gain = skip[...]
    half = modes // 2
    for part in range(2):
        ms = range(part * half, (part + 1) * half)
        fade = [jnp.exp(-row(lam, m)) for m in ms]
        weight = [row(res, m) for m in ms]

        def advance(c, state, part=part, fade=fade, weight=weight):
            x, p = state
            for i in range(SUB):
                t = c * SUB + i
                now = row(u, t)
                x = tuple(f * v + now for f, v in zip(fade, x))
                p = tuple(f * w + v for f, w, v in zip(fade, p, x))
                own = total([w * v for w, v in zip(weight, x)])
                put(y, t, own + (gain * now if part == 0 else row(y, t)))
            return x, p

        zeros = tuple(jnp.zeros((SUB, LANES), F32) for _ in ms)
        _, p = lax.fori_loop(0, steps // SUB, advance, (zeros, zeros))
        for m, v in zip(ms, p):
            put(p_out, m, v)


def summed_kernel(modes, steps, blocks, y, f0, res_pos, cot_pos, x_in, lam, res, gain, modal, summed, sums, squares, inner):
    block = pl.program_id(0)

    @pl.when(block == 0)
    def _():
        squares[...] = jnp.zeros_like(squares)
        inner[...] = jnp.zeros_like(inner)

    fade = [jnp.exp(-row(lam, m)) for m in range(modes)]
    factor = gain[...]

    def advance(c, w):
        for i in range(SUB):
            t = c * SUB + i
            w = tuple(f * v for f, v in zip(fade, w))
            long = row(y, t) + total(w)
            put(modal, t, long)
            now = row(res_pos, t) + row(f0, t) * long
            put(summed, t, now)
            put(squares, t, row(squares, t) + now * now)
            put(inner, t, row(inner, t) + factor * row(cot_pos, t) * now)
        return w

    lax.fori_loop(
        0, steps // SUB, advance, tuple(row(res, m) * row(x_in, m) for m in range(modes))
    )

    @pl.when(block == blocks - 1)
    def _():
        for which, scratch in enumerate((squares, inner)):
            for b in range(steps // LANES):
                part = total(
                    [
                        scratch[pl.ds(b * LANES * SUB + g, LANES, stride=SUB), :]
                        for g in range(SUB)
                    ]
                )
                sums[which : which + 1, b * LANES : (b + 1) * LANES] = jnp.sum(
                    part.T, axis=0, keepdims=True
                )


def grad_modal_kernel(modes, steps, width, sums, summed, cot_pos, f0, modal, lam, gain, scale, gm, a_out, gf0_head):
    @pl.when(pl.program_id(0) == 0)
    def _():
        inv = lax.rsqrt(sums[0:1, :] / width + 1e-05)
        coef = inv * inv * inv * sums[1:2, :] / width
        for which, value in enumerate((inv, coef)):
            for b in range(steps // LANES):
                piece = value[:, b * LANES : (b + 1) * LANES]
                scale[pl.ds(which * steps + b * LANES, LANES), :] = jnp.broadcast_to(
                    piece, (LANES, LANES)
                ).T

    fade = [jnp.exp(-row(lam, m)) for m in range(modes)]
    factor = gain[...]

    def advance(c, a):
        t0 = steps - SUB - c * SUB
        for i in reversed(range(SUB)):
            t = t0 + i
            inv = scale[pl.ds(t, 1), :]
            coef = scale[pl.ds(steps + t, 1), :]
            grad = inv * (factor * row(cot_pos, t)) - coef * row(summed, t)
            now = grad * row(f0, t)
            put(gm, t, now)
            a = tuple(f * v + now for f, v in zip(fade, a))
        return a

    a = lax.fori_loop(
        0, steps // SUB, advance, tuple(jnp.zeros((SUB, LANES), F32) for _ in range(modes))
    )
    for m in range(modes):
        put(a_out, m, fade[m] * a[m])
    for t in range(SUB):
        inv = scale[pl.ds(t, 1), :]
        coef = scale[pl.ds(steps + t, 1), :]
        grad = inv * (factor * row(cot_pos, t)) - coef * row(summed, t)
        put(gf0_head, t, grad * row(modal, t))


def own_adjoint_kernel(modes, steps, gm, u, lam, res, skip, gmx, res_sum, rate_sum, lag_out, skip_out):
    gain = skip[...]
    half = modes // 2
    zero = jnp.zeros((SUB, LANES), F32)
    for part in range(2):
        ms = range(part * half, (part + 1) * half)
        fade = [jnp.exp(-row(lam, m)) for m in ms]
        weight = [row(res, m) for m in ms]

        def advance(c, state, part=part, fade=fade, weight=weight):
            adj, lag, by_res, by_rate, by_skip = state
            t0 = steps - SUB - c * SUB
            for i in reversed(range(SUB)):
                t = t0 + i
                now, mixed = row(gm, t), row(u, t)
                older = tuple(f * v for f, v in zip(fade, adj))
                lag = tuple(f * v + o for f, v, o in zip(fade, lag, older))
                adj = tuple(o + now for o in older)
                by_res = tuple(s + mixed * v for s, v in zip(by_res, adj))
                by_rate = tuple(s + mixed * v for s, v in zip(by_rate, lag))
                own = total([w * v for w, v in zip(weight, adj)])
                if part == 0:
                    put(gmx, t, own + gain * now)
                    by_skip = by_skip + now * mixed
                else:
                    put(gmx, t, own + row(gmx, t))
            return adj, lag, by_res, by_rate, by_skip

        zeros = tuple(zero for _ in ms)
        _, lag, by_res, by_rate, by_skip = lax.fori_loop(
            0, steps // SUB, advance, (zeros, zeros, zeros, zeros, zero)
        )
        for i, m in enumerate(ms):
            put(res_sum, m, by_res[i])
            put(rate_sum, m, by_rate[i])
            put(lag_out, m, fade[i] * lag[i])
        if part == 0:
            skip_out[...] = by_skip


def outputs_kernel(taps, steps, scale, summed, cot_pos, modal, q_ext, gf0_next, filt, gain, normed, grad_res, grad_query, short0, gain_out, work, gf0):
    margin = taps - 1
    factor = gain[...]
    gf0[pl.ds(steps * SUB, SUB * SUB), :] = gf0_next[...]
    taps0 = taps_of(filt, 0, taps)

    def norm(c, acc):
        for i in range(SUB):
            t = c * SUB + i
            inv = scale[pl.ds(t, 1), :]
            here = row(summed, t) * inv
            put(work, t, here * factor)
            acc = acc + row(cot_pos, t) * here
        return acc

    gain_out[...] = lax.fori_loop(0, steps // SUB, norm, jnp.zeros((SUB, LANES), F32))
    gather_rows(work, normed, steps)

    def grads(c, carry):
        for i in range(SUB):
            t = c * SUB + i
            inv = scale[pl.ds(t, 1), :]
            coef = scale[pl.ds(steps + t, 1), :]
            grad = inv * (factor * row(cot_pos, t)) - coef * row(summed, t)
            put(work, t, grad)
            put(gf0, t, grad * row(modal, t))
        return carry

    lax.fori_loop(0, steps // SUB, grads, 0)
    gather_rows(work, grad_res, steps)
    sums = filter_pass(taps, steps, gf0, q_ext)
    for j in range(taps):
        put(short0, j, sums[j])
    back_pass(taps, steps, gf0, taps0, work)
    gather_rows(work, grad_query, steps)


def filter_pass(taps, steps, grad, ext):
    margin = taps - 1

    def some(c, acc):
        t0 = c * SUB
        window = [row(ext, t0 + SUB - margin + i) for i in range(SUB + margin)]
        for i in range(SUB):
            now = row(grad, t0 + i)
            acc = tuple(acc[j] + now * window[margin + i - j] for j in range(taps))
        return acc

    zero = jnp.zeros((SUB, LANES), F32)
    return lax.fori_loop(0, steps // SUB, some, tuple(zero for _ in range(taps)))


def back_pass(taps, steps, grad, weights, out):
    margin = taps - 1

    def some(c, carry):
        t0 = c * SUB
        window = [row(grad, t0 + i) for i in range(SUB + margin)]
        for i in range(SUB):
            put(out, t0 + i, total([weights[j] * window[i + j] for j in range(taps)]))
        return carry

    lax.fori_loop(0, steps // SUB, some, 0)


def mixed_kernel(modes, taps, steps, gmx, f1, f2, k_ext, v_ext, lam, res, alpha, x_in, p_own, lag_own, rate_own, gf1, gf2, heads, sums):
    rates = [row(lam, m) for m in range(modes)]
    fade = [jnp.exp(-r) for r in rates]

    def advance(c, w):
        t0 = steps - SUB - c * SUB
        for i in reversed(range(SUB)):
            t = t0 + i
            grad = row(gmx, t) + total(w)
            put(gf1, t, grad * row(f2, t))
            put(gf2, t, grad * row(f1, t))
            w = tuple(f * v for f, v in zip(fade, w))
        return w

    lax.fori_loop(
        0, steps // SUB, advance, tuple(row(res, m) * row(alpha, m) for m in range(modes))
    )
    heads[0, 0] = gf1[: SUB * SUB, :]
    heads[1, 0] = gf2[: SUB * SUB, :]
    for which, (grad, ext) in enumerate(((gf1, k_ext), (gf2, v_ext))):
        parts = filter_pass(taps, steps, grad, ext)
        for j in range(taps):
            put(sums, which * taps + j, parts[j])
    for m in range(modes):
        before, after = row(x_in, m), row(alpha, m)
        across = float(steps) * jnp.exp(-rates[m] * float(steps)) * before * after
        lagged = row(rate_own, m) + before * row(lag_own, m) + after * row(p_own, m) + across
        put(sums, 2 * taps + m, -row(res, m) * lagged)


def back_kernel(taps, steps, gf1, gf2, next_head, filt, grad_key, grad_value, work, ext):
    for which, (grad, out) in enumerate(((gf1, grad_key), (gf2, grad_value))):
        ext[pl.ds(0, steps * SUB), :] = grad[...]
        ext[pl.ds(steps * SUB, SUB * SUB), :] = next_head[which, 0]
        back_pass(taps, steps, ext, taps_of(filt, which + 1, taps), work)
        gather_rows(work, out, steps)


def finish_kernel(modes, taps, late, late_other, early, early_other, short, res, rate, skip, gain, work, work2):
    work[...] = late[...] + late_other[...]
    work2[...] = early[...] + early_other[...]
    for g in range(SUB):
        lanes = slice(g * LANES, (g + 1) * LANES)
        short[0, :, lanes] = work2[pl.ds(g, taps, stride=SUB), :]
        short[1, :, lanes] = work[pl.ds(g, taps, stride=SUB), :]
        short[2, :, lanes] = work[pl.ds(taps * SUB + g, taps, stride=SUB), :]
        rate[:, lanes] = work[pl.ds(2 * taps * SUB + g, modes, stride=SUB), :]
        res[:, lanes] = work2[pl.ds(taps * SUB + g, modes, stride=SUB), :]
    skip[...] = row(work2, taps + modes)
    gain[...] = row(work2, taps + modes + 1)


def shift(value, axis, distance):
    devices = range(lax.axis_size(axis))
    route = [(i - distance, i) for i in devices if i - distance in devices]
    return lax.ppermute(value, axis, route)


def join(state, others, lam, span, under):
    for k, other in enumerate(others):
        state = state + jnp.exp(lam * -float(span * (k + 1))) * other
    return state if under is None else state + under[0, 0]


def carried_in(own, lam, span, axis, sign, under):
    count = lax.axis_size(axis)
    reach = min(2, count - 1)
    under = list(under) + [None] * count
    first, *rest = [shift(own, axis, sign * k) for k in range(1, reach + 1)]
    state = join(first, rest, lam, span, under.pop(0))
    while reach < count - 1:
        other = shift(state, axis, sign * reach)
        state = join(state, [other], lam, span * reach, under.pop(0))
        reach *= 2
    return state


def sum_but_last(value, axis, under=None):
    count, step = lax.axis_size(axis), 1
    while True:
        other = lax.ppermute(value, axis, [(i, i ^ step) for i in range(count)])
        step *= 2
        if step >= count:
            return value, other
        value = value + other if under is None else value + other + under[0, 0]
        under = None


def shards(
    residual, query_in, key_in, value_in, short_filter, residues, decay_rate, skip_gain, norm_gain, cotangent
):
    steps, channels = residual.shape
    modes, taps = residues.shape[0], short_filter.shape[1]
    blocks = channels // WIDE
    width = channels * lax.axis_size("tp")
    skip, gain = (v.reshape(blocks * SUB, LANES) for v in (skip_gain, norm_gain))

    def pos(count):
        return jax.ShapeDtypeStruct((blocks * count * SUB, LANES), F32)

    def kept(count):
        return pltpu.VMEM((blocks * count * SUB, LANES), F32)

    def pos_spec(count):
        return pl.BlockSpec((count * SUB, LANES), lambda h: (h, 0))

    def head_spec(total_steps, start):
        return pl.BlockSpec((SUB * SUB, LANES), lambda h: (h * (total_steps // SUB) + start, 0))

    wide_spec = pl.BlockSpec((steps, WIDE), lambda h: (0, h))
    wide = jax.ShapeDtypeStruct((steps, channels), BF16)
    mode_spec, one_spec, filt_spec = pos_spec(modes), pos_spec(1), pos_spec(3 * taps)
    seq_spec, ext_spec = pos_spec(steps), pos_spec(steps + SUB)
    seq, ext, mode, one = kept(steps), kept(steps + SUB), pos(modes), pos(1)
    halo_spec = pl.BlockSpec((3, SUB, WIDE), lambda h: (0, 0, h))
    param_spec = pl.BlockSpec((modes, WIDE), lambda h: (0, h))
    short_spec = pl.BlockSpec((3, taps, WIDE), lambda h: (0, 0, h))

    def call(body, ins, in_specs, outs, out_specs, ops, name, scratch=(), aliases=None):
        elements, n_refs = steps * channels, len(ins) + len(outs)

        def with_done(*refs):
            done = refs[n_refs]
            done[...] = jnp.zeros_like(done)
            body(*refs[:n_refs], *refs[n_refs + 1 :])

        near = blocks * steps * SUB
        ins = [
            pltpu.with_memory_space_constraint(v, pltpu.VMEM) if v.shape[0] >= near else v
            for v in ins
        ]
        outs = [*outs, jax.ShapeDtypeStruct((SUB, LANES), F32)]
        out_specs = [*out_specs, pl.BlockSpec((SUB, LANES), lambda h: (0, 0))]
        return pl.pallas_call(
            with_done,
            grid=(blocks,),
            in_specs=in_specs,
            out_specs=out_specs,
            out_shape=outs,
            scratch_shapes=list(scratch),
            input_output_aliases=aliases or {},
            compiler_params=pltpu.CompilerParams(
                dimension_semantics=("arbitrary",), vmem_limit_bytes=VMEM_LIMIT
            ),
            cost_estimate=pl.CostEstimate(
                flops=ops * elements, bytes_accessed=4 * elements, transcendentals=0
            ),
            name=name,
        )(*ins)

    far = [
        pltpu.with_memory_space_constraint(v, pltpu.HBM)
        for v in (residual, query_in, key_in, value_in, cotangent, short_filter, decay_rate, residues)
    ]
    trailing = jnp.stack([s[steps - SUB :] for s in (query_in, key_in, value_in)])
    halo = shift(trailing, "ctx", 1)

    k_ext, v_ext, f1, f2, u, lam, res, filt, x_part, _ = call(
        functools.partial(features_kernel, modes, taps, steps),
        (far[2], far[3], *far[5:]),
        [wide_spec, wide_spec, short_spec, param_spec, param_spec],
        [ext, ext, seq, seq, seq, mode, mode, pos(3 * taps), mode],
        [ext_spec, ext_spec, seq_spec, seq_spec, seq_spec, mode_spec, mode_spec, filt_spec, mode_spec],
        64,
        "features",
    )
    any_spec = pl.BlockSpec(memory_space=pl.ANY)
    k_ext, v_ext, f1, f2, u, x_own, _ = call(
        functools.partial(head_kernel, modes, taps, steps),
        (halo, k_ext, v_ext, filt, lam, x_part, f1, f2, u),
        [halo_spec, head_spec(steps + SUB, 1), head_spec(steps + SUB, 1), filt_spec, mode_spec, mode_spec]
        + [any_spec] * 3,
        [ext, ext, seq, seq, seq, mode],
        [head_spec(steps + SUB, 0)] * 2 + [head_spec(steps, 0)] * 3 + [mode_spec],
        2,
        "head",
        aliases={1: 0, 2: 1, 6: 2, 7: 3, 8: 4},
    )
    q_ext, f0, res_pos, cot_pos, query_done = call(
        functools.partial(query_kernel, taps, steps),
        (far[1], far[0], far[4], halo, filt),
        [wide_spec, wide_spec, wide_spec, halo_spec, filt_spec],
        [ext, seq, seq, seq],
        [ext_spec, seq_spec, seq_spec, seq_spec],
        30,
        "query",
    )
    y, p_own, modal_done = call(
        functools.partial(own_modal_kernel, modes, steps),
        (u, lam, res, skip),
        [seq_spec, mode_spec, mode_spec, one_spec],
        [seq, mode],
        [seq_spec, mode_spec],
        96,
        "own_modal",
    )
    x_in = carried_in(x_own, lam, steps, "ctx", 1, [query_done, modal_done])
    modal, summed, sums, _ = call(
        functools.partial(summed_kernel, modes, steps, blocks),
        (y, f0, res_pos, cot_pos, x_in, lam, res, gain),
        [seq_spec] * 4 + [mode_spec] * 3 + [one_spec],
        [seq, seq, jax.ShapeDtypeStruct((2, steps), F32)],
        [seq_spec, seq_spec, pl.BlockSpec((2, steps), lambda h: (0, 0))],
        40,
        "summed",
        scratch=[pltpu.VMEM((steps * SUB, LANES), F32)] * 2,
    )
    sums = lax.psum(sums, "tp")
    scale, gm, a_own, gf0_head, _ = call(
        functools.partial(grad_modal_kernel, modes, steps, width),
        (sums, summed, cot_pos, f0, modal, lam, gain),
        [pl.BlockSpec((2, steps), lambda h: (0, 0)), seq_spec, seq_spec, seq_spec, head_spec(steps, 0), mode_spec, one_spec],
        [jax.ShapeDtypeStruct((2 * steps, LANES), F32), seq, mode, pos(SUB)],
        [pl.BlockSpec((2 * steps, LANES), lambda h: (0, 0)), seq_spec, mode_spec, pos_spec(SUB)],
        40,
        "grad_modal",
    )
    gf0_next = shift(gf0_head, "ctx", -1)
    gmx, res_sum, rate_own, lag_own, skip_sum, adjoint_done = call(
        functools.partial(own_adjoint_kernel, modes, steps),
        (gm, u, lam, res, skip),
        [seq_spec, seq_spec, mode_spec, mode_spec, one_spec],
        [seq, mode, mode, mode, one],
        [seq_spec, mode_spec, mode_spec, mode_spec, one_spec],
        160,
        "own_adjoint",
    )
    scale_spec = pl.BlockSpec((2 * steps, LANES), lambda h: (0, 0))
    normed, grad_residual, grad_query, short0, gain_sum, outputs_done = call(
        functools.partial(outputs_kernel, taps, steps),
        (scale, summed, cot_pos, modal, q_ext, gf0_next, filt, gain),
        [scale_spec, seq_spec, seq_spec, seq_spec, ext_spec, pos_spec(SUB), filt_spec, one_spec],
        [wide, wide, wide, pos(taps), one],
        [wide_spec, wide_spec, wide_spec, pos_spec(taps), one_spec],
        50,
        "outputs",
        scratch=[
            pltpu.VMEM((steps * SUB, LANES), F32),
            pltpu.VMEM(((steps + SUB) * SUB, LANES), F32),
        ],
    )
    alpha = carried_in(a_own, lam, steps, "ctx", -1, [adjoint_done, outputs_done])
    early_rows = taps + modes + 2
    early = jnp.concatenate(
        [
            v.reshape(blocks, -1, LANES)
            for v in (short0, res_sum + x_in * a_own, skip_sum, gain_sum)
        ],
        axis=1,
    ).reshape(-1, LANES)
    early, early_other = sum_but_last(early, "ctx")
    late_rows = 2 * taps + modes
    next_spec = pl.BlockSpec((2, 1, SUB * SUB, LANES), lambda h: (0, h, 0, 0))
    gf1, gf2, heads, late, _ = call(
        functools.partial(mixed_kernel, modes, taps, steps),
        (gmx, f1, f2, k_ext, v_ext, lam, res, alpha, x_in, p_own, lag_own, rate_own),
        [seq_spec] * 3 + [ext_spec] * 2 + [mode_spec] * 7,
        [seq, seq, jax.ShapeDtypeStruct((2, blocks, SUB * SUB, LANES), F32), pos(late_rows)],
        [seq_spec, seq_spec, next_spec, pos_spec(late_rows)],
        64,
        "mixed",
    )
    next_head = shift(heads, "ctx", -1)
    grad_key, grad_value, back_done = call(
        functools.partial(back_kernel, taps, steps),
        (gf1, gf2, next_head, filt),
        [seq_spec, seq_spec, next_spec, filt_spec],
        [wide, wide],
        [wide_spec, wide_spec],
        28,
        "back",
        scratch=[
            pltpu.VMEM((steps * SUB, LANES), F32),
            pltpu.VMEM(((steps + SUB) * SUB, LANES), F32),
        ],
    )
    late, late_other = sum_but_last(late, "ctx", back_done)
    late_spec, early_spec = pos_spec(late_rows), pos_spec(early_rows)
    grad_short, grad_residues, grad_rate, grad_skip, grad_gain, _ = call(
        functools.partial(finish_kernel, modes, taps),
        (late, late_other, early, early_other),
        [late_spec, late_spec, early_spec, early_spec],
        [
            jax.ShapeDtypeStruct(short_filter.shape, F32),
            jax.ShapeDtypeStruct(residues.shape, F32),
            jax.ShapeDtypeStruct(residues.shape, F32),
            one,
            one,
        ],
        [short_spec, param_spec, param_spec, one_spec, one_spec],
        1,
        "finish",
        scratch=[
            pltpu.VMEM((late_rows * SUB, LANES), F32),
            pltpu.VMEM((early_rows * SUB, LANES), F32),
        ],
    )
    return (
        normed,
        grad_residual,
        grad_query,
        grad_key,
        grad_value,
        grad_short,
        grad_residues,
        grad_rate,
        grad_skip.reshape(channels),
        grad_gain.reshape(channels),
    )


def solution(mesh):
    both, modes, vector = P("ctx", "tp"), P(None, "tp"), P("tp")
    return jax.shard_map(
        shards,
        mesh=mesh,
        in_specs=(both, both, both, both, P(None, None, "tp"), modes, modes, vector, vector, both),
        out_specs=(both,) * 5 + (P(None, None, "tp"), modes, modes, vector, vector),
        check_vma=False,
    )
```

```python
import functools

import jax
import jax.numpy as jnp
from jax import lax
from jax.experimental import pallas as pl
from jax.experimental.pallas import tpu as pltpu
from jax.sharding import PartitionSpec as P

LANES = 128
SUB = 8
WIDE = SUB * LANES
F32 = jnp.float32
BF16 = jnp.bfloat16
VMEM_LIMIT = 10 * 1024 * 1024


def row(ref, t):
    return ref[pl.ds(pl.multiple_of(t * SUB, SUB), SUB), :]


def put(ref, t, value):
    ref[pl.ds(pl.multiple_of(t * SUB, SUB), SUB), :] = value


def spread(src, dst, first, count):
    def some(i, carry):
        start = pl.multiple_of(i * 16, 16)
        for g in range(SUB):
            piece = src[pl.ds(start, 16), g * LANES : (g + 1) * LANES].astype(F32)
            dst[pl.ds((start + first) * SUB + g, 16, stride=SUB), :] = piece
        return carry

    lax.fori_loop(0, count // 16, some, 0)


def gather_rows(src, dst, count):
    def some(i, carry):
        start = pl.multiple_of(i * 16, 16)
        for g in range(SUB):
            piece = src[pl.ds(start * SUB + g, 16, stride=SUB), :]
            dst[pl.ds(start, 16), g * LANES : (g + 1) * LANES] = piece.astype(dst.dtype)
        return carry

    lax.fori_loop(0, count // 16, some, 0)


def total(values):
    values = list(values)
    while len(values) > 1:
        values = [
            values[i] + values[i + 1] if i + 1 < len(values) else values[i]
            for i in range(0, len(values), 2)
        ]
    return values[0]


def taps_of(filt, stream, taps):
    return [row(filt, stream * taps + j) for j in range(taps)]


def conv_at(window, taps, i):
    margin = len(taps) - 1
    return total([taps[j] * window[margin + i - j] for j in range(margin + 1)])


def trailing_kernel(query, key, value, out):
    for i, ref in enumerate((query, key, value)):
        out[i] = ref[...].astype(F32)[SUB:, :].astype(BF16)


def features_kernel(
    modes, taps, steps, key, value, filt3, decay, resid, k_ext, v_ext, f1, f2, u, g, lam, res, filt, x_out
):
    margin = taps - 1
    for s in range(SUB):
        lanes = slice(s * LANES, (s + 1) * LANES)
        lam[pl.ds(s, modes, stride=SUB), :] = decay[:, lanes]
        res[pl.ds(s, modes, stride=SUB), :] = resid[:, lanes]
        for i in range(3):
            filt[pl.ds(i * taps * SUB + s, taps, stride=SUB), :] = filt3[i, :, lanes]
    spread(key, k_ext, SUB, steps)
    spread(value, v_ext, SUB, steps)
    taps1, taps2 = taps_of(filt, 1, taps), taps_of(filt, 2, taps)

    def conv(c, carry):
        t0 = c * SUB
        kw = [row(k_ext, t0 + SUB - margin + i) for i in range(SUB + margin)]
        for i in range(SUB):
            put(f1, t0 + i, conv_at(kw, taps1, i))
        vw = [row(v_ext, t0 + SUB - margin + i) for i in range(SUB + margin)]
        for i in range(SUB):
            second = conv_at(vw, taps2, i)
            put(f2, t0 + i, second)
            put(u, t0 + i, second * row(f1, t0 + i))
        return carry

    lax.fori_loop(1, steps // SUB, conv, 0)
    fade, skip = fades(lam, modes, 1), fades(lam, modes, SUB)

    def advance(c, x):
        now = [row(u, c * SUB + i) for i in range(SUB)]
        new = []
        for m in range(modes):
            own = horner(fade[m], now)
            put(g, c * modes + m, own)
            new.append(own + skip[m] * x[m])
        return tuple(new)

    x = lax.fori_loop(1, steps // SUB, advance, zeros(modes))
    for m in range(modes):
        put(x_out, m, x[m])


def zeros(count):
    return tuple(jnp.zeros((SUB, LANES), F32) for _ in range(count))


def fades(lam, modes, span):
    return [jnp.exp(row(lam, m) * -float(span)) for m in range(modes)]


def horner(fade, values):
    result = values[0]
    for value in values[1:]:
        result = fade * result + value
    return result


def head_kernel(
    modes, taps, steps, halo, k_head, v_head, filt, lam, x_part, f1_in, f2_in, u_in, g_in,
    k_ext, v_ext, f1, f2, u, g, x_out,
):
    del f1_in, f2_in, u_in, g_in
    margin = taps - 1
    for s in range(SUB):
        lanes = slice(s * LANES, (s + 1) * LANES)
        k_ext[pl.ds(s, SUB, stride=SUB), :] = halo[1, :, lanes].astype(F32)
        v_ext[pl.ds(s, SUB, stride=SUB), :] = halo[2, :, lanes].astype(F32)
    taps1, taps2 = taps_of(filt, 1, taps), taps_of(filt, 2, taps)
    kw = [row(k_ext, SUB - margin + i) for i in range(margin)] + [row(k_head, i) for i in range(SUB)]
    vw = [row(v_ext, SUB - margin + i) for i in range(margin)] + [row(v_head, i) for i in range(SUB)]
    mixed = []
    for i in range(SUB):
        first, second = conv_at(kw, taps1, i), conv_at(vw, taps2, i)
        put(f1, i, first)
        put(f2, i, second)
        put(u, i, first * second)
        mixed.append(first * second)
    fade, rest = fades(lam, modes, 1), fades(lam, modes, steps - SUB)
    for m in range(modes):
        own = horner(fade[m], mixed)
        put(g, m, own)
        put(x_out, m, row(x_part, m) + rest[m] * own)


def query_kernel(taps, steps, query, halo, filt, q_ext, f0):
    margin = taps - 1
    for s in range(SUB):
        lanes = slice(s * LANES, (s + 1) * LANES)
        q_ext[pl.ds(s, SUB, stride=SUB), :] = halo[0, :, lanes].astype(F32)
    spread(query, q_ext, SUB, steps)
    taps0 = taps_of(filt, 0, taps)

    def conv(c, carry):
        t0 = c * SUB
        qw = [row(q_ext, t0 + SUB - margin + i) for i in range(SUB + margin)]
        for i in range(SUB):
            put(f0, t0 + i, conv_at(qw, taps0, i))
        return carry

    lax.fori_loop(0, steps // SUB, conv, 0)


def inputs_kernel(steps, residual, cot, res_pos, cot_pos):
    spread(residual, res_pos, 0, steps)
    spread(cot, cot_pos, 0, steps)


def near_taps(lam, res, skip, modes):
    fade, weight = fades(lam, modes, 1), [row(res, m) for m in range(modes)]
    result = []
    for k in range(SUB):
        result.append(total(weight) if k else total(weight) + skip[...])
        weight = [f * w for f, w in zip(fade, weight)]
    return result


def near_kernel(modes, steps, u, lam, res, skip, y):
    near = near_taps(lam, res, skip, modes)

    def some(c, carry):
        now = [row(u, c * SUB + i) for i in range(SUB)]
        for i in range(SUB):
            put(y, c * SUB + i, total([near[k] * now[i - k] for k in range(i + 1)]))
        return carry

    lax.fori_loop(0, steps // SUB, some, 0)


def lags_kernel(modes, steps, u, x_at, lam, lag, lag_sum):
    fade, skip = fades(lam, modes, 1), fades(lam, modes, SUB)

    def some(c, sums):
        now = [row(u, c * SUB + i) * float(SUB - i) for i in range(SUB)]
        new = []
        for m in range(modes):
            border = horner(fade[m], now) + float(SUB) * skip[m] * row(x_at, c * modes + m)
            put(lag, c * modes + m, border)
            new.append(skip[m] * sums[m] + border)
        return tuple(new)

    sums = lax.fori_loop(0, steps // SUB, some, zeros(modes))
    for m in range(modes):
        put(lag_sum, m, sums[m])


def summed_kernel(modes, steps, blocks, y, f0, res_pos, cot_pos, g, x_in, lam, res, gain, modal, summed, x_at, sums, squares, inner):
    block = pl.program_id(0)

    @pl.when(block == 0)
    def _():
        squares[...] = jnp.zeros_like(squares)
        inner[...] = jnp.zeros_like(inner)

    fade, skip = fades(lam, modes, 1), fades(lam, modes, SUB)
    factor = gain[...]

    def advance(c, x):
        w = [row(res, m) * x[m] for m in range(modes)]
        for m in range(modes):
            put(x_at, c * modes + m, x[m])
        for i in range(SUB):
            t = c * SUB + i
            w = [f * v for f, v in zip(fade, w)]
            long = row(y, t) + total(w)
            put(modal, t, long)
            now = row(res_pos, t) + row(f0, t) * long
            put(summed, t, now)
            put(squares, t, row(squares, t) + now * now)
            put(inner, t, row(inner, t) + factor * row(cot_pos, t) * now)
        return tuple(row(g, c * modes + m) + skip[m] * x[m] for m in range(modes))

    lax.fori_loop(0, steps // SUB, advance, tuple(row(x_in, m) for m in range(modes)))

    @pl.when(block == blocks - 1)
    def _():
        for which, scratch in enumerate((squares, inner)):
            for b in range(steps // LANES):
                part = total(
                    [
                        scratch[pl.ds(b * LANES * SUB + s, LANES, stride=SUB), :]
                        for s in range(SUB)
                    ]
                )
                sums[which : which + 1, b * LANES : (b + 1) * LANES] = jnp.sum(
                    part.T, axis=0, keepdims=True
                )


def grad_modal_kernel(modes, steps, width, shares, *refs):
    own_sums, (summed, cot_pos, f0, modal, lam, gain, ready) = refs[:shares], refs[shares : shares + 7]
    scale, gm, adj, a_out, border = refs[shares + 7 :]
    del ready

    @pl.when(pl.program_id(0) == 0)
    def _():
        sums = total([ref[...] for ref in own_sums])
        inv = lax.rsqrt(sums[0:1, :] / width + 1e-05)
        coef = inv * inv * inv * sums[1:2, :] / width
        for which, value in enumerate((inv, coef)):
            for b in range(steps // LANES):
                piece = value[:, b * LANES : (b + 1) * LANES]
                scale[pl.ds(which * steps + b * LANES, LANES), :] = jnp.broadcast_to(
                    piece, (LANES, LANES)
                ).T

    fade, skip = fades(lam, modes, 1), fades(lam, modes, SUB)
    factor = gain[...]

    def advance(c, a):
        block = steps // SUB - 1 - c
        now = [None] * SUB
        for i in reversed(range(SUB)):
            t = block * SUB + i
            inv = scale[pl.ds(t, 1), :]
            coef = scale[pl.ds(steps + t, 1), :]
            grad = inv * (factor * row(cot_pos, t)) - coef * row(summed, t)
            now[i] = grad * row(f0, t)
            put(gm, t, now[i])
        new = []
        for m in range(modes):
            own = fade[m] * horner(fade[m], now[::-1])
            put(adj, block * modes + m, own)
            new.append(own + skip[m] * a[m])
        return tuple(new)

    a = lax.fori_loop(0, steps // SUB, advance, zeros(modes))
    for m in range(modes):
        put(a_out, m, a[m])
        put(border, m, a[m])
    for t in range(SUB):
        inv = scale[pl.ds(t, 1), :]
        coef = scale[pl.ds(steps + t, 1), :]
        grad = inv * (factor * row(cot_pos, t)) - coef * row(summed, t)
        put(border, modes + t, grad * row(modal, t))


def own_adjoint_kernel(modes, steps, gm, u, adj, x_at, lag, lam, res, skip, gmy, res_sum, rate_sum, skip_sum):
    near = near_taps(lam, res, skip, modes)
    fade, far = fades(lam, modes, 1), fades(lam, modes, SUB)
    last = steps // SUB - 1

    def pairs(c, lags):
        now = [row(gm, c * SUB + i) for i in range(SUB)]
        for i in range(SUB):
            put(gmy, c * SUB + i, total([near[k] * now[i + k] for k in range(SUB - i)]))
        before = [row(u, c * SUB + i) for i in range(SUB)]
        return tuple(
            lags[k] + total([now[i] * before[i - k] for i in range(k, SUB)]) for k in range(SUB)
        )

    lags = lax.fori_loop(0, steps // SUB, pairs, zeros(SUB))
    skip_sum[...] = lags[0]
    half = modes // 2
    for part in range(2):
        ms = range(part * half, (part + 1) * half)

        def across(c, state, ms=ms):
            after, by_res, by_rate = (list(v) for v in state)
            block = last - c
            now = [row(gm, block * SUB + i) * float(i) for i in range(1, SUB)]
            for i, m in enumerate(ms):
                x, own = row(x_at, block * modes + m), row(adj, block * modes + m)
                tail = fade[m] * fade[m] * horner(fade[m], now[::-1])
                by_res[i] = by_res[i] + x * own
                by_rate[i] = by_rate[i] + (x * tail + after[i] * row(lag, block * modes + m))
                after[i] = own + far[m] * after[i]
            return tuple(after), tuple(by_res), tuple(by_rate)

        none = zeros(half)
        _, by_res, by_rate = lax.fori_loop(0, steps // SUB, across, (none, none, none))
        for i, m in enumerate(ms):
            put(res_sum, m, by_res[i] + horner(fade[m], lags[::-1]))
            weighted = [lags[k] * float(k) for k in range(1, SUB)]
            put(rate_sum, m, by_rate[i] + fade[m] * horner(fade[m], weighted[::-1]))


def norm_kernel(steps, scale, summed, cot_pos, gain, normed, grad_res, gain_out, work):
    factor = gain[...]

    def norm(c, acc):
        for i in range(SUB):
            t = c * SUB + i
            here = row(summed, t) * scale[pl.ds(t, 1), :]
            put(work, t, here * factor)
            acc = acc + row(cot_pos, t) * here
        return acc

    gain_out[...] = lax.fori_loop(0, steps // SUB, norm, zeros(1)[0])
    gather_rows(work, normed, steps)

    def grads(c, carry):
        for i in range(SUB):
            t = c * SUB + i
            inv = scale[pl.ds(t, 1), :]
            coef = scale[pl.ds(steps + t, 1), :]
            put(work, t, inv * (factor * row(cot_pos, t)) - coef * row(summed, t))
        return carry

    lax.fori_loop(0, steps // SUB, grads, 0)
    gather_rows(work, grad_res, steps)


def grad_query_kernel(modes, taps, steps, scale, summed, cot_pos, modal, q_ext, gf0_next, filt, gain, res_sum, skip_sum, gain_sum, grad_query, early, work, gf0):
    factor = gain[...]
    gf0[pl.ds(steps * SUB, SUB * SUB), :] = gf0_next[...]
    taps0 = taps_of(filt, 0, taps)

    def grads(c, carry):
        for i in range(SUB):
            t = c * SUB + i
            inv = scale[pl.ds(t, 1), :]
            coef = scale[pl.ds(steps + t, 1), :]
            grad = inv * (factor * row(cot_pos, t)) - coef * row(summed, t)
            put(gf0, t, grad * row(modal, t))
        return carry

    lax.fori_loop(0, steps // SUB, grads, 0)
    sums = filter_pass(taps, steps, gf0, q_ext)
    for j in range(taps):
        put(early, j, sums[j])
    early[pl.ds(taps * SUB, modes * SUB), :] = res_sum[...]
    put(early, taps + modes, skip_sum[...])
    put(early, taps + modes + 1, gain_sum[...])
    back_pass(taps, steps, gf0, taps0, work)
    gather_rows(work, grad_query, steps)


def filter_pass(taps, steps, grad, ext):
    margin = taps - 1

    def some(c, acc):
        t0 = c * SUB
        window = [row(ext, t0 + SUB - margin + i) for i in range(SUB + margin)]
        for i in range(SUB):
            now = row(grad, t0 + i)
            acc = tuple(acc[j] + now * window[margin + i - j] for j in range(taps))
        return acc

    zero = jnp.zeros((SUB, LANES), F32)
    return lax.fori_loop(0, steps // SUB, some, tuple(zero for _ in range(taps)))


def back_pass(taps, steps, grad, weights, out):
    margin = taps - 1

    def some(c, carry):
        t0 = c * SUB
        window = [row(grad, t0 + i) for i in range(SUB + margin)]
        for i in range(SUB):
            put(out, t0 + i, total([weights[j] * window[i + j] for j in range(taps)]))
        return carry

    lax.fori_loop(0, steps // SUB, some, 0)


def mixed_kernel(modes, taps, steps, gmy, f1, f2, k_ext, v_ext, adj, lam, res, alpha, gf1, gf2, heads, sums):
    fade, skip = fades(lam, modes, 1), fades(lam, modes, SUB)

    def advance(c, after):
        block = steps // SUB - 1 - c
        w = [row(res, m) * after[m] for m in range(modes)]
        for i in reversed(range(SUB)):
            t = block * SUB + i
            grad = row(gmy, t) + total(w)
            put(gf1, t, grad * row(f2, t))
            put(gf2, t, grad * row(f1, t))
            w = [f * v for f, v in zip(fade, w)]
        return tuple(row(adj, block * modes + m) + skip[m] * after[m] for m in range(modes))

    lax.fori_loop(0, steps // SUB, advance, tuple(row(alpha, m) for m in range(modes)))
    heads[0, 0] = gf1[: SUB * SUB, :]
    heads[1, 0] = gf2[: SUB * SUB, :]
    for which, (grad, ext) in enumerate(((gf1, k_ext), (gf2, v_ext))):
        parts = filter_pass(taps, steps, grad, ext)
        for j in range(taps):
            put(sums, which * taps + j, parts[j])


def back_kernel(taps, steps, gf1, gf2, next_head, filt, grad_key, grad_value, work, ext):
    for which, (grad, out) in enumerate(((gf1, grad_key), (gf2, grad_value))):
        ext[pl.ds(0, steps * SUB), :] = grad[...]
        ext[pl.ds(steps * SUB, SUB * SUB), :] = next_head[which, 0]
        back_pass(taps, steps, ext, taps_of(filt, which + 1, taps), work)
        gather_rows(work, out, steps)


def pack_kernel(modes, first_rows, half, early, res, rate_sum, lag_sum, alpha, kept, sent):
    odd = lax.axis_index("ctx") % 2
    rows = (first_rows + modes) * SUB
    for out, start in ((kept, odd * half), (sent, (1 - odd) * half)):
        for b in range(half):
            source = pl.multiple_of((start + b) * (first_rows * SUB), SUB)
            out[pl.ds(b * rows, first_rows * SUB), :] = early[pl.ds(source, first_rows * SUB), :]
            source = pl.multiple_of((start + b) * (modes * SUB), SUB)
            mine = pl.ds(source, modes * SUB)
            lagged = rate_sum[mine, :] + alpha[mine, :] * lag_sum[mine, :]
            out[pl.ds(b * rows + first_rows * SUB, modes * SUB), :] = -res[mine, :] * lagged


def finish_kernel(modes, taps, half, late, late_other, early, early_other, short, res, rate, skip, gain, work, work2):
    odd = lax.axis_index("ctx") % 2
    mine = jnp.where(odd == pl.program_id(0) // half, 1.0, 0.0)
    work[...] = late[...] + late_other[...]
    work2[...] = mine * early[...] + (1.0 - mine) * early_other[...]
    for s in range(SUB):
        lanes = slice(s * LANES, (s + 1) * LANES)
        short[0, :, lanes] = work2[pl.ds(s, taps, stride=SUB), :]
        short[1, :, lanes] = work[pl.ds(s, taps, stride=SUB), :]
        short[2, :, lanes] = work[pl.ds(taps * SUB + s, taps, stride=SUB), :]
        res[:, lanes] = work2[pl.ds(taps * SUB + s, modes, stride=SUB), :]
        rate[:, lanes] = work2[pl.ds((taps + modes + 2) * SUB + s, modes, stride=SUB), :]
    skip[...] = row(work2, taps + modes)
    gain[...] = row(work2, taps + modes + 1)


def shift(value, axis, distance):
    devices = range(lax.axis_size(axis))
    route = [(i - distance, i) for i in devices if i - distance in devices]
    return lax.ppermute(value, axis, route)


def carried_in(own, first, lam, span, axis, sign, under):
    count, reach = lax.axis_size(axis), 1
    under = list(under) + [None] * count
    before, upto = None, own
    while reach < count:
        other = first if reach == 1 else shift(upto, axis, sign * reach)
        wait = under.pop(0)
        if wait is not None:
            other = other + wait
        before = other if before is None else before + jnp.exp(lam * -float(span * (reach - 1))) * other
        upto = upto + jnp.exp(lam * -float(span * reach)) * other
        reach *= 2
    return before


def others_of(value, axis):
    count = lax.axis_size(axis)
    return [
        lax.ppermute(value, axis, [(i, (i + k) % count) for i in range(count)])
        for k in range(1, count)
    ]


def swap(value, axis, step):
    return lax.ppermute(value, axis, [(i, i ^ step) for i in range(lax.axis_size(axis))])


def sum_but_last(value, axis, first, under=None):
    count, step = lax.axis_size(axis), first
    while True:
        other = swap(value, axis, step)
        step *= 2
        if step >= count:
            return value, other
        value = value + other if under is None else value + other + under
        under = None


def shards(
    residual, query_in, key_in, value_in, short_filter, residues, decay_rate, skip_gain, norm_gain, cotangent
):
    steps, channels = residual.shape
    modes, taps = residues.shape[0], short_filter.shape[1]
    blocks = channels // WIDE
    width = channels * lax.axis_size("tp")
    skip, gain = (v.reshape(blocks * SUB, LANES) for v in (skip_gain, norm_gain))

    def pos(count):
        return jax.ShapeDtypeStruct((blocks * count * SUB, LANES), F32)

    def kept(count):
        return pltpu.VMEM((blocks * count * SUB, LANES), F32)

    def pos_spec(count):
        return pl.BlockSpec((count * SUB, LANES), lambda h: (h, 0))

    def head_spec(total_steps, start):
        return pl.BlockSpec((SUB * SUB, LANES), lambda h: (h * (total_steps // SUB) + start, 0))

    wide_spec = pl.BlockSpec((steps, WIDE), lambda h: (0, h))
    wide = jax.ShapeDtypeStruct((steps, channels), BF16)
    mode_spec, one_spec, filt_spec = pos_spec(modes), pos_spec(1), pos_spec(3 * taps)
    seq_spec, ext_spec = pos_spec(steps), pos_spec(steps + SUB)
    seq, ext, mode, one = kept(steps), kept(steps + SUB), pos(modes), pos(1)
    eights, eights_spec = kept(steps // SUB * modes), pos_spec(steps // SUB * modes)
    halo_spec = pl.BlockSpec((3, SUB, WIDE), lambda h: (0, 0, h))
    param_spec = pl.BlockSpec((modes, WIDE), lambda h: (0, h))
    short_spec = pl.BlockSpec((3, taps, WIDE), lambda h: (0, 0, h))

    def call(body, ins, in_specs, outs, out_specs, ops, name, scratch=(), aliases=None, done_rows=None):
        elements, n_refs = steps * channels, len(ins) + len(outs)

        def with_done(*refs):
            done = refs[n_refs]
            done[...] = jnp.zeros_like(done)
            body(*refs[:n_refs], *refs[n_refs + 1 :])

        near = blocks * steps * SUB
        ins = [
            pltpu.with_memory_space_constraint(v, pltpu.VMEM) if v.shape[0] >= near and v.dtype == F32 else v
            for v in ins
        ]
        done_shape = (blocks * (done_rows or modes) * SUB, LANES)
        outs = [*outs, jax.ShapeDtypeStruct(done_shape, F32)]
        out_specs = [*out_specs, pl.BlockSpec(done_shape, lambda h: (0, 0))]
        return pl.pallas_call(
            with_done,
            grid=(blocks,),
            in_specs=in_specs,
            out_specs=out_specs,
            out_shape=outs,
            scratch_shapes=list(scratch),
            input_output_aliases=aliases or {},
            compiler_params=pltpu.CompilerParams(
                dimension_semantics=("arbitrary",), vmem_limit_bytes=VMEM_LIMIT
            ),
            cost_estimate=pl.CostEstimate(
                flops=ops * elements, bytes_accessed=4 * elements, transcendentals=0
            ),
            name=name,
        )(*ins)

    far = [
        pltpu.with_memory_space_constraint(v, pltpu.HBM)
        for v in (residual, query_in, key_in, value_in, cotangent, short_filter, decay_rate, residues)
    ]
    last_spec = pl.BlockSpec((2 * SUB, channels), lambda h: (steps // (2 * SUB) - 1, 0))
    trailing = pl.pallas_call(
        trailing_kernel,
        grid=(1,),
        in_specs=[last_spec] * 3,
        out_specs=pl.BlockSpec((3, SUB, channels), lambda h: (0, 0, 0)),
        out_shape=jax.ShapeDtypeStruct((3, SUB, channels), BF16),
        compiler_params=pltpu.CompilerParams(vmem_limit_bytes=VMEM_LIMIT),
        cost_estimate=pl.CostEstimate(flops=channels, bytes_accessed=channels, transcendentals=0),
        name="trailing",
    )(*far[1:4])
    halo = shift(trailing, "ctx", 1)

    k_ext, v_ext, f1, f2, u, g, lam, res, filt, x_part, _ = call(
        functools.partial(features_kernel, modes, taps, steps),
        (far[2], far[3], *far[5:]),
        [wide_spec, wide_spec, short_spec, param_spec, param_spec],
        [ext, ext, seq, seq, seq, eights, mode, mode, pos(3 * taps), mode],
        [ext_spec, ext_spec, seq_spec, seq_spec, seq_spec, eights_spec, mode_spec, mode_spec, filt_spec, mode_spec],
        64,
        "features",
    )
    any_spec = pl.BlockSpec(memory_space=pl.ANY)
    k_ext, v_ext, f1, f2, u, g, x_own, _ = call(
        functools.partial(head_kernel, modes, taps, steps),
        (halo, k_ext, v_ext, filt, lam, x_part, f1, f2, u, g),
        [halo_spec, head_spec(steps + SUB, 1), head_spec(steps + SUB, 1), filt_spec, mode_spec, mode_spec]
        + [any_spec] * 4,
        [ext, ext, seq, seq, seq, eights, mode],
        [head_spec(steps + SUB, 0)] * 2
        + [head_spec(steps, 0)] * 3
        + [pl.BlockSpec((modes * SUB, LANES), lambda h: (h * (steps // SUB), 0)), mode_spec],
        2,
        "head",
        aliases={1: 0, 2: 1, 6: 2, 7: 3, 8: 4, 9: 5},
    )
    q_ext, f0, query_done = call(
        functools.partial(query_kernel, taps, steps),
        (far[1], halo, filt),
        [wide_spec, halo_spec, filt_spec],
        [ext, seq],
        [ext_spec, seq_spec],
        20,
        "query",
    )
    res_pos, cot_pos, inputs_done = call(
        functools.partial(inputs_kernel, steps),
        (far[0], far[4]),
        [wide_spec] * 2,
        [seq, seq],
        [seq_spec] * 2,
        10,
        "inputs",
    )
    y, near_done = call(
        functools.partial(near_kernel, modes, steps),
        (u, lam, res, skip),
        [seq_spec, mode_spec, mode_spec, one_spec],
        [seq],
        [seq_spec],
        10,
        "near",
    )
    x_in = carried_in(x_own, shift(x_own, "ctx", 1), lam, steps, "ctx", 1, [query_done, inputs_done, near_done])
    modal, summed, x_at, sums, _ = call(
        functools.partial(summed_kernel, modes, steps, blocks),
        (y, f0, res_pos, cot_pos, g, x_in, lam, res, gain),
        [seq_spec] * 4 + [eights_spec] + [mode_spec] * 3 + [one_spec],
        [seq, seq, eights, jax.ShapeDtypeStruct((2, steps), F32)],
        [seq_spec, seq_spec, eights_spec, pl.BlockSpec((2, steps), lambda h: (0, 0))],
        50,
        "summed",
        scratch=[pltpu.VMEM((steps * SUB, LANES), F32)] * 2,
    )
    all_sums = [sums, *others_of(sums, "tp")]
    lag, lag_sum, lags_done = call(
        functools.partial(lags_kernel, modes, steps),
        (u, x_at, lam),
        [seq_spec, eights_spec, mode_spec],
        [eights, mode],
        [eights_spec, mode_spec],
        32,
        "lags",
    )
    scale_spec = pl.BlockSpec((2 * steps, LANES), lambda h: (0, 0))
    scale, gm, adj, a_own, border, _ = call(
        functools.partial(grad_modal_kernel, modes, steps, width, len(all_sums)),
        (*all_sums, summed, cot_pos, f0, modal, lam, gain, lags_done),
        [pl.BlockSpec((2, steps), lambda h: (0, 0))] * len(all_sums)
        + [seq_spec, seq_spec, seq_spec, head_spec(steps, 0), mode_spec, one_spec, any_spec],
        [pltpu.VMEM((2 * steps, LANES), F32), seq, eights, mode, pos(modes + SUB)],
        [scale_spec, seq_spec, eights_spec, mode_spec, pos_spec(modes + SUB)],
        45,
        "grad_modal",
    )
    border = shift(border, "ctx", -1)
    normed, grad_residual, gain_sum, norm_done = call(
        functools.partial(norm_kernel, steps),
        (scale, summed, cot_pos, gain),
        [scale_spec, seq_spec, seq_spec, one_spec],
        [wide, wide, one],
        [wide_spec, wide_spec, one_spec],
        25,
        "norm",
        scratch=[pltpu.VMEM((steps * SUB, LANES), F32)],
    )
    gmy, res_sum, rate_sum, skip_sum, adjoint_done = call(
        functools.partial(own_adjoint_kernel, modes, steps),
        (gm, u, adj, x_at, lag, lam, res, skip),
        [seq_spec, seq_spec, eights_spec, eights_spec, eights_spec, mode_spec, mode_spec, one_spec],
        [seq, mode, mode, one],
        [seq_spec, mode_spec, mode_spec, one_spec],
        75,
        "own_adjoint",
    )
    early_rows = taps + modes + 2
    grad_query, early, query_back_done = call(
        functools.partial(grad_query_kernel, modes, taps, steps),
        (scale, summed, cot_pos, modal, q_ext, border, filt, gain, res_sum, skip_sum, gain_sum),
        [scale_spec, seq_spec, seq_spec, seq_spec, ext_spec, head_spec(modes + SUB, modes // SUB), filt_spec, one_spec, mode_spec, one_spec, one_spec],
        [wide, pos(early_rows)],
        [wide_spec, pos_spec(early_rows)],
        45,
        "grad_query",
        scratch=[
            pltpu.VMEM((steps * SUB, LANES), F32),
            pltpu.VMEM(((steps + SUB) * SUB, LANES), F32),
        ],
    )
    border_rows = modes + SUB
    alpha_first = border.reshape(blocks, border_rows * SUB, LANES)[:, : modes * SUB]
    alpha = carried_in(a_own, alpha_first.reshape(a_own.shape), lam, steps, "ctx", -1, [norm_done, adjoint_done, query_back_done])

    half = blocks // 2
    whole_spec = pl.BlockSpec(memory_space=pltpu.VMEM)
    half_shape = jax.ShapeDtypeStruct((half * (early_rows + modes) * SUB, LANES), F32)
    kept_half, sent_half = pl.pallas_call(
        functools.partial(pack_kernel, modes, early_rows, half),
        in_specs=[whole_spec] * 5,
        out_specs=[whole_spec] * 2,
        out_shape=[half_shape] * 2,
        compiler_params=pltpu.CompilerParams(vmem_limit_bytes=VMEM_LIMIT),
        cost_estimate=pl.CostEstimate(flops=half_shape.size, bytes_accessed=0, transcendentals=0),
        name="pack",
    )(early, res, rate_sum, lag_sum, alpha)
    early_rows += modes
    early = kept_half + swap(sent_half, "ctx", 1)
    late_rows = 2 * taps
    next_spec = pl.BlockSpec((2, 1, SUB * SUB, LANES), lambda h: (0, h, 0, 0))
    gf1, gf2, heads, late, _ = call(
        functools.partial(mixed_kernel, modes, taps, steps),
        (gmy, f1, f2, k_ext, v_ext, adj, lam, res, alpha),
        [seq_spec] * 3 + [ext_spec] * 2 + [eights_spec] + [mode_spec] * 3,
        [seq, seq, jax.ShapeDtypeStruct((2, blocks, SUB * SUB, LANES), F32), pos(late_rows)],
        [seq_spec, seq_spec, next_spec, pos_spec(late_rows)],
        75,
        "mixed",
    )
    next_head = shift(heads, "ctx", -1)
    grad_key, grad_value, back_done = call(
        functools.partial(back_kernel, taps, steps),
        (gf1, gf2, next_head, filt),
        [seq_spec, seq_spec, next_spec, filt_spec],
        [wide, wide],
        [wide_spec, wide_spec],
        28,
        "back",
        scratch=[
            pltpu.VMEM((steps * SUB, LANES), F32),
            pltpu.VMEM(((steps + SUB) * SUB, LANES), F32),
        ],
        done_rows=late_rows,
    )
    if lax.axis_size("ctx") > 2:
        one_part, other_part = sum_but_last(early, "ctx", 2)
        early = one_part + other_part
    early_other = swap(early, "ctx", 1)
    late, late_other = sum_but_last(late, "ctx", 1, back_done)
    late_spec = pos_spec(late_rows)
    half_spec = pl.BlockSpec((early_rows * SUB, LANES), lambda h: (h % half, 0))
    grad_short, grad_residues, grad_rate, grad_skip, grad_gain, _ = call(
        functools.partial(finish_kernel, modes, taps, half),
        (late, late_other, early, early_other),
        [late_spec, late_spec, half_spec, half_spec],
        [
            jax.ShapeDtypeStruct(short_filter.shape, F32),
            jax.ShapeDtypeStruct(residues.shape, F32),
            jax.ShapeDtypeStruct(residues.shape, F32),
            one,
            one,
        ],
        [short_spec, param_spec, param_spec, one_spec, one_spec],
        1,
        "finish",
        scratch=[
            pltpu.VMEM((late_rows * SUB, LANES), F32),
            pltpu.VMEM((early_rows * SUB, LANES), F32),
        ],
    )
    return (
        normed,
        grad_residual,
        grad_query,
        grad_key,
        grad_value,
        grad_short,
        grad_residues,
        grad_rate,
        grad_skip.reshape(channels),
        grad_gain.reshape(channels),
    )


def solution(mesh):
    both, modes, vector = P("ctx", "tp"), P(None, "tp"), P("tp")
    return jax.shard_map(
        shards,
        mesh=mesh,
        in_specs=(both, both, both, both, P(None, None, "tp"), modes, modes, vector, vector, both),
        out_specs=(both,) * 5 + (P(None, None, "tp"), modes, modes, vector, vector),
        check_vma=False,
    )
```

```python
import functools

import jax
import jax.numpy as jnp
from jax import lax
from jax.experimental import pallas as pl
from jax.experimental.pallas import tpu as pltpu
from jax.sharding import PartitionSpec as P

LANES = 128
SUB = 8
WIDE = SUB * LANES
F32 = jnp.float32
BF16 = jnp.bfloat16
VMEM_LIMIT = 10 * 1024 * 1024


def row(ref, t):
    return ref[pl.ds(pl.multiple_of(t * SUB, SUB), SUB), :]


def put(ref, t, value):
    ref[pl.ds(pl.multiple_of(t * SUB, SUB), SUB), :] = value


def loop(start, stop, body, carry):
    pairs = (stop - start) // 2

    def two(i, carry):
        return body(start + 2 * i + 1, body(start + 2 * i, carry))

    carry = lax.fori_loop(0, pairs, two, carry)
    return body(stop - 1, carry) if (stop - start) % 2 else carry


def spread(src, dst, first, count):
    def some(i, carry):
        start = pl.multiple_of(i * 16, 16)
        for g in range(SUB):
            piece = src[pl.ds(start, 16), g * LANES : (g + 1) * LANES].astype(F32)
            dst[pl.ds((start + first) * SUB + g, 16, stride=SUB), :] = piece
        return carry

    loop(0, count // 16, some, 0)


def gather_rows(src, dst, count):
    def some(i, carry):
        start = pl.multiple_of(i * 16, 16)
        for g in range(SUB):
            piece = src[pl.ds(start * SUB + g, 16, stride=SUB), :]
            dst[pl.ds(start, 16), g * LANES : (g + 1) * LANES] = piece.astype(dst.dtype)
        return carry

    loop(0, count // 16, some, 0)


def total(values):
    values = list(values)
    while len(values) > 1:
        values = [
            values[i] + values[i + 1] if i + 1 < len(values) else values[i]
            for i in range(0, len(values), 2)
        ]
    return values[0]


def taps_of(filt, stream, taps):
    return [row(filt, stream * taps + j) for j in range(taps)]


def conv_at(window, taps, i):
    margin = len(taps) - 1
    return total([taps[j] * window[margin + i - j] for j in range(margin + 1)])


def trailing_kernel(query, key, value, out):
    for i, ref in enumerate((query, key, value)):
        out[i] = ref[...].astype(F32)[SUB:, :].astype(BF16)


def features_kernel(
    modes, taps, steps, key, value, filt3, decay, resid, k_ext, v_ext, f1, f2, u, g, lam, res, filt, x_out
):
    margin = taps - 1
    for s in range(SUB):
        lanes = slice(s * LANES, (s + 1) * LANES)
        lam[pl.ds(s, modes, stride=SUB), :] = decay[:, lanes]
        res[pl.ds(s, modes, stride=SUB), :] = resid[:, lanes]
        for i in range(3):
            filt[pl.ds(i * taps * SUB + s, taps, stride=SUB), :] = filt3[i, :, lanes]
    spread(key, k_ext, SUB, steps)
    spread(value, v_ext, SUB, steps)
    taps1, taps2 = taps_of(filt, 1, taps), taps_of(filt, 2, taps)

    def conv(c, carry):
        t0 = c * SUB
        kw = [row(k_ext, t0 + SUB - margin + i) for i in range(SUB + margin)]
        for i in range(SUB):
            put(f1, t0 + i, conv_at(kw, taps1, i))
        vw = [row(v_ext, t0 + SUB - margin + i) for i in range(SUB + margin)]
        for i in range(SUB):
            second = conv_at(vw, taps2, i)
            put(f2, t0 + i, second)
            put(u, t0 + i, second * row(f1, t0 + i))
        return carry

    loop(1, steps // SUB, conv, 0)
    fade, skip = fades(lam, modes, 1), fades(lam, modes, SUB)

    def advance(c, x):
        now = [row(u, c * SUB + i) for i in range(SUB)]
        new = []
        for m in range(modes):
            own = horner(fade[m], now)
            put(g, c * modes + m, own)
            new.append(own + skip[m] * x[m])
        return tuple(new)

    x = loop(1, steps // SUB, advance, zeros(modes))
    for m in range(modes):
        put(x_out, m, x[m])


def zeros(count):
    return tuple(jnp.zeros((SUB, LANES), F32) for _ in range(count))


def fades(lam, modes, span):
    return [jnp.exp(row(lam, m) * -float(span)) for m in range(modes)]


def horner(fade, values):
    result = values[0]
    for value in values[1:]:
        result = fade * result + value
    return result


def head_kernel(
    modes, taps, steps, halo, k_head, v_head, filt, lam, x_part, f1_in, f2_in, u_in, g_in,
    k_ext, v_ext, f1, f2, u, g, x_out,
):
    del f1_in, f2_in, u_in, g_in
    margin = taps - 1
    there = jnp.where(lax.axis_index("ctx") > 0, 1.0, 0.0)
    for s in range(SUB):
        lanes = slice(s * LANES, (s + 1) * LANES)
        k_ext[pl.ds(s, SUB, stride=SUB), :] = halo[1, :, lanes].astype(F32) * there
        v_ext[pl.ds(s, SUB, stride=SUB), :] = halo[2, :, lanes].astype(F32) * there
    taps1, taps2 = taps_of(filt, 1, taps), taps_of(filt, 2, taps)
    kw = [row(k_ext, SUB - margin + i) for i in range(margin)] + [row(k_head, i) for i in range(SUB)]
    vw = [row(v_ext, SUB - margin + i) for i in range(margin)] + [row(v_head, i) for i in range(SUB)]
    mixed = []
    for i in range(SUB):
        first, second = conv_at(kw, taps1, i), conv_at(vw, taps2, i)
        put(f1, i, first)
        put(f2, i, second)
        put(u, i, first * second)
        mixed.append(first * second)
    fade, rest = fades(lam, modes, 1), fades(lam, modes, steps - SUB)
    for m in range(modes):
        own = horner(fade[m], mixed)
        put(g, m, own)
        put(x_out, m, row(x_part, m) + rest[m] * own)


def query_kernel(taps, steps, query, halo, filt, q_ext, f0):
    margin = taps - 1
    there = jnp.where(lax.axis_index("ctx") > 0, 1.0, 0.0)
    for s in range(SUB):
        lanes = slice(s * LANES, (s + 1) * LANES)
        q_ext[pl.ds(s, SUB, stride=SUB), :] = halo[0, :, lanes].astype(F32) * there
    spread(query, q_ext, SUB, steps)
    taps0 = taps_of(filt, 0, taps)

    def conv(c, carry):
        t0 = c * SUB
        qw = [row(q_ext, t0 + SUB - margin + i) for i in range(SUB + margin)]
        for i in range(SUB):
            put(f0, t0 + i, conv_at(qw, taps0, i))
        return carry

    loop(0, steps // SUB, conv, 0)


def inputs_kernel(steps, residual, cot, res_pos, cot_pos):
    spread(residual, res_pos, 0, steps)
    spread(cot, cot_pos, 0, steps)


def near_taps(lam, res, skip, modes):
    fade, weight = fades(lam, modes, 1), [row(res, m) for m in range(modes)]
    result = []
    for k in range(SUB):
        result.append(total(weight) if k else total(weight) + skip[...])
        weight = [f * w for f, w in zip(fade, weight)]
    return result


def near_kernel(modes, steps, u, lam, res, skip, y):
    near = near_taps(lam, res, skip, modes)

    def some(c, carry):
        now = [row(u, c * SUB + i) for i in range(SUB)]
        for i in range(SUB):
            put(y, c * SUB + i, total([near[k] * now[i - k] for k in range(i + 1)]))
        return carry

    loop(0, steps // SUB, some, 0)


def lags_kernel(modes, steps, u, x_at, lam, lag, lag_sum):
    fade, skip = fades(lam, modes, 1), fades(lam, modes, SUB)

    def some(c, sums):
        now = [row(u, c * SUB + i) * float(SUB - i) for i in range(SUB)]
        new = []
        for m in range(modes):
            border = horner(fade[m], now) + float(SUB) * skip[m] * row(x_at, c * modes + m)
            put(lag, c * modes + m, border)
            new.append(skip[m] * sums[m] + border)
        return tuple(new)

    sums = loop(0, steps // SUB, some, zeros(modes))
    for m in range(modes):
        put(lag_sum, m, sums[m])


def summed_kernel(modes, steps, blocks, group, y, f0, res_pos, cot_pos, g, before, other, lam, res, gain, modal, summed, x_at, sums, squares, inner):
    block = pl.program_id(0)

    @pl.when(block == 0)
    def _():
        squares[...] = jnp.zeros_like(squares)
        inner[...] = jnp.zeros_like(inner)

    fade, skip = fades(lam, modes, 1), fades(lam, modes, SUB)
    factor = gain[...]
    x_in = exclusive(before[...], other[...], lam[...], steps, group, 1)
    x_in = tuple(x_in[m * SUB : (m + 1) * SUB, :] for m in range(modes))

    def advance(c, x):
        w = [row(res, m) * x[m] for m in range(modes)]
        for m in range(modes):
            put(x_at, c * modes + m, x[m])
        for i in range(SUB):
            t = c * SUB + i
            w = [f * v for f, v in zip(fade, w)]
            long = row(y, t) + total(w)
            put(modal, t, long)
            now = row(res_pos, t) + row(f0, t) * long
            put(summed, t, now)
            put(squares, t, row(squares, t) + now * now)
            put(inner, t, row(inner, t) + factor * row(cot_pos, t) * now)
        return tuple(row(g, c * modes + m) + skip[m] * x[m] for m in range(modes))

    loop(0, steps // SUB, advance, x_in)

    @pl.when(block == blocks - 1)
    def _():
        for which, scratch in enumerate((squares, inner)):
            for b in range(steps // LANES):
                part = total(
                    [
                        scratch[pl.ds(b * LANES * SUB + s, LANES, stride=SUB), :]
                        for s in range(SUB)
                    ]
                )
                sums[which : which + 1, b * LANES : (b + 1) * LANES] = jnp.sum(
                    part.T, axis=0, keepdims=True
                )


def grad_modal_kernel(modes, steps, width, shares, *refs):
    own_sums, (summed, cot_pos, f0, lam, gain, ready) = refs[:shares], refs[shares : shares + 6]
    scale, gm, adj, a_out = refs[shares + 6 :]
    del ready

    @pl.when(pl.program_id(0) == 0)
    def _():
        sums = total([ref[...] for ref in own_sums])
        inv = lax.rsqrt(sums[0:1, :] / width + 1e-05)
        coef = inv * inv * inv * sums[1:2, :] / width
        for which, value in enumerate((inv, coef)):
            for b in range(steps // LANES):
                piece = value[:, b * LANES : (b + 1) * LANES]
                scale[pl.ds(which * steps + b * LANES, LANES), :] = jnp.broadcast_to(
                    piece, (LANES, LANES)
                ).T

    fade, skip = fades(lam, modes, 1), fades(lam, modes, SUB)
    factor = gain[...]

    def advance(c, a):
        block = steps // SUB - 1 - c
        now = [None] * SUB
        for i in reversed(range(SUB)):
            t = block * SUB + i
            inv = scale[pl.ds(t, 1), :]
            coef = scale[pl.ds(steps + t, 1), :]
            grad = inv * (factor * row(cot_pos, t)) - coef * row(summed, t)
            now[i] = grad * row(f0, t)
            put(gm, t, now[i])
        new = []
        for m in range(modes):
            own = fade[m] * horner(fade[m], now[::-1])
            put(adj, block * modes + m, own)
            new.append(own + skip[m] * a[m])
        return tuple(new)

    a = loop(0, steps // SUB, advance, zeros(modes))
    for m in range(modes):
        put(a_out, m, a[m])


def own_adjoint_kernel(modes, steps, gm, u, adj, x_at, lag, lam, res, skip, gmy, res_sum, rate_sum, skip_sum):
    near = near_taps(lam, res, skip, modes)
    fade, far = fades(lam, modes, 1), fades(lam, modes, SUB)
    last = steps // SUB - 1

    def pairs(c, lags):
        now = [row(gm, c * SUB + i) for i in range(SUB)]
        for i in range(SUB):
            put(gmy, c * SUB + i, total([near[k] * now[i + k] for k in range(SUB - i)]))
        before = [row(u, c * SUB + i) for i in range(SUB)]
        return tuple(
            lags[k] + total([now[i] * before[i - k] for i in range(k, SUB)]) for k in range(SUB)
        )

    lags = loop(0, steps // SUB, pairs, zeros(SUB))
    skip_sum[...] = lags[0]
    half = modes // 2
    for part in range(2):
        ms = range(part * half, (part + 1) * half)

        def across(c, state, ms=ms):
            after, by_res, by_rate = (list(v) for v in state)
            block = last - c
            now = [row(gm, block * SUB + i) * float(i) for i in range(1, SUB)]
            for i, m in enumerate(ms):
                x, own = row(x_at, block * modes + m), row(adj, block * modes + m)
                tail = fade[m] * fade[m] * horner(fade[m], now[::-1])
                by_res[i] = by_res[i] + x * own
                by_rate[i] = by_rate[i] + (x * tail + after[i] * row(lag, block * modes + m))
                after[i] = own + far[m] * after[i]
            return tuple(after), tuple(by_res), tuple(by_rate)

        none = zeros(half)
        _, by_res, by_rate = loop(0, steps // SUB, across, (none, none, none))
        for i, m in enumerate(ms):
            put(res_sum, m, by_res[i] + horner(fade[m], lags[::-1]))
            weighted = [lags[k] * float(k) for k in range(1, SUB)]
            put(rate_sum, m, by_rate[i] + fade[m] * horner(fade[m], weighted[::-1]))


def norm_kernel(steps, scale, summed, cot_pos, gain, normed, grad_res, gain_out, work):
    factor = gain[...]

    def norm(c, acc):
        for i in range(SUB):
            t = c * SUB + i
            here = row(summed, t) * scale[pl.ds(t, 1), :]
            put(work, t, here * factor)
            acc = acc + row(cot_pos, t) * here
        return acc

    gain_out[...] = loop(0, steps // SUB, norm, zeros(1)[0])
    gather_rows(work, normed, steps)

    def grads(c, carry):
        for i in range(SUB):
            t = c * SUB + i
            inv = scale[pl.ds(t, 1), :]
            coef = scale[pl.ds(steps + t, 1), :]
            put(work, t, inv * (factor * row(cot_pos, t)) - coef * row(summed, t))
        return carry

    loop(0, steps // SUB, grads, 0)
    gather_rows(work, grad_res, steps)


def query_sums_kernel(modes, taps, steps, scale, summed, cot_pos, modal, q_ext, gain, res_sum, skip_sum, gain_sum, gf0, early):
    factor = gain[...]

    def grads(c, carry):
        for i in range(SUB):
            t = c * SUB + i
            inv = scale[pl.ds(t, 1), :]
            coef = scale[pl.ds(steps + t, 1), :]
            grad = inv * (factor * row(cot_pos, t)) - coef * row(summed, t)
            put(gf0, t, grad * row(modal, t))
        return carry

    loop(0, steps // SUB, grads, 0)
    sums = filter_pass(taps, steps, gf0, q_ext)
    for j in range(taps):
        put(early, j, sums[j])
    early[pl.ds(taps * SUB, modes * SUB), :] = res_sum[...]
    put(early, taps + modes, skip_sum[...])
    put(early, taps + modes + 1, gain_sum[...])


def filter_pass(taps, steps, grad, ext):
    margin = taps - 1

    def some(c, acc):
        t0 = c * SUB
        window = [row(ext, t0 + SUB - margin + i) for i in range(SUB + margin)]
        for i in range(SUB):
            now = row(grad, t0 + i)
            acc = tuple(acc[j] + now * window[margin + i - j] for j in range(taps))
        return acc

    zero = jnp.zeros((SUB, LANES), F32)
    return loop(0, steps // SUB, some, tuple(zero for _ in range(taps)))


def back_pass(taps, steps, grad, weights, out):
    margin = taps - 1

    def some(c, carry):
        t0 = c * SUB
        window = [row(grad, t0 + i) for i in range(SUB + margin)]
        for i in range(SUB):
            put(out, t0 + i, total([weights[j] * window[i + j] for j in range(taps)]))
        return carry

    loop(0, steps // SUB, some, 0)


def mixed_kernel(modes, taps, steps, gmy, f1, f2, gf0, adj, lam, res, alpha, gf1, gf2, heads):
    fade, skip = fades(lam, modes, 1), fades(lam, modes, SUB)

    def advance(c, after):
        block = steps // SUB - 1 - c
        w = [row(res, m) * after[m] for m in range(modes)]
        for i in reversed(range(SUB)):
            t = block * SUB + i
            grad = row(gmy, t) + total(w)
            put(gf1, t, grad * row(f2, t))
            put(gf2, t, grad * row(f1, t))
            w = [f * v for f, v in zip(fade, w)]
        return tuple(row(adj, block * modes + m) + skip[m] * after[m] for m in range(modes))

    loop(0, steps // SUB, advance, tuple(row(alpha, m) for m in range(modes)))
    for which, grad in enumerate((gf0, gf1, gf2)):
        heads[which, 0] = grad[: SUB * SUB, :]


def filter_sums_kernel(taps, steps, gf1, gf2, k_ext, v_ext, sums):
    for which, (grad, ext) in enumerate(((gf1, k_ext), (gf2, v_ext))):
        parts = filter_pass(taps, steps, grad, ext)
        for j in range(taps):
            put(sums, which * taps + j, parts[j])


def back_kernel(which, taps, steps, last, grad, next_head, filt, out, work, ext):
    there = jnp.where(lax.axis_index("ctx") < last, 1.0, 0.0)
    ext[pl.ds(0, steps * SUB), :] = grad[...]
    ext[pl.ds(steps * SUB, SUB * SUB), :] = next_head[which, 0] * there
    back_pass(taps, steps, ext, taps_of(filt, which, taps), work)
    gather_rows(work, out, steps)


def place(group, sign):
    at = lax.axis_index("ctx")
    if sign < 0:
        at = lax.axis_size("ctx") - 1 - at
    later = (at // group) % 2
    return (at % group).astype(F32), later.astype(F32)


def exclusive(before, other, lam, span, group, sign):
    at, later = place(group, sign)
    here = later * jnp.exp(lam * (at * -float(span))) * other
    return here if before is None else before + here


def inclusive(own, other, lam, span, group, sign):
    _, later = place(group, sign)
    fall = -float(span * group)
    return jnp.exp(lam * ((1.0 - later) * fall)) * own + jnp.exp(lam * (later * fall)) * other


def join_kernel(span, group, sign, first, own, other, lam, *refs):
    before, ends = (None, refs[-2:]) if first else (refs[0][...], refs[-2:])
    ends[0][...] = exclusive(before, other[...], lam[...], span, group, sign)
    ends[1][...] = inclusive(own[...], other[...], lam[...], span, group, sign)


def add_kernel(one, other, after, out):
    del after
    out[...] = one[...] + other[...]


def gather_kernel(early_rows, kept, other, late, after, out):
    del after
    out[:early_rows, :] = kept[...] + other[...]
    out[early_rows:, :] = late[...]


def pack_kernel(span, group, modes, first_rows, half, before, other, lam, early, res, rate_sum, lag_sum, alpha, kept, sent):
    alpha[...] = exclusive(before[...], other[...], lam[...], span, group, -1)
    odd = lax.axis_index("ctx") % 2
    rows = (first_rows + modes) * SUB
    for out, start in ((kept, odd * half), (sent, (1 - odd) * half)):
        for b in range(half):
            source = pl.multiple_of((start + b) * (first_rows * SUB), SUB)
            out[pl.ds(b * rows, first_rows * SUB), :] = early[pl.ds(source, first_rows * SUB), :]
            source = pl.multiple_of((start + b) * (modes * SUB), SUB)
            mine = pl.ds(source, modes * SUB)
            lagged = rate_sum[mine, :] + alpha[mine, :] * lag_sum[mine, :]
            out[pl.ds(b * rows + first_rows * SUB, modes * SUB), :] = -res[mine, :] * lagged


def finish_kernel(modes, taps, half, early_rows, late_rows, mine, other, after, short, res, rate, skip, gain, late, early):
    del after
    block = pl.program_id(0)
    at = pl.multiple_of((half * early_rows + block * late_rows) * SUB, SUB)
    late[...] = mine[pl.ds(at, late_rows * SUB), :] + other[pl.ds(at, late_rows * SUB), :]
    own = jnp.where(lax.axis_index("ctx") % 2 == block // half, 1.0, 0.0)
    at = pl.multiple_of((block % half) * (early_rows * SUB), SUB)
    here = pl.ds(at, early_rows * SUB)
    early[...] = own * mine[here, :] + (1.0 - own) * other[here, :]
    for s in range(SUB):
        lanes = slice(s * LANES, (s + 1) * LANES)
        short[0, :, lanes] = early[pl.ds(s, taps, stride=SUB), :]
        short[1, :, lanes] = late[pl.ds(s, taps, stride=SUB), :]
        short[2, :, lanes] = late[pl.ds(taps * SUB + s, taps, stride=SUB), :]
        res[:, lanes] = early[pl.ds(taps * SUB + s, modes, stride=SUB), :]
        rate[:, lanes] = early[pl.ds((taps + modes + 2) * SUB + s, modes, stride=SUB), :]
    skip[...] = row(early, taps + modes)
    gain[...] = row(early, taps + modes + 1)


def ring(value, axis, distance):
    count = lax.axis_size(axis)
    return lax.ppermute(value, axis, [(i, (i + distance) % count) for i in range(count)])


def swap(value, axis, step):
    return lax.ppermute(value, axis, [(i, i ^ step) for i in range(lax.axis_size(axis))])


def small(body, ins, after, outs, name):
    near = pl.BlockSpec(memory_space=pltpu.VMEM)
    return pl.pallas_call(
        body,
        in_specs=[near] * len(ins) + [pl.BlockSpec(memory_space=pl.ANY)] * len(after),
        out_specs=[near] * len(outs),
        out_shape=[jax.ShapeDtypeStruct(shape, F32) for shape in outs],
        compiler_params=pltpu.CompilerParams(vmem_limit_bytes=VMEM_LIMIT),
        cost_estimate=pl.CostEstimate(flops=ins[0].size, bytes_accessed=0, transcendentals=0),
        name=name,
    )(*ins, *after)


def scan_but_last(own, lam, span, sign, under):
    count, group, before = lax.axis_size("ctx"), 1, None
    under = list(under)
    while True:
        other = swap(own, "ctx", group)
        if 2 * group >= count:
            return before, other, group
        body = functools.partial(join_kernel, span, group, sign, before is None)
        ins = [own, other, lam] + ([] if before is None else [before])
        after = [under.pop(0)] if under else []
        before, own = small(body, ins, after, [own.shape] * 2, "join")
        group *= 2


def shards(
    residual, query_in, key_in, value_in, short_filter, residues, decay_rate, skip_gain, norm_gain, cotangent
):
    steps, channels = residual.shape
    modes, taps = residues.shape[0], short_filter.shape[1]
    blocks = channels // WIDE
    width = channels * lax.axis_size("tp")
    skip, gain = (v.reshape(blocks * SUB, LANES) for v in (skip_gain, norm_gain))

    def pos(count):
        return jax.ShapeDtypeStruct((blocks * count * SUB, LANES), F32)

    def kept(count):
        return pltpu.VMEM((blocks * count * SUB, LANES), F32)

    def pos_spec(count):
        return pl.BlockSpec((count * SUB, LANES), lambda h: (h, 0))

    def head_spec(total_steps, start):
        return pl.BlockSpec((SUB * SUB, LANES), lambda h: (h * (total_steps // SUB) + start, 0))

    wide_spec = pl.BlockSpec((steps, WIDE), lambda h: (0, h))
    wide = jax.ShapeDtypeStruct((steps, channels), BF16)
    mode_spec, one_spec, filt_spec = pos_spec(modes), pos_spec(1), pos_spec(3 * taps)
    seq_spec, ext_spec = pos_spec(steps), pos_spec(steps + SUB)
    seq, ext, mode, one = kept(steps), kept(steps + SUB), pos(modes), pos(1)
    eights, eights_spec = kept(steps // SUB * modes), pos_spec(steps // SUB * modes)
    halo_spec = pl.BlockSpec((3, SUB, WIDE), lambda h: (0, 0, h))
    param_spec = pl.BlockSpec((modes, WIDE), lambda h: (0, h))
    short_spec = pl.BlockSpec((3, taps, WIDE), lambda h: (0, 0, h))

    def call(body, ins, in_specs, outs, out_specs, ops, name, scratch=(), aliases=None):
        elements, n_refs = steps * channels, len(ins) + len(outs)

        def with_done(*refs):
            done = refs[n_refs]
            done[...] = jnp.zeros_like(done)
            body(*refs[:n_refs], *refs[n_refs + 1 :])

        near = blocks * steps * SUB
        ins = [
            pltpu.with_memory_space_constraint(v, pltpu.VMEM) if v.shape[0] >= near and v.dtype == F32 else v
            for v in ins
        ]
        done_shape = (SUB, LANES)
        outs = [*outs, jax.ShapeDtypeStruct(done_shape, F32)]
        out_specs = [*out_specs, pl.BlockSpec(done_shape, lambda h: (0, 0))]
        return pl.pallas_call(
            with_done,
            grid=(blocks,),
            in_specs=in_specs,
            out_specs=out_specs,
            out_shape=outs,
            scratch_shapes=list(scratch),
            input_output_aliases=aliases or {},
            compiler_params=pltpu.CompilerParams(
                dimension_semantics=("arbitrary",), vmem_limit_bytes=VMEM_LIMIT
            ),
            cost_estimate=pl.CostEstimate(
                flops=ops * elements, bytes_accessed=4 * elements, transcendentals=0
            ),
            name=name,
        )(*ins)

    far = [
        pltpu.with_memory_space_constraint(v, pltpu.HBM)
        for v in (residual, query_in, key_in, value_in, cotangent, short_filter, decay_rate, residues)
    ]
    last_spec = pl.BlockSpec((2 * SUB, channels), lambda h: (steps // (2 * SUB) - 1, 0))
    trailing = pl.pallas_call(
        trailing_kernel,
        grid=(1,),
        in_specs=[last_spec] * 3,
        out_specs=pl.BlockSpec((3, SUB, channels), lambda h: (0, 0, 0)),
        out_shape=jax.ShapeDtypeStruct((3, SUB, channels), BF16),
        compiler_params=pltpu.CompilerParams(vmem_limit_bytes=VMEM_LIMIT),
        cost_estimate=pl.CostEstimate(flops=channels, bytes_accessed=channels, transcendentals=0),
        name="trailing",
    )(*far[1:4])
    halo = ring(trailing, "ctx", 1)

    k_ext, v_ext, f1, f2, u, g, lam, res, filt, x_part, _ = call(
        functools.partial(features_kernel, modes, taps, steps),
        (far[2], far[3], *far[5:]),
        [wide_spec, wide_spec, short_spec, param_spec, param_spec],
        [ext, ext, seq, seq, seq, eights, mode, mode, pos(3 * taps), mode],
        [ext_spec, ext_spec, seq_spec, seq_spec, seq_spec, eights_spec, mode_spec, mode_spec, filt_spec, mode_spec],
        64,
        "features",
    )
    any_spec = pl.BlockSpec(memory_space=pl.ANY)
    k_ext, v_ext, f1, f2, u, g, x_own, _ = call(
        functools.partial(head_kernel, modes, taps, steps),
        (halo, k_ext, v_ext, filt, lam, x_part, f1, f2, u, g),
        [halo_spec, head_spec(steps + SUB, 1), head_spec(steps + SUB, 1), filt_spec, mode_spec, mode_spec]
        + [any_spec] * 4,
        [ext, ext, seq, seq, seq, eights, mode],
        [head_spec(steps + SUB, 0)] * 2
        + [head_spec(steps, 0)] * 3
        + [pl.BlockSpec((modes * SUB, LANES), lambda h: (h * (steps // SUB), 0)), mode_spec],
        2,
        "head",
        aliases={1: 0, 2: 1, 6: 2, 7: 3, 8: 4, 9: 5},
    )
    q_ext, f0, query_done = call(
        functools.partial(query_kernel, taps, steps),
        (far[1], halo, filt),
        [wide_spec, halo_spec, filt_spec],
        [ext, seq],
        [ext_spec, seq_spec],
        20,
        "query",
    )
    res_pos, cot_pos, inputs_done = call(
        functools.partial(inputs_kernel, steps),
        (far[0], far[4]),
        [wide_spec] * 2,
        [seq, seq],
        [seq_spec] * 2,
        10,
        "inputs",
    )
    y, _ = call(
        functools.partial(near_kernel, modes, steps),
        (u, lam, res, skip),
        [seq_spec, mode_spec, mode_spec, one_spec],
        [seq],
        [seq_spec],
        10,
        "near",
    )
    before, other, group = scan_but_last(x_own, lam, steps, 1, [query_done, inputs_done])
    modal, summed, x_at, sums, _ = call(
        functools.partial(summed_kernel, modes, steps, blocks, group),
        (y, f0, res_pos, cot_pos, g, before, other, lam, res, gain),
        [seq_spec] * 4 + [eights_spec] + [mode_spec] * 4 + [one_spec],
        [seq, seq, eights, jax.ShapeDtypeStruct((2, steps), F32)],
        [seq_spec, seq_spec, eights_spec, pl.BlockSpec((2, steps), lambda h: (0, 0))],
        50,
        "summed",
        scratch=[pltpu.VMEM((steps * SUB, LANES), F32)] * 2,
    )
    all_sums = [sums, *(swap(sums, "tp", k) for k in range(1, lax.axis_size("tp")))]
    lag, lag_sum, lags_done = call(
        functools.partial(lags_kernel, modes, steps),
        (u, x_at, lam),
        [seq_spec, eights_spec, mode_spec],
        [eights, mode],
        [eights_spec, mode_spec],
        32,
        "lags",
    )
    scale_spec = pl.BlockSpec((2 * steps, LANES), lambda h: (0, 0))
    scale, gm, adj, a_own, _ = call(
        functools.partial(grad_modal_kernel, modes, steps, width, len(all_sums)),
        (*all_sums, summed, cot_pos, f0, lam, gain, lags_done),
        [pl.BlockSpec((2, steps), lambda h: (0, 0))] * len(all_sums)
        + [seq_spec, seq_spec, seq_spec, mode_spec, one_spec, any_spec],
        [pltpu.VMEM((2 * steps, LANES), F32), seq, eights, mode],
        [scale_spec, seq_spec, eights_spec, mode_spec],
        45,
        "grad_modal",
    )
    normed, grad_residual, gain_sum, norm_done = call(
        functools.partial(norm_kernel, steps),
        (scale, summed, cot_pos, gain),
        [scale_spec, seq_spec, seq_spec, one_spec],
        [wide, wide, one],
        [wide_spec, wide_spec, one_spec],
        25,
        "norm",
        scratch=[pltpu.VMEM((steps * SUB, LANES), F32)],
    )
    gmy, res_sum, rate_sum, skip_sum, adjoint_done = call(
        functools.partial(own_adjoint_kernel, modes, steps),
        (gm, u, adj, x_at, lag, lam, res, skip),
        [seq_spec, seq_spec, eights_spec, eights_spec, eights_spec, mode_spec, mode_spec, one_spec],
        [seq, mode, mode, one],
        [seq_spec, mode_spec, mode_spec, one_spec],
        75,
        "own_adjoint",
    )
    early_rows = taps + modes + 2
    gf0, early, _ = call(
        functools.partial(query_sums_kernel, modes, taps, steps),
        (scale, summed, cot_pos, modal, q_ext, gain, res_sum, skip_sum, gain_sum),
        [scale_spec, seq_spec, seq_spec, seq_spec, ext_spec, one_spec, mode_spec, one_spec, one_spec],
        [seq, pos(early_rows)],
        [seq_spec, pos_spec(early_rows)],
        30,
        "query_sums",
    )
    before, other, group = scan_but_last(a_own, lam, steps, -1, [norm_done, adjoint_done])

    half = blocks // 2
    half_shape = (half * (early_rows + modes) * SUB, LANES)
    alpha, kept_half, sent_half = small(
        functools.partial(pack_kernel, steps, group, modes, early_rows, half),
        [before, other, lam, early, res, rate_sum, lag_sum],
        [],
        [lam.shape, half_shape, half_shape],
        "pack",
    )
    early_rows += modes
    late_rows = 2 * taps
    next_spec = pl.BlockSpec((3, 1, SUB * SUB, LANES), lambda h: (0, h, 0, 0))
    other_half = swap(sent_half, "ctx", 1)
    gf1, gf2, heads, _ = call(
        functools.partial(mixed_kernel, modes, taps, steps),
        (gmy, f1, f2, gf0, adj, lam, res, alpha),
        [seq_spec] * 4 + [eights_spec] + [mode_spec] * 3,
        [seq, seq, jax.ShapeDtypeStruct((3, blocks, SUB * SUB, LANES), F32)],
        [seq_spec, seq_spec, next_spec],
        45,
        "mixed",
    )
    next_head = ring(heads, "ctx", -1)
    late, late_done = call(
        functools.partial(filter_sums_kernel, taps, steps),
        (gf1, gf2, k_ext, v_ext),
        [seq_spec, seq_spec, ext_spec, ext_spec],
        [pos(late_rows)],
        [pos_spec(late_rows)],
        30,
        "filter_sums",
    )

    def back(which, grad, name):
        return call(
            functools.partial(back_kernel, which, taps, steps, lax.axis_size("ctx") - 1),
            (grad, next_head, filt),
            [seq_spec, next_spec, filt_spec],
            [wide],
            [wide_spec],
            20,
            name,
            scratch=[
                pltpu.VMEM((steps * SUB, LANES), F32),
                pltpu.VMEM(((steps + SUB) * SUB, LANES), F32),
            ],
        )

    grad_query, query_done = back(0, gf0, "back_query")
    grad_key, key_done = back(1, gf1, "back_key")
    grad_value, value_done = back(2, gf2, "back_value")
    both_shape = (half_shape[0] + late.shape[0], LANES)
    mine = small(
        functools.partial(gather_kernel, half_shape[0]),
        [kept_half, other_half, late],
        [late_done],
        [both_shape],
        "gather",
    )[0]
    step, under = 2, [query_done, key_done]
    while step < lax.axis_size("ctx"):
        after = under.pop(0) if under else late_done
        mine = small(add_kernel, [mine, swap(mine, "ctx", step)], [after], [both_shape], "add")[0]
        step *= 2
    other = swap(mine, "ctx", 1)
    whole_spec = pl.BlockSpec(memory_space=pltpu.VMEM)
    grad_short, grad_residues, grad_rate, grad_skip, grad_gain, _ = call(
        functools.partial(finish_kernel, modes, taps, half, early_rows, late_rows),
        (mine, other, value_done),
        [whole_spec, whole_spec, any_spec],
        [
            jax.ShapeDtypeStruct(short_filter.shape, F32),
            jax.ShapeDtypeStruct(residues.shape, F32),
            jax.ShapeDtypeStruct(residues.shape, F32),
            one,
            one,
        ],
        [short_spec, param_spec, param_spec, one_spec, one_spec],
        1,
        "finish",
        scratch=[
            pltpu.VMEM((late_rows * SUB, LANES), F32),
            pltpu.VMEM((early_rows * SUB, LANES), F32),
        ],
    )
    return (
        normed,
        grad_residual,
        grad_query,
        grad_key,
        grad_value,
        grad_short,
        grad_residues,
        grad_rate,
        grad_skip.reshape(channels),
        grad_gain.reshape(channels),
    )


def solution(mesh):
    both, modes, vector = P("ctx", "tp"), P(None, "tp"), P("tp")
    return jax.shard_map(
        shards,
        mesh=mesh,
        in_specs=(both, both, both, both, P(None, None, "tp"), modes, modes, vector, vector, both),
        out_specs=(both,) * 5 + (P(None, None, "tp"), modes, modes, vector, vector),
        check_vma=False,
    )
```

```python
import functools

import jax
import jax.numpy as jnp
from jax import lax
from jax.experimental import pallas as pl
from jax.experimental.pallas import tpu as pltpu
from jax.sharding import PartitionSpec as P

LANES = 128
SUB = 8
WIDE = SUB * LANES
F32 = jnp.float32
BF16 = jnp.bfloat16
VMEM_LIMIT = 10 * 1024 * 1024


def row(ref, t):
    return ref[pl.ds(pl.multiple_of(t * SUB, SUB), SUB), :]


def put(ref, t, value):
    ref[pl.ds(pl.multiple_of(t * SUB, SUB), SUB), :] = value


def loop(start, stop, body, carry):
    pairs = (stop - start) // 2

    def two(i, carry):
        return body(start + 2 * i + 1, body(start + 2 * i, carry))

    carry = lax.fori_loop(0, pairs, two, carry)
    return body(stop - 1, carry) if (stop - start) % 2 else carry


def spread(src, dst, first, count):
    def some(i, carry):
        start = pl.multiple_of(i * 16, 16)
        for g in range(SUB):
            piece = src[pl.ds(start, 16), g * LANES : (g + 1) * LANES].astype(F32)
            dst[pl.ds((start + first) * SUB + g, 16, stride=SUB), :] = piece
        return carry

    loop(0, count // 16, some, 0)


def gather_rows(src, dst, count):
    def some(i, carry):
        start = pl.multiple_of(i * 16, 16)
        for g in range(SUB):
            piece = src[pl.ds(start * SUB + g, 16, stride=SUB), :]
            dst[pl.ds(start, 16), g * LANES : (g + 1) * LANES] = piece.astype(dst.dtype)
        return carry

    loop(0, count // 16, some, 0)


def total(values):
    values = list(values)
    while len(values) > 1:
        values = [
            values[i] + values[i + 1] if i + 1 < len(values) else values[i]
            for i in range(0, len(values), 2)
        ]
    return values[0]


def taps_of(filt, stream, taps):
    return [row(filt, stream * taps + j) for j in range(taps)]


def conv_at(window, taps, i):
    margin = len(taps) - 1
    return total([taps[j] * window[margin + i - j] for j in range(margin + 1)])


def trailing_kernel(query, key, value, out):
    for i, ref in enumerate((query, key, value)):
        out[i] = ref[...].astype(F32)[SUB:, :].astype(BF16)


def features_kernel(
    modes, taps, steps, key, value, filt3, decay, resid, k_ext, v_ext, f1, f2, u, g, lam, res, filt, x_out
):
    margin = taps - 1
    for s in range(SUB):
        lanes = slice(s * LANES, (s + 1) * LANES)
        lam[pl.ds(s, modes, stride=SUB), :] = decay[:, lanes]
        res[pl.ds(s, modes, stride=SUB), :] = resid[:, lanes]
        for i in range(3):
            filt[pl.ds(i * taps * SUB + s, taps, stride=SUB), :] = filt3[i, :, lanes]
    spread(key, k_ext, SUB, steps)
    spread(value, v_ext, SUB, steps)
    taps1, taps2 = taps_of(filt, 1, taps), taps_of(filt, 2, taps)

    def conv(c, carry):
        t0 = c * SUB
        kw = [row(k_ext, t0 + SUB - margin + i) for i in range(SUB + margin)]
        for i in range(SUB):
            put(f1, t0 + i, conv_at(kw, taps1, i))
        vw = [row(v_ext, t0 + SUB - margin + i) for i in range(SUB + margin)]
        for i in range(SUB):
            second = conv_at(vw, taps2, i)
            put(f2, t0 + i, second)
            put(u, t0 + i, second * row(f1, t0 + i))
        return carry

    loop(1, steps // SUB, conv, 0)
    fade, skip = fades(lam, modes, 1), fades(lam, modes, SUB)

    def advance(c, x):
        now = [row(u, c * SUB + i) for i in range(SUB)]
        new = []
        for m in range(modes):
            own = horner(fade[m], now)
            put(g, c * modes + m, own)
            new.append(own + skip[m] * x[m])
        return tuple(new)

    x = loop(1, steps // SUB, advance, zeros(modes))
    for m in range(modes):
        put(x_out, m, x[m])


def zeros(count):
    return tuple(jnp.zeros((SUB, LANES), F32) for _ in range(count))


def fades(lam, modes, span):
    return [jnp.exp(row(lam, m) * -float(span)) for m in range(modes)]


def horner(fade, values):
    result = values[0]
    for value in values[1:]:
        result = fade * result + value
    return result


def head_kernel(
    modes, taps, steps, halo, k_head, v_head, filt, lam, x_part, f1_in, f2_in, u_in, g_in,
    k_ext, v_ext, f1, f2, u, g, x_out,
):
    del f1_in, f2_in, u_in, g_in
    margin = taps - 1
    there = jnp.where(lax.axis_index("ctx") > 0, 1.0, 0.0)
    for s in range(SUB):
        lanes = slice(s * LANES, (s + 1) * LANES)
        k_ext[pl.ds(s, SUB, stride=SUB), :] = halo[1, :, lanes].astype(F32) * there
        v_ext[pl.ds(s, SUB, stride=SUB), :] = halo[2, :, lanes].astype(F32) * there
    taps1, taps2 = taps_of(filt, 1, taps), taps_of(filt, 2, taps)
    kw = [row(k_ext, SUB - margin + i) for i in range(margin)] + [row(k_head, i) for i in range(SUB)]
    vw = [row(v_ext, SUB - margin + i) for i in range(margin)] + [row(v_head, i) for i in range(SUB)]
    mixed = []
    for i in range(SUB):
        first, second = conv_at(kw, taps1, i), conv_at(vw, taps2, i)
        put(f1, i, first)
        put(f2, i, second)
        put(u, i, first * second)
        mixed.append(first * second)
    fade, rest = fades(lam, modes, 1), fades(lam, modes, steps - SUB)
    for m in range(modes):
        own = horner(fade[m], mixed)
        put(g, m, own)
        put(x_out, m, row(x_part, m) + rest[m] * own)


def query_kernel(taps, steps, query, halo, filt, q_ext, f0):
    margin = taps - 1
    there = jnp.where(lax.axis_index("ctx") > 0, 1.0, 0.0)
    for s in range(SUB):
        lanes = slice(s * LANES, (s + 1) * LANES)
        q_ext[pl.ds(s, SUB, stride=SUB), :] = halo[0, :, lanes].astype(F32) * there
    spread(query, q_ext, SUB, steps)
    taps0 = taps_of(filt, 0, taps)

    def conv(c, carry):
        t0 = c * SUB
        qw = [row(q_ext, t0 + SUB - margin + i) for i in range(SUB + margin)]
        for i in range(SUB):
            put(f0, t0 + i, conv_at(qw, taps0, i))
        return carry

    loop(0, steps // SUB, conv, 0)


def inputs_kernel(steps, residual, cot, res_pos, cot_pos):
    spread(residual, res_pos, 0, steps)
    spread(cot, cot_pos, 0, steps)


def near_taps(lam, res, skip, modes):
    fade, weight = fades(lam, modes, 1), [row(res, m) for m in range(modes)]
    result = []
    for k in range(SUB):
        result.append(total(weight) if k else total(weight) + skip[...])
        weight = [f * w for f, w in zip(fade, weight)]
    return result


def near_kernel(modes, steps, u, lam, res, skip, y):
    near = near_taps(lam, res, skip, modes)

    def some(c, carry):
        now = [row(u, c * SUB + i) for i in range(SUB)]
        for i in range(SUB):
            put(y, c * SUB + i, total([near[k] * now[i - k] for k in range(i + 1)]))
        return carry

    loop(0, steps // SUB, some, 0)


def lags_kernel(modes, steps, u, lam, lag):
    fade = fades(lam, modes, 1)

    def some(c, carry):
        now = [row(u, c * SUB + i) * float(SUB - i) for i in range(SUB)]
        for m in range(modes):
            put(lag, c * modes + m, horner(fade[m], now))
        return carry

    loop(0, steps // SUB, some, 0)


def borders_kernel(modes, steps, own_lag, x_at, lam, lag, lag_sum):
    skip = fades(lam, modes, SUB)
    eight = [float(SUB) * v for v in skip]

    def some(c, sums):
        new = []
        for m in range(modes):
            border = row(own_lag, c * modes + m) + eight[m] * row(x_at, c * modes + m)
            put(lag, c * modes + m, border)
            new.append(skip[m] * sums[m] + border)
        return tuple(new)

    sums = loop(0, steps // SUB, some, zeros(modes))
    for m in range(modes):
        put(lag_sum, m, sums[m])


def summed_kernel(modes, steps, blocks, group, y, f0, res_pos, cot_pos, g, before, other, lam, res, gain, ready, modal, summed, x_at, sums, squares, inner):
    del ready
    block = pl.program_id(0)

    @pl.when(block == 0)
    def _():
        squares[...] = jnp.zeros_like(squares)
        inner[...] = jnp.zeros_like(inner)

    fade, skip = fades(lam, modes, 1), fades(lam, modes, SUB)
    factor = gain[...]
    x_in = exclusive(before[...], other[...], lam[...], steps, group, 1)
    x_in = tuple(x_in[m * SUB : (m + 1) * SUB, :] for m in range(modes))

    def advance(c, x):
        w = [row(res, m) * x[m] for m in range(modes)]
        for m in range(modes):
            put(x_at, c * modes + m, x[m])
        for i in range(SUB):
            t = c * SUB + i
            w = [f * v for f, v in zip(fade, w)]
            long = row(y, t) + total(w)
            put(modal, t, long)
            now = row(res_pos, t) + row(f0, t) * long
            put(summed, t, now)
            put(squares, t, row(squares, t) + now * now)
            put(inner, t, row(inner, t) + factor * row(cot_pos, t) * now)
        return tuple(row(g, c * modes + m) + skip[m] * x[m] for m in range(modes))

    loop(0, steps // SUB, advance, x_in)

    @pl.when(block == blocks - 1)
    def _():
        for which, scratch in enumerate((squares, inner)):
            for b in range(steps // LANES):
                part = total(
                    [
                        scratch[pl.ds(b * LANES * SUB + s, LANES, stride=SUB), :]
                        for s in range(SUB)
                    ]
                )
                sums[which : which + 1, b * LANES : (b + 1) * LANES] = jnp.sum(
                    part.T, axis=0, keepdims=True
                )


def grad_modal_kernel(modes, steps, width, shares, *refs):
    own_sums, (summed, cot_pos, f0, lam, gain, ready) = refs[:shares], refs[shares : shares + 6]
    scale, gm, adj, a_out = refs[shares + 6 :]
    del ready

    @pl.when(pl.program_id(0) == 0)
    def _():
        sums = total([ref[...] for ref in own_sums])
        inv = lax.rsqrt(sums[0:1, :] / width + 1e-05)
        coef = inv * inv * inv * sums[1:2, :] / width
        for which, value in enumerate((inv, coef)):
            for b in range(steps // LANES):
                piece = value[:, b * LANES : (b + 1) * LANES]
                scale[pl.ds(which * steps + b * LANES, LANES), :] = jnp.broadcast_to(
                    piece, (LANES, LANES)
                ).T

    fade, skip = fades(lam, modes, 1), fades(lam, modes, SUB)
    factor = gain[...]

    def advance(c, a):
        block = steps // SUB - 1 - c
        now = [None] * SUB
        for i in reversed(range(SUB)):
            t = block * SUB + i
            inv = scale[pl.ds(t, 1), :]
            coef = scale[pl.ds(steps + t, 1), :]
            grad = inv * (factor * row(cot_pos, t)) - coef * row(summed, t)
            now[i] = grad * row(f0, t)
            put(gm, t, now[i])
        new = []
        for m in range(modes):
            own = fade[m] * horner(fade[m], now[::-1])
            put(adj, block * modes + m, own)
            new.append(own + skip[m] * a[m])
        return tuple(new)

    a = loop(0, steps // SUB, advance, zeros(modes))
    for m in range(modes):
        put(a_out, m, a[m])


def across_kernel(modes, steps, gm, adj, x_at, lag, lam, res_part, rate_part):
    fade, far = fades(lam, modes, 1), fades(lam, modes, SUB)
    last = steps // SUB - 1
    half = modes // 2
    for part in range(2):
        ms = range(part * half, (part + 1) * half)

        def across(c, state, ms=ms):
            after, by_res, by_rate = (list(v) for v in state)
            block = last - c
            now = [row(gm, block * SUB + i) * float(i) for i in range(1, SUB)]
            for i, m in enumerate(ms):
                x, own = row(x_at, block * modes + m), row(adj, block * modes + m)
                tail = fade[m] * fade[m] * horner(fade[m], now[::-1])
                by_res[i] = by_res[i] + x * own
                by_rate[i] = by_rate[i] + (x * tail + after[i] * row(lag, block * modes + m))
                after[i] = own + far[m] * after[i]
            return tuple(after), tuple(by_res), tuple(by_rate)

        none = zeros(half)
        _, by_res, by_rate = loop(0, steps // SUB, across, (none, none, none))
        for i, m in enumerate(ms):
            put(res_part, m, by_res[i])
            put(rate_part, m, by_rate[i])


def near_adjoint_kernel(modes, steps, gm, u, lam, res, skip, res_part, rate_part, gmy, res_sum, rate_sum, skip_sum):
    near = near_taps(lam, res, skip, modes)

    def pairs(c, lags):
        now = [row(gm, c * SUB + i) for i in range(SUB)]
        for i in range(SUB):
            put(gmy, c * SUB + i, total([near[k] * now[i + k] for k in range(SUB - i)]))
        before = [row(u, c * SUB + i) for i in range(SUB)]
        return tuple(
            lags[k] + total([now[i] * before[i - k] for i in range(k, SUB)]) for k in range(SUB)
        )

    lags = loop(0, steps // SUB, pairs, zeros(SUB))
    skip_sum[...] = lags[0]
    fade = fades(lam, modes, 1)
    weighted = [lags[k] * float(k) for k in range(1, SUB)]
    for m in range(modes):
        put(res_sum, m, row(res_part, m) + horner(fade[m], lags[::-1]))
        put(rate_sum, m, row(rate_part, m) + fade[m] * horner(fade[m], weighted[::-1]))


def norm_kernel(steps, scale, summed, cot_pos, gain, ready, normed, grad_res, work):
    del ready
    factor = gain[...]

    def norm(c, carry):
        for i in range(SUB):
            t = c * SUB + i
            put(work, t, row(summed, t) * scale[pl.ds(t, 1), :] * factor)
        return carry

    loop(0, steps // SUB, norm, 0)
    gather_rows(work, normed, steps)

    def grads(c, carry):
        for i in range(SUB):
            t = c * SUB + i
            inv = scale[pl.ds(t, 1), :]
            coef = scale[pl.ds(steps + t, 1), :]
            put(work, t, inv * (factor * row(cot_pos, t)) - coef * row(summed, t))
        return carry

    loop(0, steps // SUB, grads, 0)
    gather_rows(work, grad_res, steps)


def query_sums_kernel(modes, taps, steps, scale, summed, cot_pos, modal, q_ext, gain, res_sum, skip_sum, gf0, early):
    factor = gain[...]

    def grads(c, by_gain):
        for i in range(SUB):
            t = c * SUB + i
            now, here = row(cot_pos, t), row(summed, t)
            scaled = scale[pl.ds(t, 1), :] * now
            grad = factor * scaled - scale[pl.ds(steps + t, 1), :] * here
            put(gf0, t, grad * row(modal, t))
            by_gain = by_gain + scaled * here
        return by_gain

    put(early, taps + modes + 1, loop(0, steps // SUB, grads, zeros(1)[0]))
    sums = filter_pass(taps, steps, gf0, q_ext)
    for j in range(taps):
        put(early, j, sums[j])
    early[pl.ds(taps * SUB, modes * SUB), :] = res_sum[...]
    put(early, taps + modes, skip_sum[...])


def filter_pass(taps, steps, grad, ext):
    margin = taps - 1

    def some(c, acc):
        t0 = c * SUB
        window = [row(ext, t0 + SUB - margin + i) for i in range(SUB + margin)]
        for i in range(SUB):
            now = row(grad, t0 + i)
            acc = tuple(acc[j] + now * window[margin + i - j] for j in range(taps))
        return acc

    zero = jnp.zeros((SUB, LANES), F32)
    return loop(0, steps // SUB, some, tuple(zero for _ in range(taps)))


def mixed_kernel(modes, taps, steps, gmy, f1, f2, gf0, adj, lam, res, alpha, gf1, gf2, heads):
    fade, skip = fades(lam, modes, 1), fades(lam, modes, SUB)

    def advance(c, after):
        block = steps // SUB - 1 - c
        w = [row(res, m) * after[m] for m in range(modes)]
        for i in reversed(range(SUB)):
            t = block * SUB + i
            grad = row(gmy, t) + total(w)
            put(gf1, t, grad * row(f2, t))
            put(gf2, t, grad * row(f1, t))
            w = [f * v for f, v in zip(fade, w)]
        return tuple(row(adj, block * modes + m) + skip[m] * after[m] for m in range(modes))

    loop(0, steps // SUB, advance, tuple(row(alpha, m) for m in range(modes)))
    for which, grad in enumerate((gf0, gf1, gf2)):
        heads[which, 0] = grad[: SUB * SUB, :].astype(BF16)


def filter_sums_kernel(taps, steps, gf1, gf2, k_ext, v_ext, sums):
    for which, (grad, ext) in enumerate(((gf1, k_ext), (gf2, v_ext))):
        parts = filter_pass(taps, steps, grad, ext)
        for j in range(taps):
            put(sums, which * taps + j, parts[j])


def back_kernel(which, taps, steps, last, grad, next_head, filt, out, work, head):
    there = jnp.where(lax.axis_index("ctx") < last, 1.0, 0.0)
    head[...] = next_head[which, 0].astype(F32) * there
    weights = taps_of(filt, which, taps)

    def some(c, carry):
        put_back(work, c * SUB, weights, [row(grad, c * SUB + i) for i in range(SUB + taps - 1)])
        return carry

    loop(0, steps // SUB - 1, some, 0)
    start = steps - SUB
    window = [row(grad, start + i) for i in range(SUB)] + [row(head, i) for i in range(taps - 1)]
    put_back(work, start, weights, window)
    gather_rows(work, out, steps)


def put_back(out, start, weights, window):
    for i in range(SUB):
        put(out, start + i, total([w * window[i + j] for j, w in enumerate(weights)]))


def place(group, sign):
    at = lax.axis_index("ctx")
    if sign < 0:
        at = lax.axis_size("ctx") - 1 - at
    later = (at // group) % 2
    return (at % group).astype(F32), later.astype(F32)


def exclusive(before, other, lam, span, group, sign):
    at, later = place(group, sign)
    here = later * jnp.exp(lam * (at * -float(span))) * other
    return here if before is None else before + here


def inclusive(own, other, lam, span, group, sign):
    _, later = place(group, sign)
    fall = -float(span * group)
    return jnp.exp(lam * ((1.0 - later) * fall)) * own + jnp.exp(lam * (later * fall)) * other


def join_kernel(span, group, sign, first, own, other, lam, *refs):
    before, ends = (None, refs[-2:]) if first else (refs[0][...], refs[-2:])
    ends[0][...] = exclusive(before, other[...], lam[...], span, group, sign)
    ends[1][...] = inclusive(own[...], other[...], lam[...], span, group, sign)


def add_kernel(one, other, *refs):
    refs[-1][...] = one[...] + other[...]


def pack_kernel(span, group, modes, first_rows, half, before, other, lam, early, res, rate_sum, lag_sum, alpha, kept, sent):
    alpha[...] = exclusive(before[...], other[...], lam[...], span, group, -1)
    odd = lax.axis_index("ctx") % 2
    rows = (first_rows + modes) * SUB
    for out, start in ((kept, odd * half), (sent, (1 - odd) * half)):
        for b in range(half):
            source = pl.multiple_of((start + b) * (first_rows * SUB), SUB)
            out[pl.ds(b * rows, first_rows * SUB), :] = early[pl.ds(source, first_rows * SUB), :]
            source = pl.multiple_of((start + b) * (modes * SUB), SUB)
            mine = pl.ds(source, modes * SUB)
            lagged = rate_sum[mine, :] + alpha[mine, :] * lag_sum[mine, :]
            out[pl.ds(b * rows + first_rows * SUB, modes * SUB), :] = -res[mine, :] * lagged


def finish_kernel(modes, taps, half, early_rows, mine, other, late_mine, late_other, after, short, res, rate, skip, gain, late, early):
    del after
    block = pl.program_id(0)
    late[...] = late_mine[...] + late_other[...]
    own = jnp.where(lax.axis_index("ctx") % 2 == block // half, 1.0, 0.0)
    early[...] = own * mine[...] + (1.0 - own) * other[...]
    for s in range(SUB):
        lanes = slice(s * LANES, (s + 1) * LANES)
        short[0, :, lanes] = early[pl.ds(s, taps, stride=SUB), :]
        short[1, :, lanes] = late[pl.ds(s, taps, stride=SUB), :]
        short[2, :, lanes] = late[pl.ds(taps * SUB + s, taps, stride=SUB), :]
        res[:, lanes] = early[pl.ds(taps * SUB + s, modes, stride=SUB), :]
        rate[:, lanes] = early[pl.ds((taps + modes + 2) * SUB + s, modes, stride=SUB), :]
    skip[...] = row(early, taps + modes)
    gain[...] = row(early, taps + modes + 1)


def ring(value, axis, distance):
    count = lax.axis_size(axis)
    return lax.ppermute(value, axis, [(i, (i + distance) % count) for i in range(count)])


def swap(value, axis, step):
    return lax.ppermute(value, axis, [(i, i ^ step) for i in range(lax.axis_size(axis))])


def small(body, ins, after, outs, name):
    near = pl.BlockSpec(memory_space=pltpu.VMEM)
    return pl.pallas_call(
        body,
        in_specs=[near] * len(ins) + [pl.BlockSpec(memory_space=pl.ANY)] * len(after),
        out_specs=[near] * len(outs),
        out_shape=[jax.ShapeDtypeStruct(shape, F32) for shape in outs],
        compiler_params=pltpu.CompilerParams(vmem_limit_bytes=VMEM_LIMIT),
        cost_estimate=pl.CostEstimate(flops=ins[0].size, bytes_accessed=0, transcendentals=0),
        name=name,
    )(*ins, *after)


def scan_but_last(own, lam, span, sign, under):
    count, group, before = lax.axis_size("ctx"), 1, None
    under = list(under)
    while True:
        other = swap(own, "ctx", group)
        if 2 * group >= count:
            return before, other, group
        body = functools.partial(join_kernel, span, group, sign, before is None)
        ins = [own, other, lam] + ([] if before is None else [before])
        after = [under.pop(0)] if under else []
        before, own = small(body, ins, after, [own.shape] * 2, "join")
        group *= 2


def shards(
    residual, query_in, key_in, value_in, short_filter, residues, decay_rate, skip_gain, norm_gain, cotangent
):
    steps, channels = residual.shape
    modes, taps = residues.shape[0], short_filter.shape[1]
    blocks = channels // WIDE
    width = channels * lax.axis_size("tp")
    skip, gain = (v.reshape(blocks * SUB, LANES) for v in (skip_gain, norm_gain))

    def pos(count):
        return jax.ShapeDtypeStruct((blocks * count * SUB, LANES), F32)

    def kept(count):
        return pltpu.VMEM((blocks * count * SUB, LANES), F32)

    def pos_spec(count):
        return pl.BlockSpec((count * SUB, LANES), lambda h: (h, 0))

    def head_spec(total_steps, start):
        return pl.BlockSpec((SUB * SUB, LANES), lambda h: (h * (total_steps // SUB) + start, 0))

    wide_spec = pl.BlockSpec((steps, WIDE), lambda h: (0, h))
    wide = jax.ShapeDtypeStruct((steps, channels), BF16)
    mode_spec, one_spec, filt_spec = pos_spec(modes), pos_spec(1), pos_spec(3 * taps)
    seq_spec, ext_spec = pos_spec(steps), pos_spec(steps + SUB)
    seq, ext, mode, one = kept(steps), kept(steps + SUB), pos(modes), pos(1)
    eights, eights_spec = kept(steps // SUB * modes), pos_spec(steps // SUB * modes)
    halo_spec = pl.BlockSpec((3, SUB, WIDE), lambda h: (0, 0, h))
    param_spec = pl.BlockSpec((modes, WIDE), lambda h: (0, h))
    short_spec = pl.BlockSpec((3, taps, WIDE), lambda h: (0, 0, h))

    def call(body, ins, in_specs, outs, out_specs, ops, name, scratch=(), aliases=None):
        elements, n_refs = steps * channels, len(ins) + len(outs)

        def with_done(*refs):
            done = refs[n_refs]
            done[...] = jnp.zeros_like(done)
            body(*refs[:n_refs], *refs[n_refs + 1 :])

        near = blocks * steps * SUB
        ins = [
            pltpu.with_memory_space_constraint(v, pltpu.VMEM) if v.shape[0] >= near and v.dtype == F32 else v
            for v in ins
        ]
        done_shape = (SUB, LANES)
        outs = [*outs, jax.ShapeDtypeStruct(done_shape, F32)]
        out_specs = [*out_specs, pl.BlockSpec(done_shape, lambda h: (0, 0))]
        return pl.pallas_call(
            with_done,
            grid=(blocks,),
            in_specs=in_specs,
            out_specs=out_specs,
            out_shape=outs,
            scratch_shapes=list(scratch),
            input_output_aliases=aliases or {},
            compiler_params=pltpu.CompilerParams(
                dimension_semantics=("arbitrary",), vmem_limit_bytes=VMEM_LIMIT
            ),
            cost_estimate=pl.CostEstimate(
                flops=ops * elements, bytes_accessed=4 * elements, transcendentals=0
            ),
            name=name,
        )(*ins)

    far = [
        pltpu.with_memory_space_constraint(v, pltpu.HBM)
        for v in (residual, query_in, key_in, value_in, cotangent, short_filter, decay_rate, residues)
    ]
    last_spec = pl.BlockSpec((2 * SUB, channels), lambda h: (steps // (2 * SUB) - 1, 0))
    trailing = pl.pallas_call(
        trailing_kernel,
        grid=(1,),
        in_specs=[last_spec] * 3,
        out_specs=pl.BlockSpec((3, SUB, channels), lambda h: (0, 0, 0)),
        out_shape=jax.ShapeDtypeStruct((3, SUB, channels), BF16),
        compiler_params=pltpu.CompilerParams(vmem_limit_bytes=VMEM_LIMIT),
        cost_estimate=pl.CostEstimate(flops=channels, bytes_accessed=channels, transcendentals=0),
        name="trailing",
    )(*far[1:4])
    halo = ring(trailing, "ctx", 1)

    k_ext, v_ext, f1, f2, u, g, lam, res, filt, x_part, _ = call(
        functools.partial(features_kernel, modes, taps, steps),
        (far[2], far[3], *far[5:]),
        [wide_spec, wide_spec, short_spec, param_spec, param_spec],
        [ext, ext, seq, seq, seq, eights, mode, mode, pos(3 * taps), mode],
        [ext_spec, ext_spec, seq_spec, seq_spec, seq_spec, eights_spec, mode_spec, mode_spec, filt_spec, mode_spec],
        64,
        "features",
    )
    any_spec = pl.BlockSpec(memory_space=pl.ANY)
    k_ext, v_ext, f1, f2, u, g, x_own, _ = call(
        functools.partial(head_kernel, modes, taps, steps),
        (halo, k_ext, v_ext, filt, lam, x_part, f1, f2, u, g),
        [halo_spec, head_spec(steps + SUB, 1), head_spec(steps + SUB, 1), filt_spec, mode_spec, mode_spec]
        + [any_spec] * 4,
        [ext, ext, seq, seq, seq, eights, mode],
        [head_spec(steps + SUB, 0)] * 2
        + [head_spec(steps, 0)] * 3
        + [pl.BlockSpec((modes * SUB, LANES), lambda h: (h * (steps // SUB), 0)), mode_spec],
        2,
        "head",
        aliases={1: 0, 2: 1, 6: 2, 7: 3, 8: 4, 9: 5},
    )
    q_ext, f0, query_done = call(
        functools.partial(query_kernel, taps, steps),
        (far[1], halo, filt),
        [wide_spec, halo_spec, filt_spec],
        [ext, seq],
        [ext_spec, seq_spec],
        20,
        "query",
    )
    res_pos, cot_pos, inputs_done = call(
        functools.partial(inputs_kernel, steps),
        (far[0], far[4]),
        [wide_spec] * 2,
        [seq, seq],
        [seq_spec] * 2,
        10,
        "inputs",
    )
    y, _ = call(
        functools.partial(near_kernel, modes, steps),
        (u, lam, res, skip),
        [seq_spec, mode_spec, mode_spec, one_spec],
        [seq],
        [seq_spec],
        10,
        "near",
    )
    own_lag, own_lag_done = call(
        functools.partial(lags_kernel, modes, steps),
        (u, lam),
        [seq_spec, mode_spec],
        [eights],
        [eights_spec],
        32,
        "lags",
    )
    before, other, group = scan_but_last(x_own, lam, steps, 1, [query_done, inputs_done])
    modal, summed, x_at, sums, _ = call(
        functools.partial(summed_kernel, modes, steps, blocks, group),
        (y, f0, res_pos, cot_pos, g, before, other, lam, res, gain, own_lag_done),
        [seq_spec] * 4 + [eights_spec] + [mode_spec] * 4 + [one_spec, any_spec],
        [seq, seq, eights, jax.ShapeDtypeStruct((2, steps), F32)],
        [seq_spec, seq_spec, eights_spec, pl.BlockSpec((2, steps), lambda h: (0, 0))],
        50,
        "summed",
        scratch=[pltpu.VMEM((steps * SUB, LANES), F32)] * 2,
    )
    all_sums = [sums, *(swap(sums, "tp", k) for k in range(1, lax.axis_size("tp")))]
    lag, lag_sum, lags_done = call(
        functools.partial(borders_kernel, modes, steps),
        (own_lag, x_at, lam),
        [eights_spec, eights_spec, mode_spec],
        [eights, mode],
        [eights_spec, mode_spec],
        8,
        "borders",
    )
    scale_spec = pl.BlockSpec((2 * steps, LANES), lambda h: (0, 0))
    scale, gm, adj, a_own, _ = call(
        functools.partial(grad_modal_kernel, modes, steps, width, len(all_sums)),
        (*all_sums, summed, cot_pos, f0, lam, gain, lags_done),
        [pl.BlockSpec((2, steps), lambda h: (0, 0))] * len(all_sums)
        + [seq_spec, seq_spec, seq_spec, mode_spec, one_spec, any_spec],
        [pltpu.VMEM((2 * steps, LANES), F32), seq, eights, mode],
        [scale_spec, seq_spec, eights_spec, mode_spec],
        45,
        "grad_modal",
    )
    res_part, rate_part, across_done = call(
        functools.partial(across_kernel, modes, steps),
        (gm, adj, x_at, lag, lam),
        [seq_spec, eights_spec, eights_spec, eights_spec, mode_spec],
        [mode, mode],
        [mode_spec, mode_spec],
        50,
        "across",
    )
    gmy, res_sum, rate_sum, skip_sum, near_done = call(
        functools.partial(near_adjoint_kernel, modes, steps),
        (gm, u, lam, res, skip, res_part, rate_part),
        [seq_spec, seq_spec, mode_spec, mode_spec, one_spec, mode_spec, mode_spec],
        [seq, mode, mode, one],
        [seq_spec, mode_spec, mode_spec, one_spec],
        25,
        "near_adjoint",
    )
    early_rows = taps + modes + 2
    gf0, early, _ = call(
        functools.partial(query_sums_kernel, modes, taps, steps),
        (scale, summed, cot_pos, modal, q_ext, gain, res_sum, skip_sum),
        [scale_spec, seq_spec, seq_spec, seq_spec, ext_spec, one_spec, mode_spec, one_spec],
        [seq, pos(early_rows)],
        [seq_spec, pos_spec(early_rows)],
        30,
        "query_sums",
    )
    before, other, group = scan_but_last(a_own, lam, steps, -1, [across_done, near_done])

    half = blocks // 2
    half_shape = (half * (early_rows + modes) * SUB, LANES)
    alpha, kept_half, sent_half = small(
        functools.partial(pack_kernel, steps, group, modes, early_rows, half),
        [before, other, lam, early, res, rate_sum, lag_sum],
        [],
        [lam.shape, half_shape, half_shape],
        "pack",
    )
    early_rows += modes
    late_rows = 2 * taps
    next_spec = pl.BlockSpec((3, 1, SUB * SUB, LANES), lambda h: (0, h, 0, 0))
    other_half = swap(sent_half, "ctx", 1)
    gf1, gf2, heads, mixed_done = call(
        functools.partial(mixed_kernel, modes, taps, steps),
        (gmy, f1, f2, gf0, adj, lam, res, alpha),
        [seq_spec] * 4 + [eights_spec] + [mode_spec] * 3,
        [seq, seq, jax.ShapeDtypeStruct((3, blocks, SUB * SUB, LANES), BF16)],
        [seq_spec, seq_spec, next_spec],
        45,
        "mixed",
    )
    next_head = ring(heads, "ctx", -1)
    late, late_done = call(
        functools.partial(filter_sums_kernel, taps, steps),
        (gf1, gf2, k_ext, v_ext),
        [seq_spec, seq_spec, ext_spec, ext_spec],
        [pos(late_rows)],
        [pos_spec(late_rows)],
        30,
        "filter_sums",
    )

    normed, grad_residual, norm_done = call(
        functools.partial(norm_kernel, steps),
        (scale, summed, cot_pos, gain, late_done),
        [scale_spec, seq_spec, seq_spec, one_spec, any_spec],
        [wide, wide],
        [wide_spec, wide_spec],
        25,
        "norm",
        scratch=[pltpu.VMEM((steps * SUB, LANES), F32)],
    )

    def back(which, grad, name):
        return call(
            functools.partial(back_kernel, which, taps, steps, lax.axis_size("ctx") - 1),
            (grad, next_head, filt),
            [seq_spec, next_spec, filt_spec],
            [wide],
            [wide_spec],
            20,
            name,
            scratch=[
                pltpu.VMEM((steps * SUB, LANES), F32),
                pltpu.VMEM((SUB * SUB, LANES), F32),
            ],
        )

    grad_query, query_done = back(0, gf0, "back_query")
    grad_key, key_done = back(1, gf1, "back_key")
    grad_value, value_done = back(2, gf2, "back_value")
    count, under = lax.axis_size("ctx"), [[late_done, next_head], [norm_done, query_done]]
    mine = small(add_kernel, [kept_half, other_half], [mixed_done], [half_shape], "add")[0]
    step = 2
    while step < count:
        after = under.pop(0) if under else [query_done]
        mine = small(add_kernel, [mine, swap(mine, "ctx", step)], after, [half_shape], "add")[0]
        step *= 2
    other = swap(mine, "ctx", 1)
    step, under = 1, [[norm_done, query_done], [key_done]]
    late_other = swap(late, "ctx", step)
    while 2 * step < count:
        after = under.pop(0) if under else [key_done]
        late = small(add_kernel, [late, late_other], after, [late.shape], "add")[0]
        step *= 2
        late_other = swap(late, "ctx", step)
    half_spec = pl.BlockSpec((early_rows * SUB, LANES), lambda h: (h % half, 0))
    late_spec = pos_spec(late_rows)
    grad_short, grad_residues, grad_rate, grad_skip, grad_gain, _ = call(
        functools.partial(finish_kernel, modes, taps, half, early_rows),
        (mine, other, late, late_other, value_done),
        [half_spec, half_spec, late_spec, late_spec, any_spec],
        [
            jax.ShapeDtypeStruct(short_filter.shape, F32),
            jax.ShapeDtypeStruct(residues.shape, F32),
            jax.ShapeDtypeStruct(residues.shape, F32),
            one,
            one,
        ],
        [short_spec, param_spec, param_spec, one_spec, one_spec],
        1,
        "finish",
        scratch=[
            pltpu.VMEM((late_rows * SUB, LANES), F32),
            pltpu.VMEM((early_rows * SUB, LANES), F32),
        ],
    )
    return (
        normed,
        grad_residual,
        grad_query,
        grad_key,
        grad_value,
        grad_short,
        grad_residues,
        grad_rate,
        grad_skip.reshape(channels),
        grad_gain.reshape(channels),
    )


def solution(mesh):
    both, modes, vector = P("ctx", "tp"), P(None, "tp"), P("tp")
    return jax.shard_map(
        shards,
        mesh=mesh,
        in_specs=(both, both, both, both, P(None, None, "tp"), modes, modes, vector, vector, both),
        out_specs=(both,) * 5 + (P(None, None, "tp"), modes, modes, vector, vector),
        check_vma=False,
    )
```

```python
import functools

import jax
import jax.numpy as jnp
from jax import lax
from jax.experimental import pallas as pl
from jax.experimental.pallas import tpu as pltpu
from jax.sharding import PartitionSpec as P

LANES = 128
SUB = 8
CHUNK = 16
WIDE = SUB * LANES
F32 = jnp.float32
BF16 = jnp.bfloat16
VMEM_LIMIT = 10 * 1024 * 1024


def row(ref, t):
    return ref[pl.ds(pl.multiple_of(t * SUB, SUB), SUB), :]


def put(ref, t, value):
    ref[pl.ds(pl.multiple_of(t * SUB, SUB), SUB), :] = value


def loop(start, stop, body, carry):
    pairs = (stop - start) // 2

    def two(i, carry):
        return body(start + 2 * i + 1, body(start + 2 * i, carry))

    carry = lax.fori_loop(0, pairs, two, carry)
    return body(stop - 1, carry) if (stop - start) % 2 else carry


def spread_chunk(src, dst, first, c):
    start = pl.multiple_of(c * CHUNK, CHUNK)
    for g in range(SUB):
        piece = src[pl.ds(start, CHUNK), g * LANES : (g + 1) * LANES].astype(F32)
        dst[pl.ds((start + first) * SUB + g, CHUNK, stride=SUB), :] = piece


def spread(src, dst, first, count):
    def some(c, carry):
        spread_chunk(src, dst, first, c)
        return carry

    loop(0, count // CHUNK, some, 0)


def gather_rows(src, dst, count):
    def some(i, carry):
        start = pl.multiple_of(i * 16, 16)
        for g in range(SUB):
            piece = src[pl.ds(start * SUB + g, 16, stride=SUB), :]
            dst[pl.ds(start, 16), g * LANES : (g + 1) * LANES] = piece.astype(dst.dtype)
        return carry

    loop(0, count // 16, some, 0)


def total(values):
    values = list(values)
    while len(values) > 1:
        values = [
            values[i] + values[i + 1] if i + 1 < len(values) else values[i]
            for i in range(0, len(values), 2)
        ]
    return values[0]


def taps_of(filt, stream, taps):
    return [row(filt, stream * taps + j) for j in range(taps)]


def conv_at(window, taps, i):
    margin = len(taps) - 1
    return total([taps[j] * window[margin + i - j] for j in range(margin + 1)])


def trailing_kernel(query, key, value, out):
    for i, ref in enumerate((query, key, value)):
        out[i] = ref[...].astype(F32)[SUB:, :].astype(BF16)


def features_kernel(
    modes, taps, steps, key, value, filt3, decay, resid, k_ext, v_ext, f1, f2, u, g, lam, res, faded, filt, x_out
):
    margin = taps - 1
    for s in range(SUB):
        lanes = slice(s * LANES, (s + 1) * LANES)
        lam[pl.ds(s, modes, stride=SUB), :] = decay[:, lanes]
        res[pl.ds(s, modes, stride=SUB), :] = resid[:, lanes]
        for i in range(3):
            filt[pl.ds(i * taps * SUB + s, taps, stride=SUB), :] = filt3[i, :, lanes]
    faded[...] = res[...] * jnp.exp(-lam[...])
    taps1, taps2 = taps_of(filt, 1, taps), taps_of(filt, 2, taps)
    fade, skip = fades(lam, modes, 1), fades(lam, modes, SUB)
    chunks = steps // CHUNK

    def shape(c):
        for src, dst in ((key, k_ext), (value, v_ext)):
            spread_chunk(src, dst, SUB, c)

    def conv(c, skipped=0):
        t0 = c * CHUNK
        kw = [row(k_ext, t0 + SUB - margin + i) for i in range(skipped, CHUNK + margin)]
        vw = [row(v_ext, t0 + SUB - margin + i) for i in range(skipped, CHUNK + margin)]
        for i in range(CHUNK - skipped):
            first, second = conv_at(kw, taps1, i), conv_at(vw, taps2, i)
            put(f1, t0 + skipped + i, first)
            put(f2, t0 + skipped + i, second)
            put(u, t0 + skipped + i, first * second)

    def advance(c, x, skipped=0):
        for b in range(skipped, CHUNK // SUB):
            block = c * (CHUNK // SUB) + b
            now = [row(u, block * SUB + i) for i in range(SUB)]
            new = []
            for m in range(modes):
                own = horner(fade[m], now)
                put(g, block * modes + m, own)
                new.append(own + skip[m] * x[m])
            x = tuple(new)
        return x

    shape(0)
    shape(1)
    conv(0, SUB)
    shape(2)
    conv(1)
    x = advance(0, zeros(modes), 1)

    def some(c, x):
        shape(c + 1)
        conv(c)
        return advance(c - 1, x)

    x = lax.fori_loop(2, chunks - 1, some, x)
    conv(chunks - 1)
    x = advance(chunks - 1, advance(chunks - 2, x))
    for m in range(modes):
        put(x_out, m, x[m])


def zeros(count):
    return tuple(jnp.zeros((SUB, LANES), F32) for _ in range(count))


def fades(lam, modes, span):
    return [jnp.exp(row(lam, m) * -float(span)) for m in range(modes)]


def horner(fade, values):
    result = values[0]
    for value in values[1:]:
        result = fade * result + value
    return result


def head_kernel(
    modes, taps, steps, halo, k_head, v_head, filt, lam, x_part, f1_in, f2_in, u_in, g_in,
    k_ext, v_ext, f1, f2, u, g, x_out,
):
    del f1_in, f2_in, u_in, g_in
    margin = taps - 1
    there = jnp.where(lax.axis_index("ctx") > 0, 1.0, 0.0)
    for s in range(SUB):
        lanes = slice(s * LANES, (s + 1) * LANES)
        k_ext[pl.ds(s, SUB, stride=SUB), :] = halo[1, :, lanes].astype(F32) * there
        v_ext[pl.ds(s, SUB, stride=SUB), :] = halo[2, :, lanes].astype(F32) * there
    taps1, taps2 = taps_of(filt, 1, taps), taps_of(filt, 2, taps)
    kw = [row(k_ext, SUB - margin + i) for i in range(margin)] + [row(k_head, i) for i in range(SUB)]
    vw = [row(v_ext, SUB - margin + i) for i in range(margin)] + [row(v_head, i) for i in range(SUB)]
    mixed = []
    for i in range(SUB):
        first, second = conv_at(kw, taps1, i), conv_at(vw, taps2, i)
        put(f1, i, first)
        put(f2, i, second)
        put(u, i, first * second)
        mixed.append(first * second)
    fade, rest = fades(lam, modes, 1), fades(lam, modes, steps - SUB)
    for m in range(modes):
        own = horner(fade[m], mixed)
        put(g, m, own)
        put(x_out, m, row(x_part, m) + rest[m] * own)


def query_kernel(taps, steps, query, halo, filt, q_ext, f0):
    margin = taps - 1
    there = jnp.where(lax.axis_index("ctx") > 0, 1.0, 0.0)
    for s in range(SUB):
        lanes = slice(s * LANES, (s + 1) * LANES)
        q_ext[pl.ds(s, SUB, stride=SUB), :] = halo[0, :, lanes].astype(F32) * there
    spread(query, q_ext, SUB, steps)
    taps0 = taps_of(filt, 0, taps)

    def conv(c, carry):
        t0 = c * SUB
        qw = [row(q_ext, t0 + SUB - margin + i) for i in range(SUB + margin)]
        for i in range(SUB):
            put(f0, t0 + i, conv_at(qw, taps0, i))
        return carry

    loop(0, steps // SUB, conv, 0)


def inputs_kernel(steps, residual, cot, res_pos, cot_pos):
    spread(residual, res_pos, 0, steps)
    spread(cot, cot_pos, 0, steps)


def near_taps(lam, res, skip, modes):
    fade, weight = fades(lam, modes, 1), [row(res, m) for m in range(modes)]
    result = []
    for k in range(SUB):
        result.append(total(weight) if k else total(weight) + skip[...])
        weight = [f * w for f, w in zip(fade, weight)]
    return result


def near_kernel(modes, steps, u, lam, res, skip, y):
    near = near_taps(lam, res, skip, modes)

    def some(c, carry):
        now = [row(u, c * SUB + i) for i in range(SUB)]
        for i in range(SUB):
            put(y, c * SUB + i, total([near[k] * now[i - k] for k in range(i + 1)]))
        return carry

    loop(0, steps // SUB, some, 0)


def lags_kernel(modes, steps, u, lam, lag):
    fade = fades(lam, modes, 1)

    def some(c, carry):
        now = [row(u, c * SUB + i) * float(SUB - i) for i in range(SUB)]
        for m in range(modes):
            put(lag, c * modes + m, horner(fade[m], now))
        return carry

    loop(0, steps // SUB, some, 0)


def borders_kernel(modes, steps, own_lag, x_at, lam, lag, lag_sum):
    skip = fades(lam, modes, SUB)
    eight = [float(SUB) * v for v in skip]

    def some(c, sums):
        new = []
        for m in range(modes):
            border = row(own_lag, c * modes + m) + eight[m] * row(x_at, c * modes + m)
            put(lag, c * modes + m, border)
            new.append(skip[m] * sums[m] + border)
        return tuple(new)

    sums = loop(0, steps // SUB, some, zeros(modes))
    for m in range(modes):
        put(lag_sum, m, sums[m])


def summed_kernel(modes, steps, blocks, group, y, f0, res_pos, cot_pos, g, before, other, lam, faded, gain, ready, modal, summed, x_at, sums, squares, inner):
    del ready
    block = pl.program_id(0)

    @pl.when(block == 0)
    def _():
        squares[...] = jnp.zeros_like(squares)
        inner[...] = jnp.zeros_like(inner)

    fade, skip = fades(lam, modes, 1), fades(lam, modes, SUB)
    factor = gain[...]
    x_in = exclusive(before[...], other[...], lam[...], steps, group, 1)
    x_in = tuple(x_in[m * SUB : (m + 1) * SUB, :] for m in range(modes))

    def advance(c, x):
        w = [row(faded, m) * x[m] for m in range(modes)]
        for m in range(modes):
            put(x_at, c * modes + m, x[m])
        for i in range(SUB):
            t = c * SUB + i
            if i:
                w = [f * v for f, v in zip(fade, w)]
            long = row(y, t) + total(w)
            put(modal, t, long)
            now = row(res_pos, t) + row(f0, t) * long
            put(summed, t, now)
            put(squares, t, row(squares, t) + now * now)
            put(inner, t, row(inner, t) + factor * row(cot_pos, t) * now)
        return tuple(row(g, c * modes + m) + skip[m] * x[m] for m in range(modes))

    loop(0, steps // SUB, advance, x_in)

    @pl.when(block == blocks - 1)
    def _():
        for which, scratch in enumerate((squares, inner)):
            for b in range(steps // LANES):
                part = total(
                    [
                        scratch[pl.ds(b * LANES * SUB + s, LANES, stride=SUB), :]
                        for s in range(SUB)
                    ]
                )
                sums[which : which + 1, b * LANES : (b + 1) * LANES] = jnp.sum(
                    part.T, axis=0, keepdims=True
                )


def grad_modal_kernel(modes, steps, width, shares, *refs):
    own_sums, (summed, cot_pos, f0, lam, gain, ready) = refs[:shares], refs[shares : shares + 6]
    scale, gm, adj, a_out = refs[shares + 6 :]
    del ready

    @pl.when(pl.program_id(0) == 0)
    def _():
        sums = total([ref[...] for ref in own_sums])
        inv = lax.rsqrt(sums[0:1, :] / width + 1e-05)
        coef = inv * inv * inv * sums[1:2, :] / width
        for which, value in enumerate((inv, coef)):
            for b in range(steps // LANES):
                piece = value[:, b * LANES : (b + 1) * LANES]
                scale[pl.ds(which * steps + b * LANES, LANES), :] = jnp.broadcast_to(
                    piece, (LANES, LANES)
                ).T

    fade, skip = fades(lam, modes, 1), fades(lam, modes, SUB)
    factor = gain[...]

    def advance(c, a):
        block = steps // SUB - 1 - c
        now = [None] * SUB
        for i in reversed(range(SUB)):
            t = block * SUB + i
            inv = scale[pl.ds(t, 1), :]
            coef = scale[pl.ds(steps + t, 1), :]
            grad = inv * (factor * row(cot_pos, t)) - coef * row(summed, t)
            now[i] = grad * row(f0, t)
            put(gm, t, now[i])
        new = []
        for m in range(modes):
            own = horner(fade[m], now[::-1])
            put(adj, block * modes + m, own)
            new.append(own + skip[m] * a[m])
        return tuple(new)

    a = loop(0, steps // SUB, advance, zeros(modes))
    for m in range(modes):
        put(a_out, m, a[m])


def across_kernel(ms, modes, steps, gm, adj, x_at, lag, lam, res_part, rate_part):
    fade, far = fades(lam, modes, 1), fades(lam, modes, SUB)
    last = steps // SUB - 1

    def across(c, state):
        after, by_res, by_rate = (list(v) for v in state)
        block = last - c
        now = [row(gm, block * SUB + i) * float(i) for i in range(1, SUB)]
        for i, m in enumerate(ms):
            x, own = row(x_at, block * modes + m), row(adj, block * modes + m)
            tail = fade[m] * horner(fade[m], now[::-1])
            by_res[i] = by_res[i] + x * own
            by_rate[i] = by_rate[i] + (x * tail + after[i] * row(lag, block * modes + m))
            after[i] = own + far[m] * after[i]
        return tuple(after), tuple(by_res), tuple(by_rate)

    none = zeros(len(ms))
    _, by_res, by_rate = loop(0, steps // SUB, across, (none, none, none))
    for i, m in enumerate(ms):
        put(res_part, i, fade[m] * by_res[i])
        put(rate_part, i, fade[m] * by_rate[i])


def near_adjoint_kernel(modes, steps, gm, u, lam, res, skip, *refs):
    res_parts, rate_parts, (gmy, res_sum, rate_sum, skip_sum) = refs[:2], refs[2:4], refs[4:]
    half = modes // 2
    near = near_taps(lam, res, skip, modes)

    def pairs(c, lags):
        now = [row(gm, c * SUB + i) for i in range(SUB)]
        for i in range(SUB):
            put(gmy, c * SUB + i, total([near[k] * now[i + k] for k in range(SUB - i)]))
        before = [row(u, c * SUB + i) for i in range(SUB)]
        return tuple(
            lags[k] + total([now[i] * before[i - k] for i in range(k, SUB)]) for k in range(SUB)
        )

    lags = loop(0, steps // SUB, pairs, zeros(SUB))
    skip_sum[...] = lags[0]
    fade = fades(lam, modes, 1)
    weighted = [lags[k] * float(k) for k in range(1, SUB)]
    for m in range(modes):
        put(res_sum, m, row(res_parts[m // half], m % half) + horner(fade[m], lags[::-1]))
        put(rate_sum, m, row(rate_parts[m // half], m % half) + fade[m] * horner(fade[m], weighted[::-1]))


def norm_kernel(steps, scale, summed, cot_pos, gain, ready, normed, grad_res, work):
    del ready
    factor = gain[...]

    def norm(c, carry):
        for i in range(SUB):
            t = c * SUB + i
            put(work, t, row(summed, t) * scale[pl.ds(t, 1), :] * factor)
        return carry

    loop(0, steps // SUB, norm, 0)
    gather_rows(work, normed, steps)

    def grads(c, carry):
        for i in range(SUB):
            t = c * SUB + i
            inv = scale[pl.ds(t, 1), :]
            coef = scale[pl.ds(steps + t, 1), :]
            put(work, t, inv * (factor * row(cot_pos, t)) - coef * row(summed, t))
        return carry

    loop(0, steps // SUB, grads, 0)
    gather_rows(work, grad_res, steps)


def query_sums_kernel(modes, taps, steps, scale, summed, cot_pos, modal, q_ext, gain, res_sum, skip_sum, gf0, early):
    factor = gain[...]

    def grads(c, by_gain):
        for i in range(SUB):
            t = c * SUB + i
            now, here = row(cot_pos, t), row(summed, t)
            scaled = scale[pl.ds(t, 1), :] * now
            grad = factor * scaled - scale[pl.ds(steps + t, 1), :] * here
            put(gf0, t, grad * row(modal, t))
            by_gain = by_gain + scaled * here
        return by_gain

    put(early, taps + modes + 1, loop(0, steps // SUB, grads, zeros(1)[0]))
    sums = filter_pass(taps, steps, gf0, q_ext)
    for j in range(taps):
        put(early, j, sums[j])
    early[pl.ds(taps * SUB, modes * SUB), :] = res_sum[...]
    put(early, taps + modes, skip_sum[...])


def filter_pass(taps, steps, grad, ext):
    margin = taps - 1

    def some(c, acc):
        t0 = c * SUB
        window = [row(ext, t0 + SUB - margin + i) for i in range(SUB + margin)]
        for i in range(SUB):
            now = row(grad, t0 + i)
            acc = tuple(acc[j] + now * window[margin + i - j] for j in range(taps))
        return acc

    zero = jnp.zeros((SUB, LANES), F32)
    return loop(0, steps // SUB, some, tuple(zero for _ in range(taps)))


def mixed_kernel(modes, taps, steps, gmy, f1, f2, gf0, adj, lam, faded, alpha, gf1, gf2, heads):
    fade, skip = fades(lam, modes, 1), fades(lam, modes, SUB)

    def advance(c, after):
        block = steps // SUB - 1 - c
        w = [row(faded, m) * after[m] for m in range(modes)]
        for i in reversed(range(SUB)):
            t = block * SUB + i
            grad = row(gmy, t) + total(w)
            put(gf1, t, grad * row(f2, t))
            put(gf2, t, grad * row(f1, t))
            w = [f * v for f, v in zip(fade, w)]
        return tuple(row(adj, block * modes + m) + skip[m] * after[m] for m in range(modes))

    loop(0, steps // SUB, advance, tuple(row(alpha, m) for m in range(modes)))
    for which, grad in enumerate((gf0, gf1, gf2)):
        heads[which, 0] = grad[: SUB * SUB, :].astype(BF16)


def filter_sums_kernel(taps, steps, gf1, gf2, k_ext, v_ext, sums):
    for which, (grad, ext) in enumerate(((gf1, k_ext), (gf2, v_ext))):
        parts = filter_pass(taps, steps, grad, ext)
        for j in range(taps):
            put(sums, which * taps + j, parts[j])


def back_kernel(which, taps, steps, last, grad, next_head, filt, out, work, head):
    there = jnp.where(lax.axis_index("ctx") < last, 1.0, 0.0)
    head[...] = next_head[which, 0].astype(F32) * there
    weights = taps_of(filt, which, taps)

    def some(c, carry):
        put_back(work, c * SUB, weights, [row(grad, c * SUB + i) for i in range(SUB + taps - 1)])
        return carry

    loop(0, steps // SUB - 1, some, 0)
    start = steps - SUB
    window = [row(grad, start + i) for i in range(SUB)] + [row(head, i) for i in range(taps - 1)]
    put_back(work, start, weights, window)
    gather_rows(work, out, steps)


def put_back(out, start, weights, window):
    for i in range(SUB):
        put(out, start + i, total([w * window[i + j] for j, w in enumerate(weights)]))


def place(group, sign):
    at = lax.axis_index("ctx")
    if sign < 0:
        at = lax.axis_size("ctx") - 1 - at
    later = (at // group) % 2
    return (at % group).astype(F32), later.astype(F32)


def exclusive(before, other, lam, span, group, sign):
    at, later = place(group, sign)
    here = later * jnp.exp(lam * (at * -float(span))) * other
    return here if before is None else before + here


def inclusive(own, other, lam, span, group, sign):
    _, later = place(group, sign)
    fall = -float(span * group)
    return jnp.exp(lam * ((1.0 - later) * fall)) * own + jnp.exp(lam * (later * fall)) * other


def join_kernel(span, group, sign, first, own, other, lam, *refs):
    before, ends = (None, refs[-2:]) if first else (refs[0][...], refs[-2:])
    ends[0][...] = exclusive(before, other[...], lam[...], span, group, sign)
    ends[1][...] = inclusive(own[...], other[...], lam[...], span, group, sign)


def add_kernel(one, other, *refs):
    refs[-1][...] = one[...] + other[...]


def pack_kernel(span, group, modes, first_rows, half, before, other, lam, early, res, rate_sum, lag_sum, alpha, kept, sent):
    alpha[...] = exclusive(before[...], other[...], lam[...], span, group, -1)
    odd = lax.axis_index("ctx") % 2
    rows = (first_rows + modes) * SUB
    for out, start in ((kept, odd * half), (sent, (1 - odd) * half)):
        for b in range(half):
            source = pl.multiple_of((start + b) * (first_rows * SUB), SUB)
            out[pl.ds(b * rows, first_rows * SUB), :] = early[pl.ds(source, first_rows * SUB), :]
            source = pl.multiple_of((start + b) * (modes * SUB), SUB)
            mine = pl.ds(source, modes * SUB)
            lagged = rate_sum[mine, :] + jnp.exp(-lam[mine, :]) * alpha[mine, :] * lag_sum[mine, :]
            out[pl.ds(b * rows + first_rows * SUB, modes * SUB), :] = -res[mine, :] * lagged


def finish_kernel(modes, taps, half, early_rows, mine, other, late_mine, late_other, after, short, res, rate, skip, gain, late, early):
    del after
    block = pl.program_id(0)
    late[...] = late_mine[...] + late_other[...]
    own = jnp.where(lax.axis_index("ctx") % 2 == block // half, 1.0, 0.0)
    early[...] = own * mine[...] + (1.0 - own) * other[...]
    for s in range(SUB):
        lanes = slice(s * LANES, (s + 1) * LANES)
        short[0, :, lanes] = early[pl.ds(s, taps, stride=SUB), :]
        short[1, :, lanes] = late[pl.ds(s, taps, stride=SUB), :]
        short[2, :, lanes] = late[pl.ds(taps * SUB + s, taps, stride=SUB), :]
        res[:, lanes] = early[pl.ds(taps * SUB + s, modes, stride=SUB), :]
        rate[:, lanes] = early[pl.ds((taps + modes + 2) * SUB + s, modes, stride=SUB), :]
    skip[...] = row(early, taps + modes)
    gain[...] = row(early, taps + modes + 1)


def ring(value, axis, distance):
    count = lax.axis_size(axis)
    return lax.ppermute(value, axis, [(i, (i + distance) % count) for i in range(count)])


def swap(value, axis, step):
    return lax.ppermute(value, axis, [(i, i ^ step) for i in range(lax.axis_size(axis))])


def small(body, ins, after, outs, name):
    near = pl.BlockSpec(memory_space=pltpu.VMEM)
    return pl.pallas_call(
        body,
        in_specs=[near] * len(ins) + [pl.BlockSpec(memory_space=pl.ANY)] * len(after),
        out_specs=[near] * len(outs),
        out_shape=[jax.ShapeDtypeStruct(shape, F32) for shape in outs],
        compiler_params=pltpu.CompilerParams(vmem_limit_bytes=VMEM_LIMIT),
        cost_estimate=pl.CostEstimate(flops=ins[0].size, bytes_accessed=0, transcendentals=0),
        name=name,
    )(*ins, *after)


def scan_but_last(own, lam, span, sign, under):
    count, group, before = lax.axis_size("ctx"), 1, None
    under = list(under)
    while True:
        other = swap(own, "ctx", group)
        if 2 * group >= count:
            return before, other, group
        body = functools.partial(join_kernel, span, group, sign, before is None)
        ins = [own, other, lam] + ([] if before is None else [before])
        after = [under.pop(0)] if under else []
        before, own = small(body, ins, after, [own.shape] * 2, "join")
        group *= 2


def shards(
    residual, query_in, key_in, value_in, short_filter, residues, decay_rate, skip_gain, norm_gain, cotangent
):
    steps, channels = residual.shape
    modes, taps = residues.shape[0], short_filter.shape[1]
    blocks = channels // WIDE
    width = channels * lax.axis_size("tp")
    skip, gain = (v.reshape(blocks * SUB, LANES) for v in (skip_gain, norm_gain))

    def pos(count):
        return jax.ShapeDtypeStruct((blocks * count * SUB, LANES), F32)

    def kept(count):
        return pltpu.VMEM((blocks * count * SUB, LANES), F32)

    def pos_spec(count):
        return pl.BlockSpec((count * SUB, LANES), lambda h: (h, 0))

    def head_spec(total_steps, start):
        return pl.BlockSpec((SUB * SUB, LANES), lambda h: (h * (total_steps // SUB) + start, 0))

    wide_spec = pl.BlockSpec((steps, WIDE), lambda h: (0, h))
    wide = jax.ShapeDtypeStruct((steps, channels), BF16)
    mode_spec, one_spec, filt_spec = pos_spec(modes), pos_spec(1), pos_spec(3 * taps)
    seq_spec, ext_spec = pos_spec(steps), pos_spec(steps + SUB)
    seq, ext, mode, one = kept(steps), kept(steps + SUB), pos(modes), pos(1)
    eights, eights_spec = kept(steps // SUB * modes), pos_spec(steps // SUB * modes)
    halo_spec = pl.BlockSpec((3, SUB, WIDE), lambda h: (0, 0, h))
    param_spec = pl.BlockSpec((modes, WIDE), lambda h: (0, h))
    short_spec = pl.BlockSpec((3, taps, WIDE), lambda h: (0, 0, h))

    def call(body, ins, in_specs, outs, out_specs, ops, name, scratch=(), aliases=None):
        elements, n_refs = steps * channels, len(ins) + len(outs)

        def with_done(*refs):
            done = refs[n_refs]
            done[...] = jnp.zeros_like(done)
            body(*refs[:n_refs], *refs[n_refs + 1 :])

        near = blocks * steps * SUB
        ins = [
            pltpu.with_memory_space_constraint(v, pltpu.VMEM) if v.shape[0] >= near and v.dtype == F32 else v
            for v in ins
        ]
        done_shape = (SUB, LANES)
        outs = [*outs, jax.ShapeDtypeStruct(done_shape, F32)]
        out_specs = [*out_specs, pl.BlockSpec(done_shape, lambda h: (0, 0))]
        return pl.pallas_call(
            with_done,
            grid=(blocks,),
            in_specs=in_specs,
            out_specs=out_specs,
            out_shape=outs,
            scratch_shapes=list(scratch),
            input_output_aliases=aliases or {},
            compiler_params=pltpu.CompilerParams(
                dimension_semantics=("arbitrary",), vmem_limit_bytes=VMEM_LIMIT
            ),
            cost_estimate=pl.CostEstimate(
                flops=ops * elements, bytes_accessed=4 * elements, transcendentals=0
            ),
            name=name,
        )(*ins)

    far = [
        pltpu.with_memory_space_constraint(v, pltpu.HBM)
        for v in (residual, query_in, key_in, value_in, cotangent, short_filter, decay_rate, residues)
    ]
    last_spec = pl.BlockSpec((2 * SUB, channels), lambda h: (steps // (2 * SUB) - 1, 0))
    trailing = pl.pallas_call(
        trailing_kernel,
        grid=(1,),
        in_specs=[last_spec] * 3,
        out_specs=pl.BlockSpec((3, SUB, channels), lambda h: (0, 0, 0)),
        out_shape=jax.ShapeDtypeStruct((3, SUB, channels), BF16),
        compiler_params=pltpu.CompilerParams(vmem_limit_bytes=VMEM_LIMIT),
        cost_estimate=pl.CostEstimate(flops=channels, bytes_accessed=channels, transcendentals=0),
        name="trailing",
    )(*far[1:4])
    halo = ring(trailing, "ctx", 1)

    k_ext, v_ext, f1, f2, u, g, lam, res, faded, filt, x_part, _ = call(
        functools.partial(features_kernel, modes, taps, steps),
        (far[2], far[3], *far[5:]),
        [wide_spec, wide_spec, short_spec, param_spec, param_spec],
        [ext, ext, seq, seq, seq, eights, mode, mode, mode, pos(3 * taps), mode],
        [ext_spec, ext_spec, seq_spec, seq_spec, seq_spec, eights_spec, mode_spec, mode_spec, mode_spec, filt_spec, mode_spec],
        64,
        "features",
    )
    any_spec = pl.BlockSpec(memory_space=pl.ANY)
    k_ext, v_ext, f1, f2, u, g, x_own, _ = call(
        functools.partial(head_kernel, modes, taps, steps),
        (halo, k_ext, v_ext, filt, lam, x_part, f1, f2, u, g),
        [halo_spec, head_spec(steps + SUB, 1), head_spec(steps + SUB, 1), filt_spec, mode_spec, mode_spec]
        + [any_spec] * 4,
        [ext, ext, seq, seq, seq, eights, mode],
        [head_spec(steps + SUB, 0)] * 2
        + [head_spec(steps, 0)] * 3
        + [pl.BlockSpec((modes * SUB, LANES), lambda h: (h * (steps // SUB), 0)), mode_spec],
        2,
        "head",
        aliases={1: 0, 2: 1, 6: 2, 7: 3, 8: 4, 9: 5},
    )
    q_ext, f0, query_done = call(
        functools.partial(query_kernel, taps, steps),
        (far[1], halo, filt),
        [wide_spec, halo_spec, filt_spec],
        [ext, seq],
        [ext_spec, seq_spec],
        20,
        "query",
    )
    res_pos, cot_pos, inputs_done = call(
        functools.partial(inputs_kernel, steps),
        (far[0], far[4]),
        [wide_spec] * 2,
        [seq, seq],
        [seq_spec] * 2,
        10,
        "inputs",
    )
    y, _ = call(
        functools.partial(near_kernel, modes, steps),
        (u, lam, res, skip),
        [seq_spec, mode_spec, mode_spec, one_spec],
        [seq],
        [seq_spec],
        10,
        "near",
    )
    own_lag, own_lag_done = call(
        functools.partial(lags_kernel, modes, steps),
        (u, lam),
        [seq_spec, mode_spec],
        [eights],
        [eights_spec],
        32,
        "lags",
    )
    before, other, group = scan_but_last(x_own, lam, steps, 1, [query_done, inputs_done])
    modal, summed, x_at, sums, _ = call(
        functools.partial(summed_kernel, modes, steps, blocks, group),
        (y, f0, res_pos, cot_pos, g, before, other, lam, faded, gain, own_lag_done),
        [seq_spec] * 4 + [eights_spec] + [mode_spec] * 4 + [one_spec, any_spec],
        [seq, seq, eights, jax.ShapeDtypeStruct((2, steps), F32)],
        [seq_spec, seq_spec, eights_spec, pl.BlockSpec((2, steps), lambda h: (0, 0))],
        50,
        "summed",
        scratch=[pltpu.VMEM((steps * SUB, LANES), F32)] * 2,
    )
    all_sums = [sums, *(swap(sums, "tp", k) for k in range(1, lax.axis_size("tp")))]
    lag, lag_sum, lags_done = call(
        functools.partial(borders_kernel, modes, steps),
        (own_lag, x_at, lam),
        [eights_spec, eights_spec, mode_spec],
        [eights, mode],
        [eights_spec, mode_spec],
        8,
        "borders",
    )
    scale_spec = pl.BlockSpec((2 * steps, LANES), lambda h: (0, 0))
    scale, gm, adj, a_own, _ = call(
        functools.partial(grad_modal_kernel, modes, steps, width, len(all_sums)),
        (*all_sums, summed, cot_pos, f0, lam, gain, lags_done),
        [pl.BlockSpec((2, steps), lambda h: (0, 0))] * len(all_sums)
        + [seq_spec, seq_spec, seq_spec, mode_spec, one_spec, any_spec],
        [pltpu.VMEM((2 * steps, LANES), F32), seq, eights, mode],
        [scale_spec, seq_spec, eights_spec, mode_spec],
        45,
        "grad_modal",
    )
    few = modes // 2
    res_parts, rate_parts, across_done = zip(
        *(
            call(
                functools.partial(across_kernel, range(start, start + few), modes, steps),
                (gm, adj, x_at, lag, lam),
                [seq_spec, eights_spec, eights_spec, eights_spec, mode_spec],
                [pos(few), pos(few)],
                [pos_spec(few), pos_spec(few)],
                25,
                "across",
            )
            for start in (0, few)
        )
    )
    gmy, res_sum, rate_sum, skip_sum, _ = call(
        functools.partial(near_adjoint_kernel, modes, steps),
        (gm, u, lam, res, skip, *res_parts, *rate_parts),
        [seq_spec, seq_spec, mode_spec, mode_spec, one_spec] + [pos_spec(few)] * 4,
        [seq, mode, mode, one],
        [seq_spec, mode_spec, mode_spec, one_spec],
        25,
        "near_adjoint",
    )
    early_rows = taps + modes + 2
    gf0, early, _ = call(
        functools.partial(query_sums_kernel, modes, taps, steps),
        (scale, summed, cot_pos, modal, q_ext, gain, res_sum, skip_sum),
        [scale_spec, seq_spec, seq_spec, seq_spec, ext_spec, one_spec, mode_spec, one_spec],
        [seq, pos(early_rows)],
        [seq_spec, pos_spec(early_rows)],
        30,
        "query_sums",
    )
    before, other, group = scan_but_last(a_own, lam, steps, -1, across_done)

    half = blocks // 2
    half_shape = (half * (early_rows + modes) * SUB, LANES)
    alpha, kept_half, sent_half = small(
        functools.partial(pack_kernel, steps, group, modes, early_rows, half),
        [before, other, lam, early, res, rate_sum, lag_sum],
        [],
        [lam.shape, half_shape, half_shape],
        "pack",
    )
    early_rows += modes
    late_rows = 2 * taps
    next_spec = pl.BlockSpec((3, 1, SUB * SUB, LANES), lambda h: (0, h, 0, 0))
    other_half = swap(sent_half, "ctx", 1)
    gf1, gf2, heads, mixed_done = call(
        functools.partial(mixed_kernel, modes, taps, steps),
        (gmy, f1, f2, gf0, adj, lam, faded, alpha),
        [seq_spec] * 4 + [eights_spec] + [mode_spec] * 3,
        [seq, seq, jax.ShapeDtypeStruct((3, blocks, SUB * SUB, LANES), BF16)],
        [seq_spec, seq_spec, next_spec],
        45,
        "mixed",
    )
    next_head = ring(heads, "ctx", -1)
    late, late_done = call(
        functools.partial(filter_sums_kernel, taps, steps),
        (gf1, gf2, k_ext, v_ext),
        [seq_spec, seq_spec, ext_spec, ext_spec],
        [pos(late_rows)],
        [pos_spec(late_rows)],
        30,
        "filter_sums",
    )

    normed, grad_residual, norm_done = call(
        functools.partial(norm_kernel, steps),
        (scale, summed, cot_pos, gain, late_done),
        [scale_spec, seq_spec, seq_spec, one_spec, any_spec],
        [wide, wide],
        [wide_spec, wide_spec],
        25,
        "norm",
        scratch=[pltpu.VMEM((steps * SUB, LANES), F32)],
    )

    def back(which, grad, name):
        return call(
            functools.partial(back_kernel, which, taps, steps, lax.axis_size("ctx") - 1),
            (grad, next_head, filt),
            [seq_spec, next_spec, filt_spec],
            [wide],
            [wide_spec],
            20,
            name,
            scratch=[
                pltpu.VMEM((steps * SUB, LANES), F32),
                pltpu.VMEM((SUB * SUB, LANES), F32),
            ],
        )

    grad_query, query_done = back(0, gf0, "back_query")
    grad_key, key_done = back(1, gf1, "back_key")
    grad_value, value_done = back(2, gf2, "back_value")
    count, under = lax.axis_size("ctx"), [[late_done, next_head], [norm_done, query_done]]
    mine = small(add_kernel, [kept_half, other_half], [mixed_done], [half_shape], "add")[0]
    step = 2
    while step < count:
        after = under.pop(0) if under else [query_done]
        mine = small(add_kernel, [mine, swap(mine, "ctx", step)], after, [half_shape], "add")[0]
        step *= 2
    other = swap(mine, "ctx", 1)
    step, under = 1, [[norm_done, query_done], [key_done]]
    late_other = swap(late, "ctx", step)
    while 2 * step < count:
        after = under.pop(0) if under else [key_done]
        late = small(add_kernel, [late, late_other], after, [late.shape], "add")[0]
        step *= 2
        late_other = swap(late, "ctx", step)
    half_spec = pl.BlockSpec((early_rows * SUB, LANES), lambda h: (h % half, 0))
    late_spec = pos_spec(late_rows)
    grad_short, grad_residues, grad_rate, grad_skip, grad_gain, _ = call(
        functools.partial(finish_kernel, modes, taps, half, early_rows),
        (mine, other, late, late_other, value_done),
        [half_spec, half_spec, late_spec, late_spec, any_spec],
        [
            jax.ShapeDtypeStruct(short_filter.shape, F32),
            jax.ShapeDtypeStruct(residues.shape, F32),
            jax.ShapeDtypeStruct(residues.shape, F32),
            one,
            one,
        ],
        [short_spec, param_spec, param_spec, one_spec, one_spec],
        1,
        "finish",
        scratch=[
            pltpu.VMEM((late_rows * SUB, LANES), F32),
            pltpu.VMEM((early_rows * SUB, LANES), F32),
        ],
    )
    return (
        normed,
        grad_residual,
        grad_query,
        grad_key,
        grad_value,
        grad_short,
        grad_residues,
        grad_rate,
        grad_skip.reshape(channels),
        grad_gain.reshape(channels),
    )


def solution(mesh):
    both, modes, vector = P("ctx", "tp"), P(None, "tp"), P("tp")
    return jax.shard_map(
        shards,
        mesh=mesh,
        in_specs=(both, both, both, both, P(None, None, "tp"), modes, modes, vector, vector, both),
        out_specs=(both,) * 5 + (P(None, None, "tp"), modes, modes, vector, vector),
        check_vma=False,
    )
```

```python
import functools

import jax
import jax.numpy as jnp
from jax import lax
from jax.experimental import pallas as pl
from jax.experimental.pallas import tpu as pltpu
from jax.sharding import PartitionSpec as P

LANES = 128
SUB = 8
CHUNK = 16
WIDE = SUB * LANES
F32 = jnp.float32
BF16 = jnp.bfloat16
VMEM_LIMIT = 10 * 1024 * 1024


def row(ref, t):
    return ref[pl.ds(pl.multiple_of(t * SUB, SUB), SUB), :]


def put(ref, t, value):
    ref[pl.ds(pl.multiple_of(t * SUB, SUB), SUB), :] = value


def loop(start, stop, body, carry):
    pairs = (stop - start) // 2

    def two(i, carry):
        return body(start + 2 * i + 1, body(start + 2 * i, carry))

    carry = lax.fori_loop(0, pairs, two, carry)
    return body(stop - 1, carry) if (stop - start) % 2 else carry


def spread_chunk(src, dst, first, c):
    start = pl.multiple_of(c * CHUNK, CHUNK)
    for g in range(SUB):
        piece = src[pl.ds(start, CHUNK), g * LANES : (g + 1) * LANES].astype(F32)
        dst[pl.ds((start + first) * SUB + g, CHUNK, stride=SUB), :] = piece


def spread(src, dst, first, count):
    def some(c, carry):
        spread_chunk(src, dst, first, c)
        return carry

    loop(0, count // CHUNK, some, 0)


def gather_rows(src, dst, count):
    def some(i, carry):
        start = pl.multiple_of(i * 16, 16)
        for g in range(SUB):
            piece = src[pl.ds(start * SUB + g, 16, stride=SUB), :]
            dst[pl.ds(start, 16), g * LANES : (g + 1) * LANES] = piece.astype(dst.dtype)
        return carry

    loop(0, count // 16, some, 0)


def total(values):
    values = list(values)
    while len(values) > 1:
        values = [
            values[i] + values[i + 1] if i + 1 < len(values) else values[i]
            for i in range(0, len(values), 2)
        ]
    return values[0]


def taps_of(filt, stream, taps):
    return [row(filt, stream * taps + j) for j in range(taps)]


def conv_at(window, taps, i):
    margin = len(taps) - 1
    return total([taps[j] * window[margin + i - j] for j in range(margin + 1)])


def trailing_kernel(query, key, value, out):
    for i, ref in enumerate((query, key, value)):
        out[i] = ref[...].astype(F32)[SUB:, :].astype(BF16)


def features_kernel(
    modes, taps, steps, key, value, filt3, decay, resid, k_ext, v_ext, f1, f2, u, g, lam, res, faded, filt, x_out
):
    margin = taps - 1
    for s in range(SUB):
        lanes = slice(s * LANES, (s + 1) * LANES)
        lam[pl.ds(s, modes, stride=SUB), :] = decay[:, lanes]
        res[pl.ds(s, modes, stride=SUB), :] = resid[:, lanes]
        for i in range(3):
            filt[pl.ds(i * taps * SUB + s, taps, stride=SUB), :] = filt3[i, :, lanes]
    faded[...] = res[...] * jnp.exp(-lam[...])
    taps1, taps2 = taps_of(filt, 1, taps), taps_of(filt, 2, taps)
    fade, skip = fades(lam, modes, 1), fades(lam, modes, SUB)
    chunks = steps // CHUNK

    def shape(c):
        for src, dst in ((key, k_ext), (value, v_ext)):
            spread_chunk(src, dst, SUB, c)

    def conv(c, skipped=0):
        t0 = c * CHUNK
        kw = [row(k_ext, t0 + SUB - margin + i) for i in range(skipped, CHUNK + margin)]
        vw = [row(v_ext, t0 + SUB - margin + i) for i in range(skipped, CHUNK + margin)]
        for i in range(CHUNK - skipped):
            first, second = conv_at(kw, taps1, i), conv_at(vw, taps2, i)
            put(f1, t0 + skipped + i, first)
            put(f2, t0 + skipped + i, second)
            put(u, t0 + skipped + i, first * second)

    def advance(c, x, skipped=0):
        for b in range(skipped, CHUNK // SUB):
            block = c * (CHUNK // SUB) + b
            now = [row(u, block * SUB + i) for i in range(SUB)]
            new = []
            for m in range(modes):
                own = horner(fade[m], now)
                put(g, block * modes + m, own)
                new.append(own + skip[m] * x[m])
            x = tuple(new)
        return x

    shape(0)
    shape(1)
    conv(0, SUB)
    shape(2)
    conv(1)
    x = advance(0, zeros(modes), 1)

    def some(c, x):
        shape(c + 1)
        conv(c)
        return advance(c - 1, x)

    x = lax.fori_loop(2, chunks - 1, some, x)
    conv(chunks - 1)
    x = advance(chunks - 1, advance(chunks - 2, x))
    for m in range(modes):
        put(x_out, m, x[m])


def zeros(count):
    return tuple(jnp.zeros((SUB, LANES), F32) for _ in range(count))


def fades(lam, modes, span):
    return [jnp.exp(row(lam, m) * -float(span)) for m in range(modes)]


def horner(fade, values):
    result = values[0]
    for value in values[1:]:
        result = fade * result + value
    return result


def head_kernel(
    modes, taps, steps, halo, k_head, v_head, filt, lam, x_part, f1_in, f2_in, u_in, g_in,
    k_ext, v_ext, f1, f2, u, g, x_out,
):
    del f1_in, f2_in, u_in, g_in
    margin = taps - 1
    there = jnp.where(lax.axis_index("ctx") > 0, 1.0, 0.0)
    for s in range(SUB):
        lanes = slice(s * LANES, (s + 1) * LANES)
        k_ext[pl.ds(s, SUB, stride=SUB), :] = halo[1, :, lanes].astype(F32) * there
        v_ext[pl.ds(s, SUB, stride=SUB), :] = halo[2, :, lanes].astype(F32) * there
    taps1, taps2 = taps_of(filt, 1, taps), taps_of(filt, 2, taps)
    kw = [row(k_ext, SUB - margin + i) for i in range(margin)] + [row(k_head, i) for i in range(SUB)]
    vw = [row(v_ext, SUB - margin + i) for i in range(margin)] + [row(v_head, i) for i in range(SUB)]
    mixed = []
    for i in range(SUB):
        first, second = conv_at(kw, taps1, i), conv_at(vw, taps2, i)
        put(f1, i, first)
        put(f2, i, second)
        put(u, i, first * second)
        mixed.append(first * second)
    fade, rest = fades(lam, modes, 1), fades(lam, modes, steps - SUB)
    for m in range(modes):
        own = horner(fade[m], mixed)
        put(g, m, own)
        put(x_out, m, row(x_part, m) + rest[m] * own)


def query_kernel(taps, steps, query, residual, cot, halo, filt, q_ext, f0, res_pos, cot_pos):
    margin = taps - 1
    there = jnp.where(lax.axis_index("ctx") > 0, 1.0, 0.0)
    for s in range(SUB):
        lanes = slice(s * LANES, (s + 1) * LANES)
        q_ext[pl.ds(s, SUB, stride=SUB), :] = halo[0, :, lanes].astype(F32) * there
    spread(query, q_ext, SUB, steps)
    spread(residual, res_pos, 0, steps)
    spread(cot, cot_pos, 0, steps)
    taps0 = taps_of(filt, 0, taps)

    def conv(c, carry):
        t0 = c * SUB
        qw = [row(q_ext, t0 + SUB - margin + i) for i in range(SUB + margin)]
        for i in range(SUB):
            put(f0, t0 + i, conv_at(qw, taps0, i))
        return carry

    loop(0, steps // SUB, conv, 0)


def near_taps(lam, res, skip, modes):
    fade, weight = fades(lam, modes, 1), [row(res, m) for m in range(modes)]
    result = []
    for k in range(SUB):
        result.append(total(weight) if k else total(weight) + skip[...])
        weight = [f * w for f, w in zip(fade, weight)]
    return result


def near_kernel(modes, steps, u, lam, res, skip, y):
    near = near_taps(lam, res, skip, modes)

    def some(c, carry):
        now = [row(u, c * SUB + i) for i in range(SUB)]
        for i in range(SUB):
            put(y, c * SUB + i, total([near[k] * now[i - k] for k in range(i + 1)]))
        return carry

    loop(0, steps // SUB, some, 0)


def lags_kernel(modes, steps, u, lam, lag):
    fade = fades(lam, modes, 1)

    def some(c, carry):
        now = [row(u, c * SUB + i) * float(SUB - i) for i in range(SUB)]
        for m in range(modes):
            put(lag, c * modes + m, horner(fade[m], now))
        return carry

    loop(0, steps // SUB, some, 0)


def borders_kernel(modes, steps, own_lag, x_at, lam, lag, lag_sum):
    skip = fades(lam, modes, SUB)
    eight = [float(SUB) * v for v in skip]

    def some(c, sums):
        new = []
        for m in range(modes):
            border = row(own_lag, c * modes + m) + eight[m] * row(x_at, c * modes + m)
            put(lag, c * modes + m, border)
            new.append(skip[m] * sums[m] + border)
        return tuple(new)

    sums = loop(0, steps // SUB, some, zeros(modes))
    for m in range(modes):
        put(lag_sum, m, sums[m])


def summed_kernel(modes, steps, blocks, group, y, f0, res_pos, cot_pos, g, before, other, lam, faded, gain, ready, modal, summed, x_at, sums, squares, inner):
    del ready
    block = pl.program_id(0)

    @pl.when(block == 0)
    def _():
        squares[...] = jnp.zeros_like(squares)
        inner[...] = jnp.zeros_like(inner)

    fade, skip = fades(lam, modes, 1), fades(lam, modes, SUB)
    factor = gain[...]
    x_in = exclusive(before[...], other[...], lam[...], steps, group, 1)
    x_in = tuple(x_in[m * SUB : (m + 1) * SUB, :] for m in range(modes))

    def advance(c, x):
        w = [row(faded, m) * x[m] for m in range(modes)]
        for m in range(modes):
            put(x_at, c * modes + m, x[m])
        for i in range(SUB):
            t = c * SUB + i
            if i:
                w = [f * v for f, v in zip(fade, w)]
            long = row(y, t) + total(w)
            put(modal, t, long)
            now = row(res_pos, t) + row(f0, t) * long
            put(summed, t, now)
            put(squares, t, row(squares, t) + now * now)
            put(inner, t, row(inner, t) + factor * row(cot_pos, t) * now)
        return tuple(row(g, c * modes + m) + skip[m] * x[m] for m in range(modes))

    loop(0, steps // SUB, advance, x_in)

    @pl.when(block == blocks - 1)
    def _():
        for which, scratch in enumerate((squares, inner)):
            for b in range(steps // LANES):
                part = total(
                    [
                        scratch[pl.ds(b * LANES * SUB + s, LANES, stride=SUB), :]
                        for s in range(SUB)
                    ]
                )
                sums[which : which + 1, b * LANES : (b + 1) * LANES] = jnp.sum(
                    part.T, axis=0, keepdims=True
                )


def grad_modal_kernel(modes, steps, width, shares, *refs):
    own_sums, (summed, cot_pos, f0, lam, gain, ready) = refs[:shares], refs[shares : shares + 6]
    scale, gm, adj, a_out, a_next = refs[shares + 6 :]
    del ready

    @pl.when(pl.program_id(0) == 0)
    def _():
        sums = total([ref[...] for ref in own_sums])
        inv = lax.rsqrt(sums[0:1, :] / width + 1e-05)
        coef = inv * inv * inv * sums[1:2, :] / width
        for which, value in enumerate((inv, coef)):
            for b in range(steps // LANES):
                piece = value[:, b * LANES : (b + 1) * LANES]
                scale[pl.ds(which * steps + b * LANES, LANES), :] = jnp.broadcast_to(
                    piece, (LANES, LANES)
                ).T

    fade, skip = fades(lam, modes, 1), fades(lam, modes, SUB)
    factor = gain[...]

    def advance(c, a):
        block = steps // SUB - 1 - c
        now = [None] * SUB
        for i in reversed(range(SUB)):
            t = block * SUB + i
            inv = scale[pl.ds(t, 1), :]
            coef = scale[pl.ds(steps + t, 1), :]
            grad = inv * (factor * row(cot_pos, t)) - coef * row(summed, t)
            now[i] = grad * row(f0, t)
            put(gm, t, now[i])
        new = []
        for m in range(modes):
            put(a_next, m, a[m])
            own = horner(fade[m], now[::-1])
            put(adj, block * modes + m, own)
            new.append(own + skip[m] * a[m])
        return tuple(new)

    a = loop(0, steps // SUB, advance, zeros(modes))
    for m in range(modes):
        put(a_out, m, a[m])


def across_kernel(modes, steps, *refs):
    for start in (0, modes // 2):
        across_part(range(start, start + modes // 2), modes, steps, *refs)


def across_part(ms, modes, steps, gm, adj, x_at, lag, lam, res_part, rate_part):
    fade, far = fades(lam, modes, 1), fades(lam, modes, SUB)
    last = steps // SUB - 1

    def across(c, state):
        after, by_res, by_rate = (list(v) for v in state)
        block = last - c
        now = [row(gm, block * SUB + i) * float(i) for i in range(1, SUB)]
        for i, m in enumerate(ms):
            x, own = row(x_at, block * modes + m), row(adj, block * modes + m)
            tail = fade[m] * horner(fade[m], now[::-1])
            by_res[i] = by_res[i] + x * own
            by_rate[i] = by_rate[i] + (x * tail + after[i] * row(lag, block * modes + m))
            after[i] = own + far[m] * after[i]
        return tuple(after), tuple(by_res), tuple(by_rate)

    none = zeros(len(ms))
    _, by_res, by_rate = loop(0, steps // SUB, across, (none, none, none))
    for i, m in enumerate(ms):
        put(res_part, m, fade[m] * by_res[i])
        put(rate_part, m, fade[m] * by_rate[i])


def near_adjoint_kernel(modes, taps, steps, gm, u, lam, res, skip, res_part, rate_part, scale, summed, cot_pos, modal, q_ext, gain, gmy, rate_sum, gf0, early):
    near = near_taps(lam, res, skip, modes)

    def pairs(c, lags):
        now = [row(gm, c * SUB + i) for i in range(SUB)]
        for i in range(SUB):
            put(gmy, c * SUB + i, total([near[k] * now[i + k] for k in range(SUB - i)]))
        before = [row(u, c * SUB + i) for i in range(SUB)]
        return tuple(
            lags[k] + total([now[i] * before[i - k] for i in range(k, SUB)]) for k in range(SUB)
        )

    lags = loop(0, steps // SUB, pairs, zeros(SUB))
    put(early, taps + modes, lags[0])
    fade = fades(lam, modes, 1)
    weighted = [lags[k] * float(k) for k in range(1, SUB)]
    for m in range(modes):
        put(early, taps + m, row(res_part, m) + horner(fade[m], lags[::-1]))
        put(rate_sum, m, row(rate_part, m) + fade[m] * horner(fade[m], weighted[::-1]))
    query_sums(modes, taps, steps, scale, summed, cot_pos, modal, q_ext, gain, gf0, early)


def norm_kernel(taps, steps, last, scale, summed, cot_pos, gain, gf0, next_head, filt, ready, normed, grad_res, grad_query, work, head):
    del ready
    back(0, taps, steps, last, gf0, next_head, filt, grad_query, work, head)
    factor = gain[...]

    def norm(c, carry):
        for i in range(SUB):
            t = c * SUB + i
            put(work, t, row(summed, t) * scale[pl.ds(t, 1), :] * factor)
        return carry

    loop(0, steps // SUB, norm, 0)
    gather_rows(work, normed, steps)

    def grads(c, carry):
        for i in range(SUB):
            t = c * SUB + i
            inv = scale[pl.ds(t, 1), :]
            coef = scale[pl.ds(steps + t, 1), :]
            put(work, t, inv * (factor * row(cot_pos, t)) - coef * row(summed, t))
        return carry

    loop(0, steps // SUB, grads, 0)
    gather_rows(work, grad_res, steps)


def query_sums(modes, taps, steps, scale, summed, cot_pos, modal, q_ext, gain, gf0, early):
    factor = gain[...]

    def grads(c, by_gain):
        for i in range(SUB):
            t = c * SUB + i
            now, here = row(cot_pos, t), row(summed, t)
            scaled = scale[pl.ds(t, 1), :] * now
            grad = factor * scaled - scale[pl.ds(steps + t, 1), :] * here
            put(gf0, t, grad * row(modal, t))
            by_gain = by_gain + scaled * here
        return by_gain

    put(early, taps + modes + 1, loop(0, steps // SUB, grads, zeros(1)[0]))
    sums = filter_pass(taps, steps, gf0, q_ext)
    for j in range(taps):
        put(early, j, sums[j])


def filter_pass(taps, steps, grad, ext):
    margin = taps - 1

    def some(c, acc):
        t0 = c * SUB
        window = [row(ext, t0 + SUB - margin + i) for i in range(SUB + margin)]
        for i in range(SUB):
            now = row(grad, t0 + i)
            acc = tuple(acc[j] + now * window[margin + i - j] for j in range(taps))
        return acc

    zero = jnp.zeros((SUB, LANES), F32)
    return loop(0, steps // SUB, some, tuple(zero for _ in range(taps)))


def mixed_kernel(modes, steps, gmy, f1, f2, adj, lam, faded, alpha, gf1, gf2):
    fade, skip = fades(lam, modes, 1), fades(lam, modes, SUB)

    def advance(c, after):
        block = steps // SUB - 1 - c
        w = [row(faded, m) * after[m] for m in range(modes)]
        for i in reversed(range(SUB)):
            t = block * SUB + i
            grad = row(gmy, t) + total(w)
            put(gf1, t, grad * row(f2, t))
            put(gf2, t, grad * row(f1, t))
            w = [f * v for f, v in zip(fade, w)]
        return tuple(row(adj, block * modes + m) + skip[m] * after[m] for m in range(modes))

    loop(0, steps // SUB, advance, tuple(row(alpha, m) for m in range(modes)))


def filter_sums_kernel(taps, steps, gf1, gf2, k_ext, v_ext, sums):
    for which, (grad, ext) in enumerate(((gf1, k_ext), (gf2, v_ext))):
        parts = filter_pass(taps, steps, grad, ext)
        for j in range(taps):
            put(sums, which * taps + j, parts[j])


def back_kernel(taps, steps, last, gf1, gf2, next_head, filt, grad_key, grad_value, work, head):
    back(1, taps, steps, last, gf1, next_head, filt, grad_key, work, head)
    back(2, taps, steps, last, gf2, next_head, filt, grad_value, work, head)


def back(which, taps, steps, last, grad, next_head, filt, out, work, head):
    there = jnp.where(lax.axis_index("ctx") < last, 1.0, 0.0)
    head[...] = next_head[which, 0].astype(F32) * there
    weights = taps_of(filt, which, taps)

    def some(c, carry):
        put_back(work, c * SUB, weights, [row(grad, c * SUB + i) for i in range(SUB + taps - 1)])
        return carry

    loop(0, steps // SUB - 1, some, 0)
    start = steps - SUB
    window = [row(grad, start + i) for i in range(SUB)] + [row(head, i) for i in range(taps - 1)]
    put_back(work, start, weights, window)
    gather_rows(work, out, steps)


def put_back(out, start, weights, window):
    for i in range(SUB):
        put(out, start + i, total([w * window[i + j] for j, w in enumerate(weights)]))


def place(group, sign):
    at = lax.axis_index("ctx")
    if sign < 0:
        at = lax.axis_size("ctx") - 1 - at
    later = (at // group) % 2
    return (at % group).astype(F32), later.astype(F32)


def exclusive(before, other, lam, span, group, sign):
    at, later = place(group, sign)
    here = later * jnp.exp(lam * (at * -float(span))) * other
    return here if before is None else before + here


def inclusive(own, other, lam, span, group, sign):
    _, later = place(group, sign)
    fall = -float(span * group)
    return jnp.exp(lam * ((1.0 - later) * fall)) * own + jnp.exp(lam * (later * fall)) * other


def join_kernel(span, group, sign, first, own, other, lam, *refs):
    before, ends = (None, refs[-2:]) if first else (refs[0][...], refs[-2:])
    ends[0][...] = exclusive(before, other[...], lam[...], span, group, sign)
    ends[1][...] = inclusive(own[...], other[...], lam[...], span, group, sign)


def join_four_kernel(span, sign, own, first, second, third, lam, *refs):
    before, end = refs[-2:]
    at, _ = place(4, sign)
    here = lax.axis_index("ctx") if sign > 0 else lax.axis_size("ctx") - 1 - lax.axis_index("ctx")
    here, rates = here % 4, lam[...]
    total_end = jnp.exp(rates * ((3.0 - at) * -float(span))) * own[...]
    total_before = None
    for k, other in enumerate((first, second, third)):
        there = (here ^ (k + 1)).astype(F32)
        earlier = jnp.where(there < at, 1.0, 0.0)
        gap = jnp.maximum(at - 1.0 - there, 0.0)
        value = other[...]
        share = earlier * jnp.exp(rates * (gap * -float(span))) * value
        total_before = share if total_before is None else total_before + share
        total_end = total_end + jnp.exp(rates * ((3.0 - there) * -float(span))) * value
    before[...] = total_before
    end[...] = total_end


def add_four_kernel(own, first, second, third, *refs):
    refs[-1][...] = (own[...] + first[...]) + (second[...] + third[...])


def add_kernel(one, other, *refs):
    refs[-1][...] = one[...] + other[...]


def pack_kernel(span, group, modes, first_rows, half, before, other, lam, early, res, rate_sum, lag_sum, faded, a_next, gmy, f1, f2, gf0, alpha, kept, sent, heads):
    alpha[...] = exclusive(before[...], other[...], lam[...], span, group, -1)
    odd = lax.axis_index("ctx") % 2
    rows = (first_rows + modes) * SUB
    for out, start in ((kept, odd * half), (sent, (1 - odd) * half)):
        for b in range(half):
            source = pl.multiple_of((start + b) * (first_rows * SUB), SUB)
            out[pl.ds(b * rows, first_rows * SUB), :] = early[pl.ds(source, first_rows * SUB), :]
            source = pl.multiple_of((start + b) * (modes * SUB), SUB)
            mine = pl.ds(source, modes * SUB)
            lagged = rate_sum[mine, :] + jnp.exp(-lam[mine, :]) * alpha[mine, :] * lag_sum[mine, :]
            out[pl.ds(b * rows + first_rows * SUB, modes * SUB), :] = -res[mine, :] * lagged
    for b in range(2 * half):
        mine = slice(b * modes * SUB, (b + 1) * modes * SUB)
        far = jnp.exp(lam[mine, :] * -float(span - SUB))
        w, fade = faded[mine, :] * (a_next[mine, :] + far * alpha[mine, :]), jnp.exp(-lam[mine, :])
        here, grads = slice(b * span * SUB, (b * span + SUB) * SUB), []
        for t in range(SUB):
            grads.append(total([w[m * SUB : (m + 1) * SUB, :] for m in range(modes)]))
            w = fade * w
        grad = gmy[here, :] + jnp.concatenate(grads[::-1], axis=0)
        for which, value in enumerate((gf0[here, :], grad * f2[here, :], grad * f1[here, :])):
            heads[which, b] = value.astype(BF16)


def finish_kernel(modes, taps, half, early_rows, mine, other, late_mine, late_other, ready, short, res, rate, skip, gain, late, early):
    del ready
    block = pl.program_id(0)
    late[...] = late_mine[...] + late_other[...]
    own = jnp.where(lax.axis_index("ctx") % 2 == block // half, 1.0, 0.0)
    early[...] = own * mine[...] + (1.0 - own) * other[...]
    for s in range(SUB):
        lanes = slice(s * LANES, (s + 1) * LANES)
        short[0, :, lanes] = early[pl.ds(s, taps, stride=SUB), :]
        short[1, :, lanes] = late[pl.ds(s, taps, stride=SUB), :]
        short[2, :, lanes] = late[pl.ds(taps * SUB + s, taps, stride=SUB), :]
        res[:, lanes] = early[pl.ds(taps * SUB + s, modes, stride=SUB), :]
        rate[:, lanes] = early[pl.ds((taps + modes + 2) * SUB + s, modes, stride=SUB), :]
    skip[...] = row(early, taps + modes)
    gain[...] = row(early, taps + modes + 1)


def ring(value, axis, distance):
    count = lax.axis_size(axis)
    return lax.ppermute(value, axis, [(i, (i + distance) % count) for i in range(count)])


def swap(value, axis, step):
    return lax.ppermute(value, axis, [(i, i ^ step) for i in range(lax.axis_size(axis))])


def small(body, ins, after, outs, name):
    near = pl.BlockSpec(memory_space=pltpu.VMEM)
    ins = [pltpu.with_memory_space_constraint(v, pltpu.VMEM) if v.size > 1 << 18 else v for v in ins]
    return pl.pallas_call(
        body,
        in_specs=[near] * len(ins) + [pl.BlockSpec(memory_space=pl.ANY)] * len(after),
        out_specs=[near] * len(outs),
        out_shape=[jax.ShapeDtypeStruct(shape, BF16 if len(shape) > 2 else F32) for shape in outs],
        compiler_params=pltpu.CompilerParams(vmem_limit_bytes=VMEM_LIMIT),
        cost_estimate=pl.CostEstimate(flops=ins[0].size, bytes_accessed=0, transcendentals=0),
        name=name,
    )(*ins, *after)


def scan_but_last(own, lam, span, sign, under):
    count, group, before = lax.axis_size("ctx"), 1, None
    under = list(under)
    if count >= 8:
        ins = [own, *(swap(own, "ctx", k) for k in (1, 2, 3)), lam]
        body = functools.partial(join_four_kernel, span, sign)
        before, own = small(body, ins, under, [own.shape] * 2, "join")
        group, under = 4, []
    while True:
        other = swap(own, "ctx", group)
        if 2 * group >= count:
            return before, other, group
        body = functools.partial(join_kernel, span, group, sign, before is None)
        ins = [own, other, lam] + ([] if before is None else [before])
        after = [under.pop(0)] if under else []
        before, own = small(body, ins, after, [own.shape] * 2, "join")
        group *= 2


def shards(
    residual, query_in, key_in, value_in, short_filter, residues, decay_rate, skip_gain, norm_gain, cotangent
):
    steps, channels = residual.shape
    modes, taps = residues.shape[0], short_filter.shape[1]
    blocks = channels // WIDE
    width = channels * lax.axis_size("tp")
    skip, gain = (v.reshape(blocks * SUB, LANES) for v in (skip_gain, norm_gain))

    def pos(count):
        return jax.ShapeDtypeStruct((blocks * count * SUB, LANES), F32)

    def kept(count):
        return pltpu.VMEM((blocks * count * SUB, LANES), F32)

    def pos_spec(count):
        return pl.BlockSpec((count * SUB, LANES), lambda h: (h, 0))

    def head_spec(total_steps, start):
        return pl.BlockSpec((SUB * SUB, LANES), lambda h: (h * (total_steps // SUB) + start, 0))

    wide_spec = pl.BlockSpec((steps, WIDE), lambda h: (0, h))
    wide = jax.ShapeDtypeStruct((steps, channels), BF16)
    mode_spec, one_spec, filt_spec = pos_spec(modes), pos_spec(1), pos_spec(3 * taps)
    seq_spec, ext_spec = pos_spec(steps), pos_spec(steps + SUB)
    seq, ext, mode, one = kept(steps), kept(steps + SUB), pos(modes), pos(1)
    eights, eights_spec = kept(steps // SUB * modes), pos_spec(steps // SUB * modes)
    halo_spec = pl.BlockSpec((3, SUB, WIDE), lambda h: (0, 0, h))
    param_spec = pl.BlockSpec((modes, WIDE), lambda h: (0, h))
    short_spec = pl.BlockSpec((3, taps, WIDE), lambda h: (0, 0, h))

    def call(body, ins, in_specs, outs, out_specs, ops, name, scratch=(), aliases=None):
        elements, n_refs = steps * channels, len(ins) + len(outs)

        def with_done(*refs):
            done = refs[n_refs]
            done[...] = jnp.zeros_like(done)
            body(*refs[:n_refs], *refs[n_refs + 1 :])

        near = blocks * steps * SUB
        ins = [
            pltpu.with_memory_space_constraint(v, pltpu.VMEM) if v.shape[0] >= near and v.dtype == F32 else v
            for v in ins
        ]
        done_shape = (SUB, LANES)
        outs = [*outs, jax.ShapeDtypeStruct(done_shape, F32)]
        out_specs = [*out_specs, pl.BlockSpec(done_shape, lambda h: (0, 0))]
        return pl.pallas_call(
            with_done,
            grid=(blocks,),
            in_specs=in_specs,
            out_specs=out_specs,
            out_shape=outs,
            scratch_shapes=list(scratch),
            input_output_aliases=aliases or {},
            compiler_params=pltpu.CompilerParams(
                dimension_semantics=("arbitrary",), vmem_limit_bytes=VMEM_LIMIT
            ),
            cost_estimate=pl.CostEstimate(
                flops=ops * elements, bytes_accessed=4 * elements, transcendentals=0
            ),
            name=name,
        )(*ins)

    far = [
        pltpu.with_memory_space_constraint(v, pltpu.HBM)
        for v in (residual, query_in, key_in, value_in, cotangent, short_filter, decay_rate, residues)
    ]
    last_spec = pl.BlockSpec((2 * SUB, channels), lambda h: (steps // (2 * SUB) - 1, 0))
    trailing = pl.pallas_call(
        trailing_kernel,
        grid=(1,),
        in_specs=[last_spec] * 3,
        out_specs=pl.BlockSpec((3, SUB, channels), lambda h: (0, 0, 0)),
        out_shape=jax.ShapeDtypeStruct((3, SUB, channels), BF16),
        compiler_params=pltpu.CompilerParams(vmem_limit_bytes=VMEM_LIMIT),
        cost_estimate=pl.CostEstimate(flops=channels, bytes_accessed=channels, transcendentals=0),
        name="trailing",
    )(*far[1:4])
    halo = ring(trailing, "ctx", 1)

    k_ext, v_ext, f1, f2, u, g, lam, res, faded, filt, x_part, _ = call(
        functools.partial(features_kernel, modes, taps, steps),
        (far[2], far[3], *far[5:]),
        [wide_spec, wide_spec, short_spec, param_spec, param_spec],
        [ext, ext, seq, seq, seq, eights, mode, mode, mode, pos(3 * taps), mode],
        [ext_spec, ext_spec, seq_spec, seq_spec, seq_spec, eights_spec, mode_spec, mode_spec, mode_spec, filt_spec, mode_spec],
        64,
        "features",
    )
    any_spec = pl.BlockSpec(memory_space=pl.ANY)
    k_ext, v_ext, f1, f2, u, g, x_own, _ = call(
        functools.partial(head_kernel, modes, taps, steps),
        (halo, k_ext, v_ext, filt, lam, x_part, f1, f2, u, g),
        [halo_spec, head_spec(steps + SUB, 1), head_spec(steps + SUB, 1), filt_spec, mode_spec, mode_spec]
        + [any_spec] * 4,
        [ext, ext, seq, seq, seq, eights, mode],
        [head_spec(steps + SUB, 0)] * 2
        + [head_spec(steps, 0)] * 3
        + [pl.BlockSpec((modes * SUB, LANES), lambda h: (h * (steps // SUB), 0)), mode_spec],
        2,
        "head",
        aliases={1: 0, 2: 1, 6: 2, 7: 3, 8: 4, 9: 5},
    )
    q_ext, f0, res_pos, cot_pos, query_done = call(
        functools.partial(query_kernel, taps, steps),
        (far[1], far[0], far[4], halo, filt),
        [wide_spec, wide_spec, wide_spec, halo_spec, filt_spec],
        [ext, seq, seq, seq],
        [ext_spec, seq_spec, seq_spec, seq_spec],
        30,
        "query",
    )
    y, _ = call(
        functools.partial(near_kernel, modes, steps),
        (u, lam, res, skip),
        [seq_spec, mode_spec, mode_spec, one_spec],
        [seq],
        [seq_spec],
        10,
        "near",
    )
    own_lag, own_lag_done = call(
        functools.partial(lags_kernel, modes, steps),
        (u, lam),
        [seq_spec, mode_spec],
        [eights],
        [eights_spec],
        32,
        "lags",
    )
    before, other, group = scan_but_last(x_own, lam, steps, 1, [query_done])
    modal, summed, x_at, sums, _ = call(
        functools.partial(summed_kernel, modes, steps, blocks, group),
        (y, f0, res_pos, cot_pos, g, before, other, lam, faded, gain, own_lag_done),
        [seq_spec] * 4 + [eights_spec] + [mode_spec] * 4 + [one_spec, any_spec],
        [seq, seq, eights, jax.ShapeDtypeStruct((2, steps), F32)],
        [seq_spec, seq_spec, eights_spec, pl.BlockSpec((2, steps), lambda h: (0, 0))],
        50,
        "summed",
        scratch=[pltpu.VMEM((steps * SUB, LANES), F32)] * 2,
    )
    all_sums = [sums, *(swap(sums, "tp", k) for k in range(1, lax.axis_size("tp")))]
    lag, lag_sum, lags_done = call(
        functools.partial(borders_kernel, modes, steps),
        (own_lag, x_at, lam),
        [eights_spec, eights_spec, mode_spec],
        [eights, mode],
        [eights_spec, mode_spec],
        8,
        "borders",
    )
    scale_spec = pl.BlockSpec((2 * steps, LANES), lambda h: (0, 0))
    scale, gm, adj, a_own, a_next, _ = call(
        functools.partial(grad_modal_kernel, modes, steps, width, len(all_sums)),
        (*all_sums, summed, cot_pos, f0, lam, gain, lags_done),
        [pl.BlockSpec((2, steps), lambda h: (0, 0))] * len(all_sums)
        + [seq_spec, seq_spec, seq_spec, mode_spec, one_spec, any_spec],
        [pltpu.VMEM((2 * steps, LANES), F32), seq, eights, mode, mode],
        [scale_spec, seq_spec, eights_spec, mode_spec, mode_spec],
        45,
        "grad_modal",
    )
    res_part, rate_part, across_done = call(
        functools.partial(across_kernel, modes, steps),
        (gm, adj, x_at, lag, lam),
        [seq_spec, eights_spec, eights_spec, eights_spec, mode_spec],
        [mode, mode],
        [mode_spec, mode_spec],
        50,
        "across",
    )
    early_rows = taps + modes + 2
    gmy, rate_sum, gf0, early, _ = call(
        functools.partial(near_adjoint_kernel, modes, taps, steps),
        (gm, u, lam, res, skip, res_part, rate_part, scale, summed, cot_pos, modal, q_ext, gain),
        [seq_spec, seq_spec, mode_spec, mode_spec, one_spec, mode_spec, mode_spec, scale_spec, seq_spec, seq_spec, seq_spec, ext_spec, one_spec],
        [seq, mode, seq, pos(early_rows)],
        [seq_spec, mode_spec, seq_spec, pos_spec(early_rows)],
        55,
        "near_adjoint",
    )
    before, other, group = scan_but_last(a_own, lam, steps, -1, [across_done])

    half = blocks // 2
    half_shape = (half * (early_rows + modes) * SUB, LANES)
    alpha, kept_half, sent_half, heads = small(
        functools.partial(pack_kernel, steps, group, modes, early_rows, half),
        [before, other, lam, early, res, rate_sum, lag_sum, faded, a_next, gmy, f1, f2, gf0],
        [],
        [lam.shape, half_shape, half_shape, (3, blocks, SUB * SUB, LANES)],
        "pack",
    )
    early_rows += modes
    late_rows = 2 * taps
    next_spec = pl.BlockSpec((3, 1, SUB * SUB, LANES), lambda h: (0, h, 0, 0))
    other_half = swap(sent_half, "ctx", 1)
    next_head = ring(heads, "ctx", -1)
    gf1, gf2, mixed_done = call(
        functools.partial(mixed_kernel, modes, steps),
        (gmy, f1, f2, adj, lam, faded, alpha),
        [seq_spec] * 3 + [eights_spec] + [mode_spec] * 3,
        [seq, seq],
        [seq_spec, seq_spec],
        45,
        "mixed",
    )
    late, late_done = call(
        functools.partial(filter_sums_kernel, taps, steps),
        (gf1, gf2, k_ext, v_ext),
        [seq_spec, seq_spec, ext_spec, ext_spec],
        [pos(late_rows)],
        [pos_spec(late_rows)],
        30,
        "filter_sums",
    )

    last = lax.axis_size("ctx") - 1
    back_scratch = [pltpu.VMEM((steps * SUB, LANES), F32), pltpu.VMEM((SUB * SUB, LANES), F32)]
    normed, grad_residual, grad_query, norm_done = call(
        functools.partial(norm_kernel, taps, steps, last),
        (scale, summed, cot_pos, gain, gf0, next_head, filt, late_done),
        [scale_spec, seq_spec, seq_spec, one_spec, seq_spec, next_spec, filt_spec, any_spec],
        [wide, wide, wide],
        [wide_spec, wide_spec, wide_spec],
        45,
        "norm",
        scratch=back_scratch,
    )
    grad_key, grad_value, back_done = call(
        functools.partial(back_kernel, taps, steps, last),
        (gf1, gf2, next_head, filt),
        [seq_spec, seq_spec, next_spec, filt_spec],
        [wide, wide],
        [wide_spec, wide_spec],
        40,
        "back",
        scratch=back_scratch,
    )
    count, under = lax.axis_size("ctx"), [[late_done], [norm_done]]
    mine = small(add_kernel, [kept_half, other_half], [mixed_done, next_head], [half_shape], "add")[0]
    step = 2
    while step < count:
        after = under.pop(0) if under else [norm_done]
        mine = small(add_kernel, [mine, swap(mine, "ctx", step)], after, [half_shape], "add")[0]
        step *= 2
    other = swap(mine, "ctx", 1)
    step = 1
    if count >= 8:
        ins = [late, *(swap(late, "ctx", k) for k in (1, 2, 3))]
        late = small(add_four_kernel, ins, [norm_done], [late.shape], "add")[0]
        step = 4
    late_other = swap(late, "ctx", step)
    while 2 * step < count:
        late = small(add_kernel, [late, late_other], [norm_done], [late.shape], "add")[0]
        step *= 2
        late_other = swap(late, "ctx", step)
    half_spec = pl.BlockSpec((early_rows * SUB, LANES), lambda h: (h % half, 0))
    late_spec = pos_spec(late_rows)
    grad_short, grad_residues, grad_rate, grad_skip, grad_gain, _ = call(
        functools.partial(finish_kernel, modes, taps, half, early_rows),
        (mine, other, late, late_other, back_done),
        [half_spec, half_spec, late_spec, late_spec, any_spec],
        [
            jax.ShapeDtypeStruct(short_filter.shape, F32),
            jax.ShapeDtypeStruct(residues.shape, F32),
            jax.ShapeDtypeStruct(residues.shape, F32),
            one,
            one,
        ],
        [short_spec, param_spec, param_spec, one_spec, one_spec],
        1,
        "finish",
        scratch=[
            pltpu.VMEM((late_rows * SUB, LANES), F32),
            pltpu.VMEM((early_rows * SUB, LANES), F32),
        ],
    )
    return (
        normed,
        grad_residual,
        grad_query,
        grad_key,
        grad_value,
        grad_short,
        grad_residues,
        grad_rate,
        grad_skip.reshape(channels),
        grad_gain.reshape(channels),
    )


def solution(mesh):
    both, modes, vector = P("ctx", "tp"), P(None, "tp"), P("tp")
    return jax.shard_map(
        shards,
        mesh=mesh,
        in_specs=(both, both, both, both, P(None, None, "tp"), modes, modes, vector, vector, both),
        out_specs=(both,) * 5 + (P(None, None, "tp"), modes, modes, vector, vector),
        check_vma=False,
    )
```

```python
import functools

import jax
import jax.numpy as jnp
from jax import lax
from jax.experimental import pallas as pl
from jax.experimental.pallas import tpu as pltpu
from jax.sharding import PartitionSpec as P

LANES = 128
SUB = 8
CHUNK = 16
WIDE = SUB * LANES
F32 = jnp.float32
BF16 = jnp.bfloat16
VMEM_LIMIT = 10 * 1024 * 1024


def row(ref, t):
    return ref[pl.ds(pl.multiple_of(t * SUB, SUB), SUB), :]


def put(ref, t, value):
    ref[pl.ds(pl.multiple_of(t * SUB, SUB), SUB), :] = value


def loop(start, stop, body, carry):
    fours = (stop - start) // 4

    def four(i, carry):
        for k in range(4):
            carry = body(start + 4 * i + k, carry)
        return carry

    carry = lax.fori_loop(0, fours, four, carry)
    for i in range(start + 4 * fours, stop):
        carry = body(i, carry)
    return carry


def spread_chunk(src, dst, first, c):
    start = pl.multiple_of(c * CHUNK, CHUNK)
    for g in range(SUB):
        piece = src[pl.ds(start, CHUNK), g * LANES : (g + 1) * LANES].astype(F32)
        dst[pl.ds((start + first) * SUB + g, CHUNK, stride=SUB), :] = piece


def gather_chunk(src, dst, c):
    start = pl.multiple_of(c * CHUNK, CHUNK)
    for g in range(SUB):
        piece = src[pl.ds(start * SUB + g, CHUNK, stride=SUB), :]
        dst[pl.ds(start, CHUNK), g * LANES : (g + 1) * LANES] = piece.astype(dst.dtype)


def skewed(chunks, make, lay, make_last=None):
    make(0)

    def some(c, carry):
        lay(c - 1)
        make(c)
        return carry

    lax.fori_loop(1, chunks - 1, some, 0)
    lay(chunks - 2)
    (make_last or make)(chunks - 1)
    lay(chunks - 1)


def total(values):
    values = list(values)
    while len(values) > 1:
        values = [
            values[i] + values[i + 1] if i + 1 < len(values) else values[i]
            for i in range(0, len(values), 2)
        ]
    return values[0]


def taps_of(filt, stream, taps):
    return [row(filt, stream * taps + j) for j in range(taps)]


def conv_at(window, taps, i):
    margin = len(taps) - 1
    return total([taps[j] * window[margin + i - j] for j in range(margin + 1)])


def trailing_kernel(query, key, value, out):
    for i, ref in enumerate((query, key, value)):
        out[i] = ref[...].astype(F32)[SUB:, :].astype(BF16)


def features_kernel(
    modes, taps, steps, key, value, filt3, decay, resid, k_ext, v_ext, f1, f2, u, g, lam, res, faded, filt, x_out
):
    margin = taps - 1
    for s in range(SUB):
        lanes = slice(s * LANES, (s + 1) * LANES)
        lam[pl.ds(s, modes, stride=SUB), :] = decay[:, lanes]
        res[pl.ds(s, modes, stride=SUB), :] = resid[:, lanes]
        for i in range(3):
            filt[pl.ds(i * taps * SUB + s, taps, stride=SUB), :] = filt3[i, :, lanes]
    faded[...] = res[...] * jnp.exp(-lam[...])
    taps1, taps2 = taps_of(filt, 1, taps), taps_of(filt, 2, taps)
    fade, skip = fades(lam, modes, 1), fades(lam, modes, SUB)
    chunks = steps // CHUNK

    def shape(c):
        for src, dst in ((key, k_ext), (value, v_ext)):
            spread_chunk(src, dst, SUB, c)

    def conv(c, skipped=0):
        t0 = c * CHUNK
        kw = [row(k_ext, t0 + SUB - margin + i) for i in range(skipped, CHUNK + margin)]
        vw = [row(v_ext, t0 + SUB - margin + i) for i in range(skipped, CHUNK + margin)]
        for i in range(CHUNK - skipped):
            first, second = conv_at(kw, taps1, i), conv_at(vw, taps2, i)
            put(f1, t0 + skipped + i, first)
            put(f2, t0 + skipped + i, second)
            put(u, t0 + skipped + i, first * second)

    def advance(c, x, skipped=0):
        for b in range(skipped, CHUNK // SUB):
            block = c * (CHUNK // SUB) + b
            now = [row(u, block * SUB + i) for i in range(SUB)]
            new = []
            for m in range(modes):
                own = horner(fade[m], now)
                put(g, block * modes + m, own)
                new.append(own + skip[m] * x[m])
            x = tuple(new)
        return x

    shape(0)
    shape(1)
    conv(0, SUB)
    shape(2)
    conv(1)
    x = advance(0, zeros(modes), 1)

    def some(c, x):
        shape(c + 1)
        conv(c)
        return advance(c - 1, x)

    x = lax.fori_loop(2, chunks - 1, some, x)
    conv(chunks - 1)
    x = advance(chunks - 1, advance(chunks - 2, x))
    for m in range(modes):
        put(x_out, m, x[m])


def zeros(count):
    return tuple(jnp.zeros((SUB, LANES), F32) for _ in range(count))


def fades(lam, modes, span):
    return [jnp.exp(row(lam, m) * -float(span)) for m in range(modes)]


def horner(fade, values):
    result = values[0]
    for value in values[1:]:
        result = fade * result + value
    return result


def head_kernel(
    modes, taps, steps, halo, k_head, v_head, filt, lam, x_part, f1_in, f2_in, u_in, g_in,
    k_ext, v_ext, f1, f2, u, g, x_out,
):
    del f1_in, f2_in, u_in, g_in
    margin = taps - 1
    there = jnp.where(lax.axis_index("ctx") > 0, 1.0, 0.0)
    for s in range(SUB):
        lanes = slice(s * LANES, (s + 1) * LANES)
        k_ext[pl.ds(s, SUB, stride=SUB), :] = halo[1, :, lanes].astype(F32) * there
        v_ext[pl.ds(s, SUB, stride=SUB), :] = halo[2, :, lanes].astype(F32) * there
    taps1, taps2 = taps_of(filt, 1, taps), taps_of(filt, 2, taps)
    kw = [row(k_ext, SUB - margin + i) for i in range(margin)] + [row(k_head, i) for i in range(SUB)]
    vw = [row(v_ext, SUB - margin + i) for i in range(margin)] + [row(v_head, i) for i in range(SUB)]
    mixed = []
    for i in range(SUB):
        first, second = conv_at(kw, taps1, i), conv_at(vw, taps2, i)
        put(f1, i, first)
        put(f2, i, second)
        put(u, i, first * second)
        mixed.append(first * second)
    fade, rest = fades(lam, modes, 1), fades(lam, modes, steps - SUB)
    for m in range(modes):
        own = horner(fade[m], mixed)
        put(g, m, own)
        put(x_out, m, row(x_part, m) + rest[m] * own)


def query_kernel(taps, steps, query, residual, cot, halo, filt, q_ext, f0, res_pos, cot_pos):
    margin = taps - 1
    there = jnp.where(lax.axis_index("ctx") > 0, 1.0, 0.0)
    for s in range(SUB):
        lanes = slice(s * LANES, (s + 1) * LANES)
        q_ext[pl.ds(s, SUB, stride=SUB), :] = halo[0, :, lanes].astype(F32) * there
    taps0, chunks = taps_of(filt, 0, taps), steps // CHUNK

    def conv(c):
        t0 = c * CHUNK
        qw = [row(q_ext, t0 + SUB - margin + i) for i in range(CHUNK + margin)]
        for i in range(CHUNK):
            put(f0, t0 + i, conv_at(qw, taps0, i))

    def shape(c):
        spread_chunk(query, q_ext, SUB, c)
        spread_chunk(residual, res_pos, 0, c)
        spread_chunk(cot, cot_pos, 0, c)

    shape(0)

    def some(c, carry):
        conv(c - 1)
        shape(c)
        return carry

    lax.fori_loop(1, chunks, some, 0)
    conv(chunks - 1)


def near_taps(lam, res, skip, modes):
    fade, weight = fades(lam, modes, 1), [row(res, m) for m in range(modes)]
    result = []
    for k in range(SUB):
        result.append(total(weight) if k else total(weight) + skip[...])
        weight = [f * w for f, w in zip(fade, weight)]
    return result


def near_kernel(modes, steps, u, lam, res, skip, y):
    near = near_taps(lam, res, skip, modes)

    def some(c, carry):
        now = [row(u, c * SUB + i) for i in range(SUB)]
        for i in range(SUB):
            put(y, c * SUB + i, total([near[k] * now[i - k] for k in range(i + 1)]))
        return carry

    loop(0, steps // SUB, some, 0)


def lags_kernel(modes, steps, u, lam, lag):
    fade = fades(lam, modes, 1)

    def some(c, carry):
        now = [row(u, c * SUB + i) * float(SUB - i) for i in range(SUB)]
        for m in range(modes):
            put(lag, c * modes + m, horner(fade[m], now))
        return carry

    loop(0, steps // SUB, some, 0)


def borders_kernel(modes, steps, own_lag, x_at, lam, lag, lag_sum):
    skip = fades(lam, modes, SUB)
    eight = [float(SUB) * v for v in skip]

    def some(c, sums):
        new = []
        for m in range(modes):
            border = row(own_lag, c * modes + m) + eight[m] * row(x_at, c * modes + m)
            put(lag, c * modes + m, border)
            new.append(skip[m] * sums[m] + border)
        return tuple(new)

    sums = loop(0, steps // SUB, some, zeros(modes))
    for m in range(modes):
        put(lag_sum, m, sums[m])


def summed_kernel(modes, steps, blocks, group, y, f0, res_pos, cot_pos, g, before, other, lam, faded, gain, ready, modal, summed, x_at, sums, squares, inner):
    del ready
    block = pl.program_id(0)

    @pl.when(block == 0)
    def _():
        squares[...] = jnp.zeros_like(squares)
        inner[...] = jnp.zeros_like(inner)

    fade, skip = fades(lam, modes, 1), fades(lam, modes, SUB)
    factor = gain[...]
    x_in = exclusive(before[...], other[...], lam[...], steps, group, 1)
    x_in = tuple(x_in[m * SUB : (m + 1) * SUB, :] for m in range(modes))

    def advance(c, x):
        w = [row(faded, m) * x[m] for m in range(modes)]
        for m in range(modes):
            put(x_at, c * modes + m, x[m])
        for i in range(SUB):
            t = c * SUB + i
            if i:
                w = [f * v for f, v in zip(fade, w)]
            long = row(y, t) + total(w)
            put(modal, t, long)
            now = row(res_pos, t) + row(f0, t) * long
            put(summed, t, now)
            put(squares, t, row(squares, t) + now * now)
            put(inner, t, row(inner, t) + factor * row(cot_pos, t) * now)
        return tuple(row(g, c * modes + m) + skip[m] * x[m] for m in range(modes))

    loop(0, steps // SUB, advance, x_in)

    @pl.when(block == blocks - 1)
    def _():
        for which, scratch in enumerate((squares, inner)):
            for b in range(steps // LANES):
                part = total(
                    [
                        scratch[pl.ds(b * LANES * SUB + s, LANES, stride=SUB), :]
                        for s in range(SUB)
                    ]
                )
                sums[which : which + 1, b * LANES : (b + 1) * LANES] = jnp.sum(
                    part.T, axis=0, keepdims=True
                )


def grad_modal_kernel(modes, steps, width, shares, *refs):
    own_sums, (summed, cot_pos, f0, lam, gain, ready) = refs[:shares], refs[shares : shares + 6]
    scale, gm, adj, a_out, a_next = refs[shares + 6 :]
    del ready

    @pl.when(pl.program_id(0) == 0)
    def _():
        sums = total([ref[...] for ref in own_sums])
        inv = lax.rsqrt(sums[0:1, :] / width + 1e-05)
        coef = inv * inv * inv * sums[1:2, :] / width
        for which, value in enumerate((inv, coef)):
            for b in range(steps // LANES):
                piece = value[:, b * LANES : (b + 1) * LANES]
                scale[pl.ds(which * steps + b * LANES, LANES), :] = jnp.broadcast_to(
                    piece, (LANES, LANES)
                ).T

    fade, skip = fades(lam, modes, 1), fades(lam, modes, SUB)
    factor = gain[...]

    def advance(c, a):
        block = steps // SUB - 1 - c
        now = [None] * SUB
        for i in reversed(range(SUB)):
            t = block * SUB + i
            inv = scale[pl.ds(t, 1), :]
            coef = scale[pl.ds(steps + t, 1), :]
            grad = inv * (factor * row(cot_pos, t)) - coef * row(summed, t)
            now[i] = grad * row(f0, t)
            put(gm, t, now[i])
        new = []
        for m in range(modes):
            put(a_next, m, a[m])
            own = horner(fade[m], now[::-1])
            put(adj, block * modes + m, own)
            new.append(own + skip[m] * a[m])
        return tuple(new)

    a = loop(0, steps // SUB, advance, zeros(modes))
    for m in range(modes):
        put(a_out, m, a[m])


def across_kernel(modes, steps, *refs):
    for start in (0, modes // 2):
        across_part(range(start, start + modes // 2), modes, steps, *refs)


def across_part(ms, modes, steps, gm, adj, x_at, lag, lam, res_part, rate_part):
    fade, far = fades(lam, modes, 1), fades(lam, modes, SUB)
    last = steps // SUB - 1

    def across(c, state):
        after, by_res, by_rate = (list(v) for v in state)
        block = last - c
        now = [row(gm, block * SUB + i) * float(i) for i in range(1, SUB)]
        for i, m in enumerate(ms):
            x, own = row(x_at, block * modes + m), row(adj, block * modes + m)
            tail = fade[m] * horner(fade[m], now[::-1])
            by_res[i] = by_res[i] + x * own
            by_rate[i] = by_rate[i] + (x * tail + after[i] * row(lag, block * modes + m))
            after[i] = own + far[m] * after[i]
        return tuple(after), tuple(by_res), tuple(by_rate)

    none = zeros(len(ms))
    _, by_res, by_rate = loop(0, steps // SUB, across, (none, none, none))
    for i, m in enumerate(ms):
        put(res_part, m, fade[m] * by_res[i])
        put(rate_part, m, fade[m] * by_rate[i])


def near_adjoint_kernel(modes, taps, steps, gm, u, lam, res, skip, res_part, rate_part, scale, summed, cot_pos, modal, q_ext, gain, gmy, rate_sum, gf0, early):
    near = near_taps(lam, res, skip, modes)

    def pairs(c, lags):
        now = [row(gm, c * SUB + i) for i in range(SUB)]
        for i in range(SUB):
            put(gmy, c * SUB + i, total([near[k] * now[i + k] for k in range(SUB - i)]))
        before = [row(u, c * SUB + i) for i in range(SUB)]
        return tuple(
            lags[k] + total([now[i] * before[i - k] for i in range(k, SUB)]) for k in range(SUB)
        )

    lags = loop(0, steps // SUB, pairs, zeros(SUB))
    put(early, taps + modes, lags[0])
    fade = fades(lam, modes, 1)
    weighted = [lags[k] * float(k) for k in range(1, SUB)]
    for m in range(modes):
        put(early, taps + m, row(res_part, m) + horner(fade[m], lags[::-1]))
        put(rate_sum, m, row(rate_part, m) + fade[m] * horner(fade[m], weighted[::-1]))
    query_sums(modes, taps, steps, scale, summed, cot_pos, modal, q_ext, gain, gf0, early)


def norm_kernel(taps, steps, last, scale, summed, cot_pos, gain, gf0, next_head, filt, ready, normed, grad_res, grad_query, work, head, work2):
    del ready
    back(0, taps, steps, last, gf0, next_head, filt, grad_query, work, head)
    factor = gain[...]

    def make(c):
        for i in range(CHUNK):
            t = c * CHUNK + i
            inv, now = scale[pl.ds(t, 1), :], row(summed, t)
            put(work, t, now * inv * factor)
            put(work2, t, inv * (factor * row(cot_pos, t)) - scale[pl.ds(steps + t, 1), :] * now)

    def lay(c):
        gather_chunk(work, normed, c)
        gather_chunk(work2, grad_res, c)

    skewed(steps // CHUNK, make, lay)


def query_sums(modes, taps, steps, scale, summed, cot_pos, modal, q_ext, gain, gf0, early):
    factor = gain[...]

    margin = taps - 1

    def grads(c, sums):
        by_gain, acc = sums
        window = [row(q_ext, c * SUB + SUB - margin + i) for i in range(SUB + margin)]
        for i in range(SUB):
            t = c * SUB + i
            now, here = row(cot_pos, t), row(summed, t)
            scaled = scale[pl.ds(t, 1), :] * now
            grad = factor * scaled - scale[pl.ds(steps + t, 1), :] * here
            front = grad * row(modal, t)
            put(gf0, t, front)
            by_gain = by_gain + scaled * here
            acc = tuple(acc[j] + front * window[margin + i - j] for j in range(taps))
        return by_gain, acc

    by_gain, acc = loop(0, steps // SUB, grads, (zeros(1)[0], zeros(taps)))
    put(early, taps + modes + 1, by_gain)
    for j in range(taps):
        put(early, j, acc[j])


def filter_pass(taps, steps, grad, ext):
    margin = taps - 1

    def some(c, acc):
        t0 = c * SUB
        window = [row(ext, t0 + SUB - margin + i) for i in range(SUB + margin)]
        for i in range(SUB):
            now = row(grad, t0 + i)
            acc = tuple(acc[j] + now * window[margin + i - j] for j in range(taps))
        return acc

    zero = jnp.zeros((SUB, LANES), F32)
    return loop(0, steps // SUB, some, tuple(zero for _ in range(taps)))


def mixed_kernel(modes, steps, gmy, f1, f2, adj, lam, faded, alpha, gf1, gf2):
    fade, skip = fades(lam, modes, 1), fades(lam, modes, SUB)

    def advance(c, after):
        block = steps // SUB - 1 - c
        w = [row(faded, m) * after[m] for m in range(modes)]
        for i in reversed(range(SUB)):
            t = block * SUB + i
            grad = row(gmy, t) + total(w)
            put(gf1, t, grad * row(f2, t))
            put(gf2, t, grad * row(f1, t))
            w = [f * v for f, v in zip(fade, w)]
        return tuple(row(adj, block * modes + m) + skip[m] * after[m] for m in range(modes))

    loop(0, steps // SUB, advance, tuple(row(alpha, m) for m in range(modes)))


def filter_sums_kernel(taps, steps, gf1, gf2, k_ext, v_ext, sums):
    for which, (grad, ext) in enumerate(((gf1, k_ext), (gf2, v_ext))):
        parts = filter_pass(taps, steps, grad, ext)
        for j in range(taps):
            put(sums, which * taps + j, parts[j])


def back_kernel(taps, steps, last, gf1, gf2, next_head, filt, grad_key, grad_value, work, head):
    back(1, taps, steps, last, gf1, next_head, filt, grad_key, work, head)
    back(2, taps, steps, last, gf2, next_head, filt, grad_value, work, head)


def back(which, taps, steps, last, grad, next_head, filt, out, work, head):
    there = jnp.where(lax.axis_index("ctx") < last, 1.0, 0.0)
    head[...] = next_head[which, 0].astype(F32) * there
    weights = taps_of(filt, which, taps)

    def make(c):
        window = [row(grad, c * CHUNK + i) for i in range(CHUNK + taps - 1)]
        put_back(work, c * CHUNK, weights, window)

    def make_last(c):
        window = [row(grad, c * CHUNK + i) for i in range(CHUNK)]
        put_back(work, c * CHUNK, weights, window + [row(head, i) for i in range(taps - 1)])

    skewed(steps // CHUNK, make, lambda c: gather_chunk(work, out, c), make_last)


def put_back(out, start, weights, window):
    for i in range(CHUNK):
        put(out, start + i, total([w * window[i + j] for j, w in enumerate(weights)]))


def place(group, sign):
    at = lax.axis_index("ctx")
    if sign < 0:
        at = lax.axis_size("ctx") - 1 - at
    later = (at // group) % 2
    return (at % group).astype(F32), later.astype(F32)


def exclusive(before, other, lam, span, group, sign):
    at, later = place(group, sign)
    here = later * jnp.exp(lam * (at * -float(span))) * other
    return here if before is None else before + here


def inclusive(own, other, lam, span, group, sign):
    _, later = place(group, sign)
    fall = -float(span * group)
    return jnp.exp(lam * ((1.0 - later) * fall)) * own + jnp.exp(lam * (later * fall)) * other


def join_kernel(span, group, sign, first, own, other, lam, *refs):
    before, ends = (None, refs[-2:]) if first else (refs[0][...], refs[-2:])
    ends[0][...] = exclusive(before, other[...], lam[...], span, group, sign)
    ends[1][...] = inclusive(own[...], other[...], lam[...], span, group, sign)


def join_four_kernel(span, sign, own, first, second, third, lam, *refs):
    before, end = refs[-2:]
    at, _ = place(4, sign)
    here = lax.axis_index("ctx") if sign > 0 else lax.axis_size("ctx") - 1 - lax.axis_index("ctx")
    here, rates = here % 4, lam[...]
    total_end = jnp.exp(rates * ((3.0 - at) * -float(span))) * own[...]
    total_before = None
    for k, other in enumerate((first, second, third)):
        there = (here ^ (k + 1)).astype(F32)
        earlier = jnp.where(there < at, 1.0, 0.0)
        gap = jnp.maximum(at - 1.0 - there, 0.0)
        value = other[...]
        share = earlier * jnp.exp(rates * (gap * -float(span))) * value
        total_before = share if total_before is None else total_before + share
        total_end = total_end + jnp.exp(rates * ((3.0 - there) * -float(span))) * value
    before[...] = total_before
    end[...] = total_end


def add_four_kernel(own, first, second, third, *refs):
    refs[-1][...] = (own[...] + first[...]) + (second[...] + third[...])


def add_kernel(one, other, *refs):
    refs[-1][...] = one[...] + other[...]


def pack_kernel(span, group, modes, first_rows, half, before, other, lam, early, res, rate_sum, lag_sum, faded, a_next, gmy, f1, f2, gf0, alpha, kept, sent, heads):
    alpha[...] = exclusive(before[...], other[...], lam[...], span, group, -1)
    odd = lax.axis_index("ctx") % 2
    rows = (first_rows + modes) * SUB
    for out, start in ((kept, odd * half), (sent, (1 - odd) * half)):
        for b in range(half):
            source = pl.multiple_of((start + b) * (first_rows * SUB), SUB)
            out[pl.ds(b * rows, first_rows * SUB), :] = early[pl.ds(source, first_rows * SUB), :]
            source = pl.multiple_of((start + b) * (modes * SUB), SUB)
            mine = pl.ds(source, modes * SUB)
            lagged = rate_sum[mine, :] + jnp.exp(-lam[mine, :]) * alpha[mine, :] * lag_sum[mine, :]
            out[pl.ds(b * rows + first_rows * SUB, modes * SUB), :] = -res[mine, :] * lagged
    for b in range(2 * half):
        mine = slice(b * modes * SUB, (b + 1) * modes * SUB)
        far = jnp.exp(lam[mine, :] * -float(span - SUB))
        w, fade = faded[mine, :] * (a_next[mine, :] + far * alpha[mine, :]), jnp.exp(-lam[mine, :])
        here, grads = slice(b * span * SUB, (b * span + SUB) * SUB), []
        for t in range(SUB):
            grads.append(total([w[m * SUB : (m + 1) * SUB, :] for m in range(modes)]))
            w = fade * w
        grad = gmy[here, :] + jnp.concatenate(grads[::-1], axis=0)
        for which, value in enumerate((gf0[here, :], grad * f2[here, :], grad * f1[here, :])):
            heads[which, b] = value.astype(BF16)


def finish_kernel(modes, taps, half, early_rows, mine, other, late_mine, late_other, ready, short, res, rate, skip, gain, late, early):
    del ready
    block = pl.program_id(0)
    late[...] = late_mine[...] + late_other[...]
    own = jnp.where(lax.axis_index("ctx") % 2 == block // half, 1.0, 0.0)
    early[...] = own * mine[...] + (1.0 - own) * other[...]
    for s in range(SUB):
        lanes = slice(s * LANES, (s + 1) * LANES)
        short[0, :, lanes] = early[pl.ds(s, taps, stride=SUB), :]
        short[1, :, lanes] = late[pl.ds(s, taps, stride=SUB), :]
        short[2, :, lanes] = late[pl.ds(taps * SUB + s, taps, stride=SUB), :]
        res[:, lanes] = early[pl.ds(taps * SUB + s, modes, stride=SUB), :]
        rate[:, lanes] = early[pl.ds((taps + modes + 2) * SUB + s, modes, stride=SUB), :]
    skip[...] = row(early, taps + modes)
    gain[...] = row(early, taps + modes + 1)


def ring(value, axis, distance):
    count = lax.axis_size(axis)
    return lax.ppermute(value, axis, [(i, (i + distance) % count) for i in range(count)])


def swap(value, axis, step):
    return lax.ppermute(value, axis, [(i, i ^ step) for i in range(lax.axis_size(axis))])


def small(body, ins, after, outs, name):
    near = pl.BlockSpec(memory_space=pltpu.VMEM)
    ins = [pltpu.with_memory_space_constraint(v, pltpu.VMEM) if v.size > 1 << 18 else v for v in ins]
    return pl.pallas_call(
        body,
        in_specs=[near] * len(ins) + [pl.BlockSpec(memory_space=pl.ANY)] * len(after),
        out_specs=[near] * len(outs),
        out_shape=[jax.ShapeDtypeStruct(shape, BF16 if len(shape) > 2 else F32) for shape in outs],
        compiler_params=pltpu.CompilerParams(vmem_limit_bytes=VMEM_LIMIT),
        cost_estimate=pl.CostEstimate(flops=ins[0].size, bytes_accessed=0, transcendentals=0),
        name=name,
    )(*ins, *after)


def scan_but_last(own, lam, span, sign, under):
    count, group, before = lax.axis_size("ctx"), 1, None
    under = list(under)
    if count >= 8:
        ins = [own, *(swap(own, "ctx", k) for k in (1, 2, 3)), lam]
        body = functools.partial(join_four_kernel, span, sign)
        before, own = small(body, ins, under, [own.shape] * 2, "join")
        group, under = 4, []
    while True:
        other = swap(own, "ctx", group)
        if 2 * group >= count:
            return before, other, group
        body = functools.partial(join_kernel, span, group, sign, before is None)
        ins = [own, other, lam] + ([] if before is None else [before])
        after = [under.pop(0)] if under else []
        before, own = small(body, ins, after, [own.shape] * 2, "join")
        group *= 2


def shards(
    residual, query_in, key_in, value_in, short_filter, residues, decay_rate, skip_gain, norm_gain, cotangent
):
    steps, channels = residual.shape
    modes, taps = residues.shape[0], short_filter.shape[1]
    blocks = channels // WIDE
    width = channels * lax.axis_size("tp")
    skip, gain = (v.reshape(blocks * SUB, LANES) for v in (skip_gain, norm_gain))

    def pos(count):
        return jax.ShapeDtypeStruct((blocks * count * SUB, LANES), F32)

    def kept(count):
        return pltpu.VMEM((blocks * count * SUB, LANES), F32)

    def pos_spec(count):
        return pl.BlockSpec((count * SUB, LANES), lambda h: (h, 0))

    def head_spec(total_steps, start):
        return pl.BlockSpec((SUB * SUB, LANES), lambda h: (h * (total_steps // SUB) + start, 0))

    wide_spec = pl.BlockSpec((steps, WIDE), lambda h: (0, h))
    wide = jax.ShapeDtypeStruct((steps, channels), BF16)
    mode_spec, one_spec, filt_spec = pos_spec(modes), pos_spec(1), pos_spec(3 * taps)
    seq_spec, ext_spec = pos_spec(steps), pos_spec(steps + SUB)
    seq, ext, mode, one = kept(steps), kept(steps + SUB), pos(modes), pos(1)
    eights, eights_spec = kept(steps // SUB * modes), pos_spec(steps // SUB * modes)
    halo_spec = pl.BlockSpec((3, SUB, WIDE), lambda h: (0, 0, h))
    param_spec = pl.BlockSpec((modes, WIDE), lambda h: (0, h))
    short_spec = pl.BlockSpec((3, taps, WIDE), lambda h: (0, 0, h))

    def call(body, ins, in_specs, outs, out_specs, ops, name, scratch=(), aliases=None):
        elements, n_refs = steps * channels, len(ins) + len(outs)

        def with_done(*refs):
            done = refs[n_refs]
            done[...] = jnp.zeros_like(done)
            body(*refs[:n_refs], *refs[n_refs + 1 :])

        near = blocks * steps * SUB
        ins = [
            pltpu.with_memory_space_constraint(v, pltpu.VMEM) if v.shape[0] >= near and v.dtype == F32 else v
            for v in ins
        ]
        done_shape = (SUB, LANES)
        outs = [*outs, jax.ShapeDtypeStruct(done_shape, F32)]
        out_specs = [*out_specs, pl.BlockSpec(done_shape, lambda h: (0, 0))]
        return pl.pallas_call(
            with_done,
            grid=(blocks,),
            in_specs=in_specs,
            out_specs=out_specs,
            out_shape=outs,
            scratch_shapes=list(scratch),
            input_output_aliases=aliases or {},
            compiler_params=pltpu.CompilerParams(
                dimension_semantics=("arbitrary",), vmem_limit_bytes=VMEM_LIMIT
            ),
            cost_estimate=pl.CostEstimate(
                flops=ops * elements, bytes_accessed=4 * elements, transcendentals=0
            ),
            name=name,
        )(*ins)

    far = [
        pltpu.with_memory_space_constraint(v, pltpu.HBM)
        for v in (residual, query_in, key_in, value_in, cotangent, short_filter, decay_rate, residues)
    ]
    last_spec = pl.BlockSpec((2 * SUB, channels), lambda h: (steps // (2 * SUB) - 1, 0))
    trailing = pl.pallas_call(
        trailing_kernel,
        grid=(1,),
        in_specs=[last_spec] * 3,
        out_specs=pl.BlockSpec((3, SUB, channels), lambda h: (0, 0, 0)),
        out_shape=jax.ShapeDtypeStruct((3, SUB, channels), BF16),
        compiler_params=pltpu.CompilerParams(vmem_limit_bytes=VMEM_LIMIT),
        cost_estimate=pl.CostEstimate(flops=channels, bytes_accessed=channels, transcendentals=0),
        name="trailing",
    )(*far[1:4])
    halo = ring(trailing, "ctx", 1)

    k_ext, v_ext, f1, f2, u, g, lam, res, faded, filt, x_part, _ = call(
        functools.partial(features_kernel, modes, taps, steps),
        (far[2], far[3], *far[5:]),
        [wide_spec, wide_spec, short_spec, param_spec, param_spec],
        [ext, ext, seq, seq, seq, eights, mode, mode, mode, pos(3 * taps), mode],
        [ext_spec, ext_spec, seq_spec, seq_spec, seq_spec, eights_spec, mode_spec, mode_spec, mode_spec, filt_spec, mode_spec],
        64,
        "features",
    )
    any_spec = pl.BlockSpec(memory_space=pl.ANY)
    k_ext, v_ext, f1, f2, u, g, x_own, _ = call(
        functools.partial(head_kernel, modes, taps, steps),
        (halo, k_ext, v_ext, filt, lam, x_part, f1, f2, u, g),
        [halo_spec, head_spec(steps + SUB, 1), head_spec(steps + SUB, 1), filt_spec, mode_spec, mode_spec]
        + [any_spec] * 4,
        [ext, ext, seq, seq, seq, eights, mode],
        [head_spec(steps + SUB, 0)] * 2
        + [head_spec(steps, 0)] * 3
        + [pl.BlockSpec((modes * SUB, LANES), lambda h: (h * (steps // SUB), 0)), mode_spec],
        2,
        "head",
        aliases={1: 0, 2: 1, 6: 2, 7: 3, 8: 4, 9: 5},
    )
    q_ext, f0, res_pos, cot_pos, query_done = call(
        functools.partial(query_kernel, taps, steps),
        (far[1], far[0], far[4], halo, filt),
        [wide_spec, wide_spec, wide_spec, halo_spec, filt_spec],
        [ext, seq, seq, seq],
        [ext_spec, seq_spec, seq_spec, seq_spec],
        30,
        "query",
    )
    y, _ = call(
        functools.partial(near_kernel, modes, steps),
        (u, lam, res, skip),
        [seq_spec, mode_spec, mode_spec, one_spec],
        [seq],
        [seq_spec],
        10,
        "near",
    )
    own_lag, own_lag_done = call(
        functools.partial(lags_kernel, modes, steps),
        (u, lam),
        [seq_spec, mode_spec],
        [eights],
        [eights_spec],
        32,
        "lags",
    )
    before, other, group = scan_but_last(x_own, lam, steps, 1, [query_done])
    modal, summed, x_at, sums, _ = call(
        functools.partial(summed_kernel, modes, steps, blocks, group),
        (y, f0, res_pos, cot_pos, g, before, other, lam, faded, gain, own_lag_done),
        [seq_spec] * 4 + [eights_spec] + [mode_spec] * 4 + [one_spec, any_spec],
        [seq, seq, eights, jax.ShapeDtypeStruct((2, steps), F32)],
        [seq_spec, seq_spec, eights_spec, pl.BlockSpec((2, steps), lambda h: (0, 0))],
        50,
        "summed",
        scratch=[pltpu.VMEM((steps * SUB, LANES), F32)] * 2,
    )
    all_sums = [sums, *(swap(sums, "tp", k) for k in range(1, lax.axis_size("tp")))]
    lag, lag_sum, lags_done = call(
        functools.partial(borders_kernel, modes, steps),
        (own_lag, x_at, lam),
        [eights_spec, eights_spec, mode_spec],
        [eights, mode],
        [eights_spec, mode_spec],
        8,
        "borders",
    )
    scale_spec = pl.BlockSpec((2 * steps, LANES), lambda h: (0, 0))
    scale, gm, adj, a_own, a_next, _ = call(
        functools.partial(grad_modal_kernel, modes, steps, width, len(all_sums)),
        (*all_sums, summed, cot_pos, f0, lam, gain, lags_done),
        [pl.BlockSpec((2, steps), lambda h: (0, 0))] * len(all_sums)
        + [seq_spec, seq_spec, seq_spec, mode_spec, one_spec, any_spec],
        [pltpu.VMEM((2 * steps, LANES), F32), seq, eights, mode, mode],
        [scale_spec, seq_spec, eights_spec, mode_spec, mode_spec],
        45,
        "grad_modal",
    )
    res_part, rate_part, across_done = call(
        functools.partial(across_kernel, modes, steps),
        (gm, adj, x_at, lag, lam),
        [seq_spec, eights_spec, eights_spec, eights_spec, mode_spec],
        [mode, mode],
        [mode_spec, mode_spec],
        50,
        "across",
    )
    early_rows = taps + modes + 2
    gmy, rate_sum, gf0, early, _ = call(
        functools.partial(near_adjoint_kernel, modes, taps, steps),
        (gm, u, lam, res, skip, res_part, rate_part, scale, summed, cot_pos, modal, q_ext, gain),
        [seq_spec, seq_spec, mode_spec, mode_spec, one_spec, mode_spec, mode_spec, scale_spec, seq_spec, seq_spec, seq_spec, ext_spec, one_spec],
        [seq, mode, seq, pos(early_rows)],
        [seq_spec, mode_spec, seq_spec, pos_spec(early_rows)],
        55,
        "near_adjoint",
    )
    before, other, group = scan_but_last(a_own, lam, steps, -1, [across_done])

    half = blocks // 2
    half_shape = (half * (early_rows + modes) * SUB, LANES)
    alpha, kept_half, sent_half, heads = small(
        functools.partial(pack_kernel, steps, group, modes, early_rows, half),
        [before, other, lam, early, res, rate_sum, lag_sum, faded, a_next, gmy, f1, f2, gf0],
        [],
        [lam.shape, half_shape, half_shape, (3, blocks, SUB * SUB, LANES)],
        "pack",
    )
    early_rows += modes
    late_rows = 2 * taps
    next_spec = pl.BlockSpec((3, 1, SUB * SUB, LANES), lambda h: (0, h, 0, 0))
    other_half = swap(sent_half, "ctx", 1)
    next_head = ring(heads, "ctx", -1)
    gf1, gf2, mixed_done = call(
        functools.partial(mixed_kernel, modes, steps),
        (gmy, f1, f2, adj, lam, faded, alpha),
        [seq_spec] * 3 + [eights_spec] + [mode_spec] * 3,
        [seq, seq],
        [seq_spec, seq_spec],
        45,
        "mixed",
    )
    late, late_done = call(
        functools.partial(filter_sums_kernel, taps, steps),
        (gf1, gf2, k_ext, v_ext),
        [seq_spec, seq_spec, ext_spec, ext_spec],
        [pos(late_rows)],
        [pos_spec(late_rows)],
        30,
        "filter_sums",
    )

    last = lax.axis_size("ctx") - 1
    back_scratch = [pltpu.VMEM((steps * SUB, LANES), F32), pltpu.VMEM((SUB * SUB, LANES), F32)]
    normed, grad_residual, grad_query, norm_done = call(
        functools.partial(norm_kernel, taps, steps, last),
        (scale, summed, cot_pos, gain, gf0, next_head, filt, late_done),
        [scale_spec, seq_spec, seq_spec, one_spec, seq_spec, next_spec, filt_spec, any_spec],
        [wide, wide, wide],
        [wide_spec, wide_spec, wide_spec],
        45,
        "norm",
        scratch=[*back_scratch, pltpu.VMEM((steps * SUB, LANES), F32)],
    )
    grad_key, grad_value, back_done = call(
        functools.partial(back_kernel, taps, steps, last),
        (gf1, gf2, next_head, filt),
        [seq_spec, seq_spec, next_spec, filt_spec],
        [wide, wide],
        [wide_spec, wide_spec],
        40,
        "back",
        scratch=back_scratch,
    )
    count, under = lax.axis_size("ctx"), [[late_done], [norm_done]]
    mine = small(add_kernel, [kept_half, other_half], [mixed_done, next_head], [half_shape], "add")[0]
    step = 2
    while step < count:
        after = under.pop(0) if under else [norm_done]
        mine = small(add_kernel, [mine, swap(mine, "ctx", step)], after, [half_shape], "add")[0]
        step *= 2
    other = swap(mine, "ctx", 1)
    step = 1
    if count >= 8:
        ins = [late, *(swap(late, "ctx", k) for k in (1, 2, 3))]
        late = small(add_four_kernel, ins, [norm_done], [late.shape], "add")[0]
        step = 4
    late_other = swap(late, "ctx", step)
    while 2 * step < count:
        late = small(add_kernel, [late, late_other], [norm_done], [late.shape], "add")[0]
        step *= 2
        late_other = swap(late, "ctx", step)
    half_spec = pl.BlockSpec((early_rows * SUB, LANES), lambda h: (h % half, 0))
    late_spec = pos_spec(late_rows)
    grad_short, grad_residues, grad_rate, grad_skip, grad_gain, _ = call(
        functools.partial(finish_kernel, modes, taps, half, early_rows),
        (mine, other, late, late_other, back_done),
        [half_spec, half_spec, late_spec, late_spec, any_spec],
        [
            jax.ShapeDtypeStruct(short_filter.shape, F32),
            jax.ShapeDtypeStruct(residues.shape, F32),
            jax.ShapeDtypeStruct(residues.shape, F32),
            one,
            one,
        ],
        [short_spec, param_spec, param_spec, one_spec, one_spec],
        1,
        "finish",
        scratch=[
            pltpu.VMEM((late_rows * SUB, LANES), F32),
            pltpu.VMEM((early_rows * SUB, LANES), F32),
        ],
    )
    return (
        normed,
        grad_residual,
        grad_query,
        grad_key,
        grad_value,
        grad_short,
        grad_residues,
        grad_rate,
        grad_skip.reshape(channels),
        grad_gain.reshape(channels),
    )


def solution(mesh):
    both, modes, vector = P("ctx", "tp"), P(None, "tp"), P("tp")
    return jax.shard_map(
        shards,
        mesh=mesh,
        in_specs=(both, both, both, both, P(None, None, "tp"), modes, modes, vector, vector, both),
        out_specs=(both,) * 5 + (P(None, None, "tp"), modes, modes, vector, vector),
        check_vma=False,
    )
```

```python
import functools

import jax
import jax.numpy as jnp
from jax import lax
from jax.experimental import pallas as pl
from jax.experimental.pallas import tpu as pltpu
from jax.sharding import PartitionSpec as P

LANES = 128
SUB = 8
CHUNK = 16
WIDE = SUB * LANES
F32 = jnp.float32
BF16 = jnp.bfloat16
VMEM_LIMIT = 10 * 1024 * 1024


def row(ref, t):
    return ref[pl.ds(pl.multiple_of(t * SUB, SUB), SUB), :]


def put(ref, t, value):
    ref[pl.ds(pl.multiple_of(t * SUB, SUB), SUB), :] = value


def loop(start, stop, body, carry):
    fours = (stop - start) // 4

    def four(i, carry):
        for k in range(4):
            carry = body(start + 4 * i + k, carry)
        return carry

    carry = lax.fori_loop(0, fours, four, carry)
    for i in range(start + 4 * fours, stop):
        carry = body(i, carry)
    return carry


def spread_chunk(src, dst, first, c):
    start = pl.multiple_of(c * CHUNK, CHUNK)
    for g in range(SUB):
        piece = src[pl.ds(start, CHUNK), g * LANES : (g + 1) * LANES].astype(F32)
        dst[pl.ds((start + first) * SUB + g, CHUNK, stride=SUB), :] = piece


def gather_chunk(src, dst, c):
    start = pl.multiple_of(c * CHUNK, CHUNK)
    for g in range(SUB):
        piece = src[pl.ds(start * SUB + g, CHUNK, stride=SUB), :]
        dst[pl.ds(start, CHUNK), g * LANES : (g + 1) * LANES] = piece.astype(dst.dtype)


def skewed(chunks, make, lay, make_last=None):
    make(0)

    def some(c, carry):
        lay(c - 1)
        make(c)
        return carry

    lax.fori_loop(1, chunks - 1, some, 0)
    lay(chunks - 2)
    (make_last or make)(chunks - 1)
    lay(chunks - 1)


def total(values):
    values = list(values)
    while len(values) > 1:
        values = [
            values[i] + values[i + 1] if i + 1 < len(values) else values[i]
            for i in range(0, len(values), 2)
        ]
    return values[0]


def taps_of(filt, stream, taps):
    return [row(filt, stream * taps + j) for j in range(taps)]


def conv_at(window, taps, i):
    margin = len(taps) - 1
    return total([taps[j] * window[margin + i - j] for j in range(margin + 1)])


def trailing_kernel(query, key, value, out):
    for i, ref in enumerate((query, key, value)):
        out[i] = ref[...].astype(F32)[SUB:, :].astype(BF16)


def features_kernel(
    modes, taps, steps, key, value, filt3, decay, resid, k_ext, v_ext, f1, f2, u, g, lam, res, faded, filt, x_out
):
    margin = taps - 1
    for s in range(SUB):
        lanes = slice(s * LANES, (s + 1) * LANES)
        lam[pl.ds(s, modes, stride=SUB), :] = decay[:, lanes]
        res[pl.ds(s, modes, stride=SUB), :] = resid[:, lanes]
        for i in range(3):
            filt[pl.ds(i * taps * SUB + s, taps, stride=SUB), :] = filt3[i, :, lanes]
    faded[...] = res[...] * jnp.exp(-lam[...])
    taps1, taps2 = taps_of(filt, 1, taps), taps_of(filt, 2, taps)
    fade, skip = fades(lam, modes, 1), fades(lam, modes, SUB)
    chunks = steps // CHUNK

    def shape(c):
        for src, dst in ((key, k_ext), (value, v_ext)):
            spread_chunk(src, dst, SUB, c)

    def conv(c, skipped=0):
        t0 = c * CHUNK
        kw = [row(k_ext, t0 + SUB - margin + i) for i in range(skipped, CHUNK + margin)]
        vw = [row(v_ext, t0 + SUB - margin + i) for i in range(skipped, CHUNK + margin)]
        for i in range(CHUNK - skipped):
            first, second = conv_at(kw, taps1, i), conv_at(vw, taps2, i)
            put(f1, t0 + skipped + i, first)
            put(f2, t0 + skipped + i, second)
            put(u, t0 + skipped + i, first * second)

    def advance(c, x, skipped=0):
        for b in range(skipped, CHUNK // SUB):
            block = c * (CHUNK // SUB) + b
            now = [row(u, block * SUB + i) for i in range(SUB)]
            new = []
            for m in range(modes):
                own = horner(fade[m], now)
                put(g, block * modes + m, own)
                new.append(own + skip[m] * x[m])
            x = tuple(new)
        return x

    shape(0)
    shape(1)
    conv(0, SUB)
    shape(2)
    conv(1)
    x = advance(0, zeros(modes), 1)

    def some(c, x):
        shape(c + 1)
        conv(c)
        return advance(c - 1, x)

    x = lax.fori_loop(2, chunks - 1, some, x)
    conv(chunks - 1)
    x = advance(chunks - 1, advance(chunks - 2, x))
    for m in range(modes):
        put(x_out, m, x[m])


def zeros(count):
    return tuple(jnp.zeros((SUB, LANES), F32) for _ in range(count))


def fades(lam, modes, span):
    return [jnp.exp(row(lam, m) * -float(span)) for m in range(modes)]


def horner(fade, values):
    result = values[0]
    for value in values[1:]:
        result = fade * result + value
    return result


def head_kernel(
    modes, taps, steps, halo, k_head, v_head, filt, lam, x_part, f1_in, f2_in, u_in, g_in,
    k_ext, v_ext, f1, f2, u, g, x_out,
):
    del f1_in, f2_in, u_in, g_in
    margin = taps - 1
    there = jnp.where(lax.axis_index("ctx") > 0, 1.0, 0.0)
    for s in range(SUB):
        lanes = slice(s * LANES, (s + 1) * LANES)
        k_ext[pl.ds(s, SUB, stride=SUB), :] = halo[1, :, lanes].astype(F32) * there
        v_ext[pl.ds(s, SUB, stride=SUB), :] = halo[2, :, lanes].astype(F32) * there
    taps1, taps2 = taps_of(filt, 1, taps), taps_of(filt, 2, taps)
    kw = [row(k_ext, SUB - margin + i) for i in range(margin)] + [row(k_head, i) for i in range(SUB)]
    vw = [row(v_ext, SUB - margin + i) for i in range(margin)] + [row(v_head, i) for i in range(SUB)]
    mixed = []
    for i in range(SUB):
        first, second = conv_at(kw, taps1, i), conv_at(vw, taps2, i)
        put(f1, i, first)
        put(f2, i, second)
        put(u, i, first * second)
        mixed.append(first * second)
    fade, rest = fades(lam, modes, 1), fades(lam, modes, steps - SUB)
    for m in range(modes):
        own = horner(fade[m], mixed)
        put(g, m, own)
        put(x_out, m, row(x_part, m) + rest[m] * own)


def query_kernel(taps, steps, query, residual, cot, halo, filt, q_ext, f0, res_pos, cot_pos):
    margin = taps - 1
    there = jnp.where(lax.axis_index("ctx") > 0, 1.0, 0.0)
    for s in range(SUB):
        lanes = slice(s * LANES, (s + 1) * LANES)
        q_ext[pl.ds(s, SUB, stride=SUB), :] = halo[0, :, lanes].astype(F32) * there
    taps0, chunks = taps_of(filt, 0, taps), steps // CHUNK

    def conv(c):
        t0 = c * CHUNK
        qw = [row(q_ext, t0 + SUB - margin + i) for i in range(CHUNK + margin)]
        for i in range(CHUNK):
            put(f0, t0 + i, conv_at(qw, taps0, i))

    def shape(c):
        spread_chunk(query, q_ext, SUB, c)
        spread_chunk(residual, res_pos, 0, c)
        spread_chunk(cot, cot_pos, 0, c)

    shape(0)

    def some(c, carry):
        conv(c - 1)
        shape(c)
        return carry

    lax.fori_loop(1, chunks, some, 0)
    conv(chunks - 1)


def near_taps(lam, res, skip, modes):
    fade, weight = fades(lam, modes, 1), [row(res, m) for m in range(modes)]
    result = []
    for k in range(SUB):
        result.append(total(weight) if k else total(weight) + skip[...])
        weight = [f * w for f, w in zip(fade, weight)]
    return result


def near_kernel(modes, steps, u, lam, res, skip, y):
    near = near_taps(lam, res, skip, modes)

    def some(c, carry):
        now = [row(u, c * SUB + i) for i in range(SUB)]
        for i in range(SUB):
            put(y, c * SUB + i, total([near[k] * now[i - k] for k in range(i + 1)]))
        return carry

    loop(0, steps // SUB, some, 0)


def lags_kernel(modes, steps, u, lam, lag):
    fade = fades(lam, modes, 1)

    def some(c, carry):
        now = [row(u, c * SUB + i) * float(SUB - i) for i in range(SUB)]
        for m in range(modes):
            put(lag, c * modes + m, horner(fade[m], now))
        return carry

    loop(0, steps // SUB, some, 0)


def borders_kernel(modes, steps, own_lag, x_at, lam, lag, lag_sum):
    skip = fades(lam, modes, SUB)
    eight = [float(SUB) * v for v in skip]

    def some(c, sums):
        new = []
        for m in range(modes):
            border = row(own_lag, c * modes + m) + eight[m] * row(x_at, c * modes + m)
            put(lag, c * modes + m, border)
            new.append(skip[m] * sums[m] + border)
        return tuple(new)

    sums = loop(0, steps // SUB, some, zeros(modes))
    for m in range(modes):
        put(lag_sum, m, sums[m])


def summed_kernel(modes, steps, blocks, group, y, f0, res_pos, cot_pos, g, before, other, lam, faded, gain, ready, modal, summed, x_at, sums, squares, inner):
    del ready
    block = pl.program_id(0)

    @pl.when(block == 0)
    def _():
        squares[...] = jnp.zeros_like(squares)
        inner[...] = jnp.zeros_like(inner)

    fade, skip = fades(lam, modes, 1), fades(lam, modes, SUB)
    factor = gain[...]
    x_in = exclusive(before[...], other[...], lam[...], steps, group, 1)
    x_in = tuple(x_in[m * SUB : (m + 1) * SUB, :] for m in range(modes))

    def advance(c, x):
        w = [row(faded, m) * x[m] for m in range(modes)]
        for m in range(modes):
            put(x_at, c * modes + m, x[m])
        for i in range(SUB):
            t = c * SUB + i
            if i:
                w = [f * v for f, v in zip(fade, w)]
            long = row(y, t) + total(w)
            put(modal, t, long)
            now = row(res_pos, t) + row(f0, t) * long
            put(summed, t, now)
            put(squares, t, row(squares, t) + now * now)
            put(inner, t, row(inner, t) + factor * row(cot_pos, t) * now)
        return tuple(row(g, c * modes + m) + skip[m] * x[m] for m in range(modes))

    loop(0, steps // SUB, advance, x_in)

    @pl.when(block == blocks - 1)
    def _():
        for which, scratch in enumerate((squares, inner)):
            for b in range(steps // LANES):
                part = total(
                    [
                        scratch[pl.ds(b * LANES * SUB + s, LANES, stride=SUB), :]
                        for s in range(SUB)
                    ]
                )
                sums[which : which + 1, b * LANES : (b + 1) * LANES] = jnp.sum(
                    part.T, axis=0, keepdims=True
                )


def grad_modal_kernel(modes, steps, width, shares, *refs):
    own_sums, (summed, cot_pos, f0, lam, gain, ready) = refs[:shares], refs[shares : shares + 6]
    scale, gm, adj, a_out, a_next = refs[shares + 6 :]
    del ready

    @pl.when(pl.program_id(0) == 0)
    def _():
        sums = total([ref[...] for ref in own_sums])
        inv = lax.rsqrt(sums[0:1, :] / width + 1e-05)
        coef = inv * inv * inv * sums[1:2, :] / width
        for which, value in enumerate((inv, coef)):
            for b in range(steps // LANES):
                piece = value[:, b * LANES : (b + 1) * LANES]
                scale[pl.ds(which * steps + b * LANES, LANES), :] = jnp.broadcast_to(
                    piece, (LANES, LANES)
                ).T

    fade, skip = fades(lam, modes, 1), fades(lam, modes, SUB)
    factor = gain[...]

    def advance(c, a):
        block = steps // SUB - 1 - c
        now = [None] * SUB
        for i in reversed(range(SUB)):
            t = block * SUB + i
            inv = scale[pl.ds(t, 1), :]
            coef = scale[pl.ds(steps + t, 1), :]
            grad = inv * (factor * row(cot_pos, t)) - coef * row(summed, t)
            now[i] = grad * row(f0, t)
            put(gm, t, now[i])
        new = []
        for m in range(modes):
            put(a_next, m, a[m])
            own = horner(fade[m], now[::-1])
            put(adj, block * modes + m, own)
            new.append(own + skip[m] * a[m])
        return tuple(new)

    a = loop(0, steps // SUB, advance, zeros(modes))
    for m in range(modes):
        put(a_out, m, a[m])


def across_kernel(modes, steps, *refs):
    for start in (0, modes // 2):
        across_part(range(start, start + modes // 2), modes, steps, *refs)


def across_part(ms, modes, steps, gm, adj, x_at, lag, lam, res_part, rate_part):
    fade, far = fades(lam, modes, 1), fades(lam, modes, SUB)
    last = steps // SUB - 1

    def across(c, state):
        after, by_res, by_rate = (list(v) for v in state)
        block = last - c
        now = [row(gm, block * SUB + i) * float(i) for i in range(1, SUB)]
        for i, m in enumerate(ms):
            x, own = row(x_at, block * modes + m), row(adj, block * modes + m)
            tail = fade[m] * horner(fade[m], now[::-1])
            by_res[i] = by_res[i] + x * own
            by_rate[i] = by_rate[i] + (x * tail + after[i] * row(lag, block * modes + m))
            after[i] = own + far[m] * after[i]
        return tuple(after), tuple(by_res), tuple(by_rate)

    none = zeros(len(ms))
    _, by_res, by_rate = loop(0, steps // SUB, across, (none, none, none))
    for i, m in enumerate(ms):
        put(res_part, m, fade[m] * by_res[i])
        put(rate_part, m, fade[m] * by_rate[i])


def near_adjoint_kernel(modes, taps, steps, gm, u, lam, res, skip, res_part, rate_part, scale, summed, cot_pos, modal, q_ext, gain, gmy, rate_sum, gf0, early):
    near = near_taps(lam, res, skip, modes)

    def pairs(c, lags):
        now = [row(gm, c * SUB + i) for i in range(SUB)]
        for i in range(SUB):
            put(gmy, c * SUB + i, total([near[k] * now[i + k] for k in range(SUB - i)]))
        before = [row(u, c * SUB + i) for i in range(SUB)]
        return tuple(
            lags[k] + total([now[i] * before[i - k] for i in range(k, SUB)]) for k in range(SUB)
        )

    lags = loop(0, steps // SUB, pairs, zeros(SUB))
    put(early, taps + modes, lags[0])
    fade = fades(lam, modes, 1)
    weighted = [lags[k] * float(k) for k in range(1, SUB)]
    for m in range(modes):
        put(early, taps + m, row(res_part, m) + horner(fade[m], lags[::-1]))
        put(rate_sum, m, row(rate_part, m) + fade[m] * horner(fade[m], weighted[::-1]))
    query_sums(modes, taps, steps, scale, summed, cot_pos, modal, q_ext, gain, gf0, early)


def normed_kernel(steps, scale, summed, gain, ready, normed, work):
    del ready
    factor = gain[...]

    def make(c):
        for i in range(CHUNK):
            t = c * CHUNK + i
            put(work, t, row(summed, t) * scale[pl.ds(t, 1), :] * factor)

    skewed(steps // CHUNK, make, lambda c: gather_chunk(work, normed, c))


def residual_kernel(taps, steps, last, scale, summed, cot_pos, gain, gf0, next_head, filt, ready, grad_res, grad_query, work, head):
    del ready
    back(0, taps, steps, last, gf0, next_head, filt, grad_query, work, head)
    factor = gain[...]

    def make(c):
        for i in range(CHUNK):
            t = c * CHUNK + i
            scaled = scale[pl.ds(t, 1), :] * (factor * row(cot_pos, t))
            put(work, t, scaled - scale[pl.ds(steps + t, 1), :] * row(summed, t))

    skewed(steps // CHUNK, make, lambda c: gather_chunk(work, grad_res, c))


def query_sums(modes, taps, steps, scale, summed, cot_pos, modal, q_ext, gain, gf0, early):
    factor = gain[...]

    margin = taps - 1

    def grads(c, sums):
        by_gain, acc = sums
        window = [row(q_ext, c * SUB + SUB - margin + i) for i in range(SUB + margin)]
        for i in range(SUB):
            t = c * SUB + i
            now, here = row(cot_pos, t), row(summed, t)
            scaled = scale[pl.ds(t, 1), :] * now
            grad = factor * scaled - scale[pl.ds(steps + t, 1), :] * here
            front = grad * row(modal, t)
            put(gf0, t, front)
            by_gain = by_gain + scaled * here
            acc = tuple(acc[j] + front * window[margin + i - j] for j in range(taps))
        return by_gain, acc

    by_gain, acc = loop(0, steps // SUB, grads, (zeros(1)[0], zeros(taps)))
    put(early, taps + modes + 1, by_gain)
    for j in range(taps):
        put(early, j, acc[j])


def filter_pass(taps, steps, grad, ext):
    margin = taps - 1

    def some(c, acc):
        t0 = c * SUB
        window = [row(ext, t0 + SUB - margin + i) for i in range(SUB + margin)]
        for i in range(SUB):
            now = row(grad, t0 + i)
            acc = tuple(acc[j] + now * window[margin + i - j] for j in range(taps))
        return acc

    zero = jnp.zeros((SUB, LANES), F32)
    return loop(0, steps // SUB, some, tuple(zero for _ in range(taps)))


def mixed_kernel(modes, steps, gmy, f1, f2, adj, lam, faded, alpha, gf1, gf2):
    fade, skip = fades(lam, modes, 1), fades(lam, modes, SUB)

    def advance(c, after):
        block = steps // SUB - 1 - c
        w = [row(faded, m) * after[m] for m in range(modes)]
        for i in reversed(range(SUB)):
            t = block * SUB + i
            grad = row(gmy, t) + total(w)
            put(gf1, t, grad * row(f2, t))
            put(gf2, t, grad * row(f1, t))
            w = [f * v for f, v in zip(fade, w)]
        return tuple(row(adj, block * modes + m) + skip[m] * after[m] for m in range(modes))

    loop(0, steps // SUB, advance, tuple(row(alpha, m) for m in range(modes)))


def filter_sums_kernel(taps, steps, gf1, gf2, k_ext, v_ext, sums):
    for which, (grad, ext) in enumerate(((gf1, k_ext), (gf2, v_ext))):
        parts = filter_pass(taps, steps, grad, ext)
        for j in range(taps):
            put(sums, which * taps + j, parts[j])


def back_kernel(taps, steps, last, gf1, gf2, next_head, filt, grad_key, grad_value, work, head):
    back(1, taps, steps, last, gf1, next_head, filt, grad_key, work, head)
    back(2, taps, steps, last, gf2, next_head, filt, grad_value, work, head)


def back(which, taps, steps, last, grad, next_head, filt, out, work, head):
    there = jnp.where(lax.axis_index("ctx") < last, 1.0, 0.0)
    head[...] = next_head[which, 0].astype(F32) * there
    weights = taps_of(filt, which, taps)

    def make(c):
        window = [row(grad, c * CHUNK + i) for i in range(CHUNK + taps - 1)]
        put_back(work, c * CHUNK, weights, window)

    def make_last(c):
        window = [row(grad, c * CHUNK + i) for i in range(CHUNK)]
        put_back(work, c * CHUNK, weights, window + [row(head, i) for i in range(taps - 1)])

    skewed(steps // CHUNK, make, lambda c: gather_chunk(work, out, c), make_last)


def put_back(out, start, weights, window):
    for i in range(CHUNK):
        put(out, start + i, total([w * window[i + j] for j, w in enumerate(weights)]))


def place(group, sign):
    at = lax.axis_index("ctx")
    if sign < 0:
        at = lax.axis_size("ctx") - 1 - at
    later = (at // group) % 2
    return (at % group).astype(F32), later.astype(F32)


def exclusive(before, other, lam, span, group, sign):
    at, later = place(group, sign)
    here = later * jnp.exp(lam * (at * -float(span))) * other.astype(F32)
    return here if before is None else before + here


def inclusive(own, other, lam, span, group, sign):
    _, later = place(group, sign)
    fall = -float(span * group)
    return jnp.exp(lam * ((1.0 - later) * fall)) * own + jnp.exp(lam * (later * fall)) * other.astype(F32)


def join_kernel(span, group, sign, first, own, other, lam, *refs):
    before, ends = (None, refs[-3:]) if first else (refs[0][...], refs[-3:])
    ends[0][...] = exclusive(before, other[...], lam[...], span, group, sign)
    ends[1][...] = inclusive(own[...], other[...], lam[...], span, group, sign)
    ends[2][...] = ends[1][...].astype(BF16)


def join_four_kernel(span, sign, own, first, second, third, lam, *refs):
    before, end, sent = refs[-3:]
    at, _ = place(4, sign)
    here = lax.axis_index("ctx") if sign > 0 else lax.axis_size("ctx") - 1 - lax.axis_index("ctx")
    here, rates = here % 4, lam[...]
    total_end = jnp.exp(rates * ((3.0 - at) * -float(span))) * own[...]
    total_before = None
    for k, other in enumerate((first, second, third)):
        there = (here ^ (k + 1)).astype(F32)
        earlier = jnp.where(there < at, 1.0, 0.0)
        gap = jnp.maximum(at - 1.0 - there, 0.0)
        value = other[...]
        share = earlier * jnp.exp(rates * (gap * -float(span))) * value
        total_before = share if total_before is None else total_before + share
        total_end = total_end + jnp.exp(rates * ((3.0 - there) * -float(span))) * value
    before[...] = total_before
    end[...] = total_end
    sent[...] = total_end.astype(BF16)


def add_four_kernel(own, first, second, third, *refs):
    refs[-1][...] = (own[...] + first[...]) + (second[...] + third[...])


def add_kernel(one, other, *refs):
    refs[-1][...] = one[...] + other[...]


def pack_kernel(span, group, modes, first_rows, half, before, other, lam, early, res, rate_sum, lag_sum, faded, a_next, gmy, f1, f2, gf0, alpha, kept, sent, heads):
    alpha[...] = exclusive(before[...], other[...], lam[...], span, group, -1)
    odd = lax.axis_index("ctx") % 2
    rows = (first_rows + modes) * SUB
    for out, start in ((kept, odd * half), (sent, (1 - odd) * half)):
        for b in range(half):
            source = pl.multiple_of((start + b) * (first_rows * SUB), SUB)
            out[pl.ds(b * rows, first_rows * SUB), :] = early[pl.ds(source, first_rows * SUB), :]
            source = pl.multiple_of((start + b) * (modes * SUB), SUB)
            mine = pl.ds(source, modes * SUB)
            lagged = rate_sum[mine, :] + jnp.exp(-lam[mine, :]) * alpha[mine, :] * lag_sum[mine, :]
            out[pl.ds(b * rows + first_rows * SUB, modes * SUB), :] = -res[mine, :] * lagged
    for b in range(2 * half):
        mine = slice(b * modes * SUB, (b + 1) * modes * SUB)
        far = jnp.exp(lam[mine, :] * -float(span - SUB))
        w, fade = faded[mine, :] * (a_next[mine, :] + far * alpha[mine, :]), jnp.exp(-lam[mine, :])
        here, grads = slice(b * span * SUB, (b * span + SUB) * SUB), []
        for t in range(SUB):
            grads.append(total([w[m * SUB : (m + 1) * SUB, :] for m in range(modes)]))
            w = fade * w
        grad = gmy[here, :] + jnp.concatenate(grads[::-1], axis=0)
        for which, value in enumerate((gf0[here, :], grad * f2[here, :], grad * f1[here, :])):
            heads[which, b] = value.astype(BF16)


def finish_kernel(modes, taps, half, early_rows, mine, other, late_mine, late_other, ready, short, res, rate, skip, gain, late, early):
    del ready
    block = pl.program_id(0)
    late[...] = late_mine[...] + late_other[...]
    own = jnp.where(lax.axis_index("ctx") % 2 == block // half, 1.0, 0.0)
    early[...] = own * mine[...] + (1.0 - own) * other[...]
    for s in range(SUB):
        lanes = slice(s * LANES, (s + 1) * LANES)
        short[0, :, lanes] = early[pl.ds(s, taps, stride=SUB), :]
        short[1, :, lanes] = late[pl.ds(s, taps, stride=SUB), :]
        short[2, :, lanes] = late[pl.ds(taps * SUB + s, taps, stride=SUB), :]
        res[:, lanes] = early[pl.ds(taps * SUB + s, modes, stride=SUB), :]
        rate[:, lanes] = early[pl.ds((taps + modes + 2) * SUB + s, modes, stride=SUB), :]
    skip[...] = row(early, taps + modes)
    gain[...] = row(early, taps + modes + 1)


def ring(value, axis, distance):
    count = lax.axis_size(axis)
    return lax.ppermute(value, axis, [(i, (i + distance) % count) for i in range(count)])


def swap(value, axis, step):
    return lax.ppermute(value, axis, [(i, i ^ step) for i in range(lax.axis_size(axis))])


def small(body, ins, after, outs, name):
    near = pl.BlockSpec(memory_space=pltpu.VMEM)
    ins = [pltpu.with_memory_space_constraint(v, pltpu.VMEM) if v.size > 1 << 18 else v for v in ins]
    return pl.pallas_call(
        body,
        in_specs=[near] * len(ins) + [pl.BlockSpec(memory_space=pl.ANY)] * len(after),
        out_specs=[near] * len(outs),
        out_shape=[jax.ShapeDtypeStruct(v, F32) if isinstance(v, tuple) else v for v in outs],
        compiler_params=pltpu.CompilerParams(vmem_limit_bytes=VMEM_LIMIT),
        cost_estimate=pl.CostEstimate(flops=ins[0].size, bytes_accessed=0, transcendentals=0),
        name=name,
    )(*ins, *after)


def scan_but_last(own, lam, span, sign, under):
    count, group, before = lax.axis_size("ctx"), 1, None
    under, sent = list(under), own
    outs = [own.shape, own.shape, jax.ShapeDtypeStruct(own.shape, BF16)]
    if count >= 8:
        ins = [own, *(swap(own, "ctx", k) for k in (1, 2, 3)), lam]
        body = functools.partial(join_four_kernel, span, sign)
        before, own, sent = small(body, ins, under, outs, "join")
        group, under = 4, []
    while True:
        other = swap(sent, "ctx", group)
        if 2 * group >= count:
            return before, other, group
        body = functools.partial(join_kernel, span, group, sign, before is None)
        ins = [own, other, lam] + ([] if before is None else [before])
        after = [under.pop(0)] if under else []
        before, own, sent = small(body, ins, after, outs, "join")
        group *= 2


def shards(
    residual, query_in, key_in, value_in, short_filter, residues, decay_rate, skip_gain, norm_gain, cotangent
):
    steps, channels = residual.shape
    modes, taps = residues.shape[0], short_filter.shape[1]
    blocks = channels // WIDE
    width = channels * lax.axis_size("tp")
    skip, gain = (v.reshape(blocks * SUB, LANES) for v in (skip_gain, norm_gain))

    def pos(count):
        return jax.ShapeDtypeStruct((blocks * count * SUB, LANES), F32)

    def kept(count):
        return pltpu.VMEM((blocks * count * SUB, LANES), F32)

    def pos_spec(count):
        return pl.BlockSpec((count * SUB, LANES), lambda h: (h, 0))

    def head_spec(total_steps, start):
        return pl.BlockSpec((SUB * SUB, LANES), lambda h: (h * (total_steps // SUB) + start, 0))

    wide_spec = pl.BlockSpec((steps, WIDE), lambda h: (0, h))
    wide = jax.ShapeDtypeStruct((steps, channels), BF16)
    mode_spec, one_spec, filt_spec = pos_spec(modes), pos_spec(1), pos_spec(3 * taps)
    seq_spec, ext_spec = pos_spec(steps), pos_spec(steps + SUB)
    seq, ext, mode, one = kept(steps), kept(steps + SUB), pos(modes), pos(1)
    eights, eights_spec = kept(steps // SUB * modes), pos_spec(steps // SUB * modes)
    halo_spec = pl.BlockSpec((3, SUB, WIDE), lambda h: (0, 0, h))
    param_spec = pl.BlockSpec((modes, WIDE), lambda h: (0, h))
    short_spec = pl.BlockSpec((3, taps, WIDE), lambda h: (0, 0, h))

    def call(body, ins, in_specs, outs, out_specs, ops, name, scratch=(), aliases=None):
        elements, n_refs = steps * channels, len(ins) + len(outs)

        def with_done(*refs):
            done = refs[n_refs]
            done[...] = jnp.zeros_like(done)
            body(*refs[:n_refs], *refs[n_refs + 1 :])

        near = blocks * steps * SUB
        ins = [
            pltpu.with_memory_space_constraint(v, pltpu.VMEM) if v.shape[0] >= near and v.dtype == F32 else v
            for v in ins
        ]
        done_shape = (SUB, LANES)
        outs = [*outs, jax.ShapeDtypeStruct(done_shape, F32)]
        out_specs = [*out_specs, pl.BlockSpec(done_shape, lambda h: (0, 0))]
        return pl.pallas_call(
            with_done,
            grid=(blocks,),
            in_specs=in_specs,
            out_specs=out_specs,
            out_shape=outs,
            scratch_shapes=list(scratch),
            input_output_aliases=aliases or {},
            compiler_params=pltpu.CompilerParams(
                dimension_semantics=("arbitrary",), vmem_limit_bytes=VMEM_LIMIT
            ),
            cost_estimate=pl.CostEstimate(
                flops=ops * elements, bytes_accessed=4 * elements, transcendentals=0
            ),
            name=name,
        )(*ins)

    far = [
        pltpu.with_memory_space_constraint(v, pltpu.HBM)
        for v in (residual, query_in, key_in, value_in, cotangent, short_filter, decay_rate, residues)
    ]
    last_spec = pl.BlockSpec((2 * SUB, channels), lambda h: (steps // (2 * SUB) - 1, 0))
    trailing = pl.pallas_call(
        trailing_kernel,
        grid=(1,),
        in_specs=[last_spec] * 3,
        out_specs=pl.BlockSpec((3, SUB, channels), lambda h: (0, 0, 0)),
        out_shape=jax.ShapeDtypeStruct((3, SUB, channels), BF16),
        compiler_params=pltpu.CompilerParams(vmem_limit_bytes=VMEM_LIMIT),
        cost_estimate=pl.CostEstimate(flops=channels, bytes_accessed=channels, transcendentals=0),
        name="trailing",
    )(*far[1:4])
    halo = ring(trailing, "ctx", 1)

    k_ext, v_ext, f1, f2, u, g, lam, res, faded, filt, x_part, _ = call(
        functools.partial(features_kernel, modes, taps, steps),
        (far[2], far[3], *far[5:]),
        [wide_spec, wide_spec, short_spec, param_spec, param_spec],
        [ext, ext, seq, seq, seq, eights, mode, mode, mode, pos(3 * taps), mode],
        [ext_spec, ext_spec, seq_spec, seq_spec, seq_spec, eights_spec, mode_spec, mode_spec, mode_spec, filt_spec, mode_spec],
        64,
        "features",
    )
    any_spec = pl.BlockSpec(memory_space=pl.ANY)
    k_ext, v_ext, f1, f2, u, g, x_own, _ = call(
        functools.partial(head_kernel, modes, taps, steps),
        (halo, k_ext, v_ext, filt, lam, x_part, f1, f2, u, g),
        [halo_spec, head_spec(steps + SUB, 1), head_spec(steps + SUB, 1), filt_spec, mode_spec, mode_spec]
        + [any_spec] * 4,
        [ext, ext, seq, seq, seq, eights, mode],
        [head_spec(steps + SUB, 0)] * 2
        + [head_spec(steps, 0)] * 3
        + [pl.BlockSpec((modes * SUB, LANES), lambda h: (h * (steps // SUB), 0)), mode_spec],
        2,
        "head",
        aliases={1: 0, 2: 1, 6: 2, 7: 3, 8: 4, 9: 5},
    )
    q_ext, f0, res_pos, cot_pos, query_done = call(
        functools.partial(query_kernel, taps, steps),
        (far[1], far[0], far[4], halo, filt),
        [wide_spec, wide_spec, wide_spec, halo_spec, filt_spec],
        [ext, seq, seq, seq],
        [ext_spec, seq_spec, seq_spec, seq_spec],
        30,
        "query",
    )
    y, near_done = call(
        functools.partial(near_kernel, modes, steps),
        (u, lam, res, skip),
        [seq_spec, mode_spec, mode_spec, one_spec],
        [seq],
        [seq_spec],
        10,
        "near",
    )
    own_lag, own_lag_done = call(
        functools.partial(lags_kernel, modes, steps),
        (u, lam),
        [seq_spec, mode_spec],
        [eights],
        [eights_spec],
        32,
        "lags",
    )
    before, other, group = scan_but_last(x_own, lam, steps, 1, [query_done, near_done])
    modal, summed, x_at, sums, _ = call(
        functools.partial(summed_kernel, modes, steps, blocks, group),
        (y, f0, res_pos, cot_pos, g, before, other, lam, faded, gain, own_lag_done),
        [seq_spec] * 4 + [eights_spec] + [mode_spec] * 4 + [one_spec, any_spec],
        [seq, seq, eights, jax.ShapeDtypeStruct((2, steps), F32)],
        [seq_spec, seq_spec, eights_spec, pl.BlockSpec((2, steps), lambda h: (0, 0))],
        50,
        "summed",
        scratch=[pltpu.VMEM((steps * SUB, LANES), F32)] * 2,
    )
    all_sums = [sums, *(swap(sums, "tp", k) for k in range(1, lax.axis_size("tp")))]
    lag, lag_sum, lags_done = call(
        functools.partial(borders_kernel, modes, steps),
        (own_lag, x_at, lam),
        [eights_spec, eights_spec, mode_spec],
        [eights, mode],
        [eights_spec, mode_spec],
        8,
        "borders",
    )
    scale_spec = pl.BlockSpec((2 * steps, LANES), lambda h: (0, 0))
    scale, gm, adj, a_own, a_next, _ = call(
        functools.partial(grad_modal_kernel, modes, steps, width, len(all_sums)),
        (*all_sums, summed, cot_pos, f0, lam, gain, lags_done),
        [pl.BlockSpec((2, steps), lambda h: (0, 0))] * len(all_sums)
        + [seq_spec, seq_spec, seq_spec, mode_spec, one_spec, any_spec],
        [pltpu.VMEM((2 * steps, LANES), F32), seq, eights, mode, mode],
        [scale_spec, seq_spec, eights_spec, mode_spec, mode_spec],
        45,
        "grad_modal",
    )
    res_part, rate_part, across_done = call(
        functools.partial(across_kernel, modes, steps),
        (gm, adj, x_at, lag, lam),
        [seq_spec, eights_spec, eights_spec, eights_spec, mode_spec],
        [mode, mode],
        [mode_spec, mode_spec],
        50,
        "across",
    )
    early_rows = taps + modes + 2
    gmy, rate_sum, gf0, early, _ = call(
        functools.partial(near_adjoint_kernel, modes, taps, steps),
        (gm, u, lam, res, skip, res_part, rate_part, scale, summed, cot_pos, modal, q_ext, gain),
        [seq_spec, seq_spec, mode_spec, mode_spec, one_spec, mode_spec, mode_spec, scale_spec, seq_spec, seq_spec, seq_spec, ext_spec, one_spec],
        [seq, mode, seq, pos(early_rows)],
        [seq_spec, mode_spec, seq_spec, pos_spec(early_rows)],
        55,
        "near_adjoint",
    )
    before, other, group = scan_but_last(a_own, lam, steps, -1, [across_done])

    half = blocks // 2
    half_shape = (half * (early_rows + modes) * SUB, LANES)
    alpha, kept_half, sent_half, heads = small(
        functools.partial(pack_kernel, steps, group, modes, early_rows, half),
        [before, other, lam, early, res, rate_sum, lag_sum, faded, a_next, gmy, f1, f2, gf0],
        [],
        [lam.shape, half_shape, half_shape, jax.ShapeDtypeStruct((3, blocks, SUB * SUB, LANES), BF16)],
        "pack",
    )
    early_rows += modes
    late_rows = 2 * taps
    next_spec = pl.BlockSpec((3, 1, SUB * SUB, LANES), lambda h: (0, h, 0, 0))
    other_half = swap(sent_half, "ctx", 1)
    next_head = ring(heads, "ctx", -1)
    gf1, gf2, mixed_done = call(
        functools.partial(mixed_kernel, modes, steps),
        (gmy, f1, f2, adj, lam, faded, alpha),
        [seq_spec] * 3 + [eights_spec] + [mode_spec] * 3,
        [seq, seq],
        [seq_spec, seq_spec],
        45,
        "mixed",
    )
    late, late_done = call(
        functools.partial(filter_sums_kernel, taps, steps),
        (gf1, gf2, k_ext, v_ext),
        [seq_spec, seq_spec, ext_spec, ext_spec],
        [pos(late_rows)],
        [pos_spec(late_rows)],
        30,
        "filter_sums",
    )

    last = lax.axis_size("ctx") - 1
    back_scratch = [pltpu.VMEM((steps * SUB, LANES), F32), pltpu.VMEM((SUB * SUB, LANES), F32)]
    normed, normed_done = call(
        functools.partial(normed_kernel, steps),
        (scale, summed, gain, mixed_done),
        [scale_spec, seq_spec, one_spec, any_spec],
        [wide],
        [wide_spec],
        10,
        "normed",
        scratch=back_scratch[:1],
    )
    grad_residual, grad_query, norm_done = call(
        functools.partial(residual_kernel, taps, steps, last),
        (scale, summed, cot_pos, gain, gf0, next_head, filt, late_done),
        [scale_spec, seq_spec, seq_spec, one_spec, seq_spec, next_spec, filt_spec, any_spec],
        [wide, wide],
        [wide_spec, wide_spec],
        35,
        "residual",
        scratch=back_scratch,
    )
    grad_key, grad_value, back_done = call(
        functools.partial(back_kernel, taps, steps, last),
        (gf1, gf2, next_head, filt),
        [seq_spec, seq_spec, next_spec, filt_spec],
        [wide, wide],
        [wide_spec, wide_spec],
        40,
        "back",
        scratch=back_scratch,
    )
    count, under = lax.axis_size("ctx"), [[late_done, normed_done], [norm_done]]
    mine = small(add_kernel, [kept_half, other_half], [mixed_done, next_head], [half_shape], "add")[0]
    step = 2
    while step < count:
        after = under.pop(0) if under else [norm_done]
        mine = small(add_kernel, [mine, swap(mine, "ctx", step)], after, [half_shape], "add")[0]
        step *= 2
    other = swap(mine, "ctx", 1)
    step = 1
    if count >= 8:
        ins = [late, *(swap(late, "ctx", k) for k in (1, 2, 3))]
        late = small(add_four_kernel, ins, [norm_done], [late.shape], "add")[0]
        step = 4
    late_other = swap(late, "ctx", step)
    while 2 * step < count:
        late = small(add_kernel, [late, late_other], [norm_done], [late.shape], "add")[0]
        step *= 2
        late_other = swap(late, "ctx", step)
    half_spec = pl.BlockSpec((early_rows * SUB, LANES), lambda h: (h % half, 0))
    late_spec = pos_spec(late_rows)
    grad_short, grad_residues, grad_rate, grad_skip, grad_gain, _ = call(
        functools.partial(finish_kernel, modes, taps, half, early_rows),
        (mine, other, late, late_other, back_done),
        [half_spec, half_spec, late_spec, late_spec, any_spec],
        [
            jax.ShapeDtypeStruct(short_filter.shape, F32),
            jax.ShapeDtypeStruct(residues.shape, F32),
            jax.ShapeDtypeStruct(residues.shape, F32),
            one,
            one,
        ],
        [short_spec, param_spec, param_spec, one_spec, one_spec],
        1,
        "finish",
        scratch=[
            pltpu.VMEM((late_rows * SUB, LANES), F32),
            pltpu.VMEM((early_rows * SUB, LANES), F32),
        ],
    )
    return (
        normed,
        grad_residual,
        grad_query,
        grad_key,
        grad_value,
        grad_short,
        grad_residues,
        grad_rate,
        grad_skip.reshape(channels),
        grad_gain.reshape(channels),
    )


def solution(mesh):
    both, modes, vector = P("ctx", "tp"), P(None, "tp"), P("tp")
    return jax.shard_map(
        shards,
        mesh=mesh,
        in_specs=(both, both, both, both, P(None, None, "tp"), modes, modes, vector, vector, both),
        out_specs=(both,) * 5 + (P(None, None, "tp"), modes, modes, vector, vector),
        check_vma=False,
    )
```

```python
import functools

import jax
import jax.numpy as jnp
from jax import lax
from jax.experimental import pallas as pl
from jax.experimental.pallas import tpu as pltpu
from jax.sharding import PartitionSpec as P

LANES = 128
SUB = 8
CHUNK = 16
WIDE = SUB * LANES
F32 = jnp.float32
BF16 = jnp.bfloat16
VMEM_LIMIT = 10 * 1024 * 1024


def row(ref, t):
    return ref[pl.ds(pl.multiple_of(t * SUB, SUB), SUB), :]


def put(ref, t, value):
    ref[pl.ds(pl.multiple_of(t * SUB, SUB), SUB), :] = value


def loop(start, stop, body, carry):
    eights = (stop - start) // 8

    def eight(i, carry):
        for k in range(8):
            carry = body(start + 8 * i + k, carry)
        return carry

    carry = lax.fori_loop(0, eights, eight, carry)
    for i in range(start + 8 * eights, stop):
        carry = body(i, carry)
    return carry


def spread_chunk(src, dst, first, c):
    start = pl.multiple_of(c * CHUNK, CHUNK)
    for g in range(SUB):
        piece = src[pl.ds(start, CHUNK), g * LANES : (g + 1) * LANES].astype(F32)
        dst[pl.ds((start + first) * SUB + g, CHUNK, stride=SUB), :] = piece


def gather_chunk(src, dst, c):
    start = pl.multiple_of(c * CHUNK, CHUNK)
    for g in range(SUB):
        piece = src[pl.ds(start * SUB + g, CHUNK, stride=SUB), :]
        dst[pl.ds(start, CHUNK), g * LANES : (g + 1) * LANES] = piece.astype(dst.dtype)


def skewed(chunks, make, lay, make_last=None):
    make(0)

    def some(c, carry):
        lay(c - 1)
        make(c)
        return carry

    lax.fori_loop(1, chunks - 1, some, 0)
    lay(chunks - 2)
    (make_last or make)(chunks - 1)
    lay(chunks - 1)


def total(values):
    values = list(values)
    while len(values) > 1:
        values = [
            values[i] + values[i + 1] if i + 1 < len(values) else values[i]
            for i in range(0, len(values), 2)
        ]
    return values[0]


def taps_of(filt, stream, taps):
    return [row(filt, stream * taps + j) for j in range(taps)]


def conv_at(window, taps, i):
    margin = len(taps) - 1
    return total([taps[j] * window[margin + i - j] for j in range(margin + 1)])


def trailing_kernel(query, key, value, out):
    for i, ref in enumerate((query, key, value)):
        out[i] = ref[...].astype(F32)[SUB:, :].astype(BF16)


def features_kernel(
    modes, taps, steps, key, value, filt3, decay, resid, k_ext, v_ext, f1, f2, u, g, lam, res, faded, filt, x_out
):
    margin = taps - 1
    for s in range(SUB):
        lanes = slice(s * LANES, (s + 1) * LANES)
        lam[pl.ds(s, modes, stride=SUB), :] = decay[:, lanes]
        res[pl.ds(s, modes, stride=SUB), :] = resid[:, lanes]
        for i in range(3):
            filt[pl.ds(i * taps * SUB + s, taps, stride=SUB), :] = filt3[i, :, lanes]
    faded[...] = res[...] * jnp.exp(-lam[...])
    taps1, taps2 = taps_of(filt, 1, taps), taps_of(filt, 2, taps)
    fade, skip = fades(lam, modes, 1), fades(lam, modes, SUB)
    chunks = steps // CHUNK

    def shape(c):
        for src, dst in ((key, k_ext), (value, v_ext)):
            spread_chunk(src, dst, SUB, c)

    def conv(c, skipped=0):
        t0 = c * CHUNK
        kw = [row(k_ext, t0 + SUB - margin + i) for i in range(skipped, CHUNK + margin)]
        vw = [row(v_ext, t0 + SUB - margin + i) for i in range(skipped, CHUNK + margin)]
        for i in range(CHUNK - skipped):
            first, second = conv_at(kw, taps1, i), conv_at(vw, taps2, i)
            put(f1, t0 + skipped + i, first)
            put(f2, t0 + skipped + i, second)
            put(u, t0 + skipped + i, first * second)

    def advance(c, x, skipped=0):
        for b in range(skipped, CHUNK // SUB):
            block = c * (CHUNK // SUB) + b
            now = [row(u, block * SUB + i) for i in range(SUB)]
            new = []
            for m in range(modes):
                own = horner(fade[m], now)
                put(g, block * modes + m, own)
                new.append(own + skip[m] * x[m])
            x = tuple(new)
        return x

    shape(0)
    shape(1)
    conv(0, SUB)
    shape(2)
    conv(1)
    x = advance(0, zeros(modes), 1)

    def some(c, x):
        shape(c + 1)
        conv(c)
        return advance(c - 1, x)

    x = lax.fori_loop(2, chunks - 1, some, x)
    conv(chunks - 1)
    x = advance(chunks - 1, advance(chunks - 2, x))
    for m in range(modes):
        put(x_out, m, x[m])


def zeros(count):
    return tuple(jnp.zeros((SUB, LANES), F32) for _ in range(count))


def fades(lam, modes, span):
    return [jnp.exp(row(lam, m) * -float(span)) for m in range(modes)]


def horner(fade, values):
    result = values[0]
    for value in values[1:]:
        result = fade * result + value
    return result


def head_kernel(
    modes, taps, steps, halo, k_head, v_head, filt, lam, x_part, f1_in, f2_in, u_in, g_in,
    k_ext, v_ext, f1, f2, u, g, x_out,
):
    del f1_in, f2_in, u_in, g_in
    margin = taps - 1
    there = jnp.where(lax.axis_index("ctx") > 0, 1.0, 0.0)
    for s in range(SUB):
        lanes = slice(s * LANES, (s + 1) * LANES)
        k_ext[pl.ds(s, SUB, stride=SUB), :] = halo[1, :, lanes].astype(F32) * there
        v_ext[pl.ds(s, SUB, stride=SUB), :] = halo[2, :, lanes].astype(F32) * there
    taps1, taps2 = taps_of(filt, 1, taps), taps_of(filt, 2, taps)
    kw = [row(k_ext, SUB - margin + i) for i in range(margin)] + [row(k_head, i) for i in range(SUB)]
    vw = [row(v_ext, SUB - margin + i) for i in range(margin)] + [row(v_head, i) for i in range(SUB)]
    mixed = []
    for i in range(SUB):
        first, second = conv_at(kw, taps1, i), conv_at(vw, taps2, i)
        put(f1, i, first)
        put(f2, i, second)
        put(u, i, first * second)
        mixed.append(first * second)
    fade, rest = fades(lam, modes, 1), fades(lam, modes, steps - SUB)
    for m in range(modes):
        own = horner(fade[m], mixed)
        put(g, m, own)
        put(x_out, m, row(x_part, m) + rest[m] * own)


def query_kernel(taps, steps, query, residual, cot, halo, filt, q_ext, f0, res_pos, cot_pos):
    margin = taps - 1
    there = jnp.where(lax.axis_index("ctx") > 0, 1.0, 0.0)
    for s in range(SUB):
        lanes = slice(s * LANES, (s + 1) * LANES)
        q_ext[pl.ds(s, SUB, stride=SUB), :] = halo[0, :, lanes].astype(F32) * there
    taps0, chunks = taps_of(filt, 0, taps), steps // CHUNK

    def conv(c):
        t0 = c * CHUNK
        qw = [row(q_ext, t0 + SUB - margin + i) for i in range(CHUNK + margin)]
        for i in range(CHUNK):
            put(f0, t0 + i, conv_at(qw, taps0, i))

    def shape(c):
        spread_chunk(query, q_ext, SUB, c)
        spread_chunk(residual, res_pos, 0, c)
        spread_chunk(cot, cot_pos, 0, c)

    shape(0)

    def some(c, carry):
        conv(c - 1)
        shape(c)
        return carry

    lax.fori_loop(1, chunks, some, 0)
    conv(chunks - 1)


def near_taps(lam, res, skip, modes):
    fade, weight = fades(lam, modes, 1), [row(res, m) for m in range(modes)]
    result = []
    for k in range(SUB):
        result.append(total(weight) if k else total(weight) + skip[...])
        weight = [f * w for f, w in zip(fade, weight)]
    return result


def near_kernel(modes, steps, u, lam, res, skip, y):
    near = near_taps(lam, res, skip, modes)

    def some(c, carry):
        now = [row(u, c * SUB + i) for i in range(SUB)]
        for i in range(SUB):
            put(y, c * SUB + i, total([near[k] * now[i - k] for k in range(i + 1)]))
        return carry

    loop(0, steps // SUB, some, 0)


def lags_kernel(modes, steps, u, lam, lag):
    fade = fades(lam, modes, 1)

    def some(c, carry):
        now = [row(u, c * SUB + i) * float(SUB - i) for i in range(SUB)]
        for m in range(modes):
            put(lag, c * modes + m, horner(fade[m], now))
        return carry

    loop(0, steps // SUB, some, 0)


def borders_kernel(modes, steps, own_lag, x_at, lam, lag, lag_sum):
    skip = fades(lam, modes, SUB)
    eight = [float(SUB) * v for v in skip]

    def some(c, sums):
        new = []
        for m in range(modes):
            border = row(own_lag, c * modes + m) + eight[m] * row(x_at, c * modes + m)
            put(lag, c * modes + m, border)
            new.append(skip[m] * sums[m] + border)
        return tuple(new)

    sums = loop(0, steps // SUB, some, zeros(modes))
    for m in range(modes):
        put(lag_sum, m, sums[m])


def summed_kernel(modes, steps, blocks, group, y, f0, res_pos, cot_pos, g, before, other, lam, faded, gain, ready, modal, summed, x_at, sums, squares, inner):
    del ready
    block = pl.program_id(0)

    @pl.when(block == 0)
    def _():
        squares[...] = jnp.zeros_like(squares)
        inner[...] = jnp.zeros_like(inner)

    fade, skip = fades(lam, modes, 1), fades(lam, modes, SUB)
    factor = gain[...]
    x_in = exclusive(before[...], other[...], lam[...], steps, group, 1)
    x_in = tuple(x_in[m * SUB : (m + 1) * SUB, :] for m in range(modes))

    def advance(c, x):
        w = [row(faded, m) * x[m] for m in range(modes)]
        for m in range(modes):
            put(x_at, c * modes + m, x[m])
        for i in range(SUB):
            t = c * SUB + i
            if i:
                w = [f * v for f, v in zip(fade, w)]
            long = row(y, t) + total(w)
            put(modal, t, long)
            now = row(res_pos, t) + row(f0, t) * long
            put(summed, t, now)
            put(squares, t, row(squares, t) + now * now)
            put(inner, t, row(inner, t) + factor * row(cot_pos, t) * now)
        return tuple(row(g, c * modes + m) + skip[m] * x[m] for m in range(modes))

    loop(0, steps // SUB, advance, x_in)

    @pl.when(block == blocks - 1)
    def _():
        for which, scratch in enumerate((squares, inner)):
            for b in range(steps // LANES):
                part = total(
                    [
                        scratch[pl.ds(b * LANES * SUB + s, LANES, stride=SUB), :]
                        for s in range(SUB)
                    ]
                )
                sums[which : which + 1, b * LANES : (b + 1) * LANES] = jnp.sum(
                    part.T, axis=0, keepdims=True
                )


def grad_modal_kernel(modes, steps, width, shares, *refs):
    own_sums, (summed, cot_pos, f0, lam, gain, ready) = refs[:shares], refs[shares : shares + 6]
    scale, gm, adj, a_out, a_next = refs[shares + 6 :]
    del ready

    @pl.when(pl.program_id(0) == 0)
    def _():
        sums = total([ref[...] for ref in own_sums])
        inv = lax.rsqrt(sums[0:1, :] / width + 1e-05)
        coef = inv * inv * inv * sums[1:2, :] / width
        for which, value in enumerate((inv, coef)):
            for b in range(steps // LANES):
                piece = value[:, b * LANES : (b + 1) * LANES]
                scale[pl.ds(which * steps + b * LANES, LANES), :] = jnp.broadcast_to(
                    piece, (LANES, LANES)
                ).T

    fade, skip = fades(lam, modes, 1), fades(lam, modes, SUB)
    factor = gain[...]

    def advance(c, a):
        block = steps // SUB - 1 - c
        now = [None] * SUB
        for i in reversed(range(SUB)):
            t = block * SUB + i
            inv = scale[pl.ds(t, 1), :]
            coef = scale[pl.ds(steps + t, 1), :]
            grad = inv * (factor * row(cot_pos, t)) - coef * row(summed, t)
            now[i] = grad * row(f0, t)
            put(gm, t, now[i])
        new = []
        for m in range(modes):
            put(a_next, m, a[m])
            own = horner(fade[m], now[::-1])
            put(adj, block * modes + m, own)
            new.append(own + skip[m] * a[m])
        return tuple(new)

    a = loop(0, steps // SUB, advance, zeros(modes))
    for m in range(modes):
        put(a_out, m, a[m])


def across_kernel(modes, steps, *refs):
    for start in (0, modes // 2):
        across_part(range(start, start + modes // 2), modes, steps, *refs)


def across_part(ms, modes, steps, gm, adj, x_at, lag, lam, res_part, rate_part):
    fade, far = fades(lam, modes, 1), fades(lam, modes, SUB)
    last = steps // SUB - 1

    def across(c, state):
        after, by_res, by_rate = (list(v) for v in state)
        block = last - c
        now = [row(gm, block * SUB + i) * float(i) for i in range(1, SUB)]
        for i, m in enumerate(ms):
            x, own = row(x_at, block * modes + m), row(adj, block * modes + m)
            tail = fade[m] * horner(fade[m], now[::-1])
            by_res[i] = by_res[i] + x * own
            by_rate[i] = by_rate[i] + (x * tail + after[i] * row(lag, block * modes + m))
            after[i] = own + far[m] * after[i]
        return tuple(after), tuple(by_res), tuple(by_rate)

    none = zeros(len(ms))
    _, by_res, by_rate = loop(0, steps // SUB, across, (none, none, none))
    for i, m in enumerate(ms):
        put(res_part, m, fade[m] * by_res[i])
        put(rate_part, m, fade[m] * by_rate[i])


def near_adjoint_kernel(modes, taps, steps, gm, u, lam, res, skip, res_part, rate_part, scale, summed, cot_pos, modal, q_ext, gain, gmy, rate_sum, gf0, early):
    near = near_taps(lam, res, skip, modes)

    def pairs(c, lags):
        now = [row(gm, c * SUB + i) for i in range(SUB)]
        for i in range(SUB):
            put(gmy, c * SUB + i, total([near[k] * now[i + k] for k in range(SUB - i)]))
        before = [row(u, c * SUB + i) for i in range(SUB)]
        return tuple(
            lags[k] + total([now[i] * before[i - k] for i in range(k, SUB)]) for k in range(SUB)
        )

    lags = loop(0, steps // SUB, pairs, zeros(SUB))
    put(early, taps + modes, lags[0])
    fade = fades(lam, modes, 1)
    weighted = [lags[k] * float(k) for k in range(1, SUB)]
    for m in range(modes):
        put(early, taps + m, row(res_part, m) + horner(fade[m], lags[::-1]))
        put(rate_sum, m, row(rate_part, m) + fade[m] * horner(fade[m], weighted[::-1]))
    query_sums(modes, taps, steps, scale, summed, cot_pos, modal, q_ext, gain, gf0, early)


def normed_kernel(steps, scale, summed, gain, ready, normed, work):
    del ready
    factor = gain[...]

    def make(c):
        for i in range(CHUNK):
            t = c * CHUNK + i
            put(work, t, row(summed, t) * scale[pl.ds(t, 1), :] * factor)

    skewed(steps // CHUNK, make, lambda c: gather_chunk(work, normed, c))


def residual_kernel(taps, steps, last, scale, summed, cot_pos, gain, gf0, next_head, filt, ready, grad_res, grad_query, work, head):
    del ready
    back(0, taps, steps, last, gf0, next_head, filt, grad_query, work, head)
    factor = gain[...]

    def make(c):
        for i in range(CHUNK):
            t = c * CHUNK + i
            scaled = scale[pl.ds(t, 1), :] * (factor * row(cot_pos, t))
            put(work, t, scaled - scale[pl.ds(steps + t, 1), :] * row(summed, t))

    skewed(steps // CHUNK, make, lambda c: gather_chunk(work, grad_res, c))


def query_sums(modes, taps, steps, scale, summed, cot_pos, modal, q_ext, gain, gf0, early):
    factor = gain[...]

    margin = taps - 1

    def grads(c, sums):
        by_gain, acc = sums
        window = [row(q_ext, c * SUB + SUB - margin + i) for i in range(SUB + margin)]
        for i in range(SUB):
            t = c * SUB + i
            now, here = row(cot_pos, t), row(summed, t)
            scaled = scale[pl.ds(t, 1), :] * now
            grad = factor * scaled - scale[pl.ds(steps + t, 1), :] * here
            front = grad * row(modal, t)
            put(gf0, t, front)
            by_gain = by_gain + scaled * here
            acc = tuple(acc[j] + front * window[margin + i - j] for j in range(taps))
        return by_gain, acc

    by_gain, acc = loop(0, steps // SUB, grads, (zeros(1)[0], zeros(taps)))
    put(early, taps + modes + 1, by_gain)
    for j in range(taps):
        put(early, j, acc[j])


def filter_pass(taps, steps, grad, ext):
    margin = taps - 1

    def some(c, acc):
        t0 = c * SUB
        window = [row(ext, t0 + SUB - margin + i) for i in range(SUB + margin)]
        for i in range(SUB):
            now = row(grad, t0 + i)
            acc = tuple(acc[j] + now * window[margin + i - j] for j in range(taps))
        return acc

    zero = jnp.zeros((SUB, LANES), F32)
    return loop(0, steps // SUB, some, tuple(zero for _ in range(taps)))


def mixed_kernel(modes, steps, gmy, f1, f2, adj, lam, faded, alpha, gf1, gf2):
    fade, skip = fades(lam, modes, 1), fades(lam, modes, SUB)

    def advance(c, after):
        block = steps // SUB - 1 - c
        w = [row(faded, m) * after[m] for m in range(modes)]
        for i in reversed(range(SUB)):
            t = block * SUB + i
            grad = row(gmy, t) + total(w)
            put(gf1, t, grad * row(f2, t))
            put(gf2, t, grad * row(f1, t))
            w = [f * v for f, v in zip(fade, w)]
        return tuple(row(adj, block * modes + m) + skip[m] * after[m] for m in range(modes))

    loop(0, steps // SUB, advance, tuple(row(alpha, m) for m in range(modes)))


def filter_sums_kernel(taps, steps, gf1, gf2, k_ext, v_ext, sums):
    for which, (grad, ext) in enumerate(((gf1, k_ext), (gf2, v_ext))):
        parts = filter_pass(taps, steps, grad, ext)
        for j in range(taps):
            put(sums, which * taps + j, parts[j])


def back_kernel(taps, steps, last, gf1, gf2, next_head, filt, grad_key, grad_value, work, head):
    back(1, taps, steps, last, gf1, next_head, filt, grad_key, work, head)
    back(2, taps, steps, last, gf2, next_head, filt, grad_value, work, head)


def back(which, taps, steps, last, grad, next_head, filt, out, work, head):
    there = jnp.where(lax.axis_index("ctx") < last, 1.0, 0.0)
    head[...] = next_head[which, 0].astype(F32) * there
    weights = taps_of(filt, which, taps)

    def make(c):
        window = [row(grad, c * CHUNK + i) for i in range(CHUNK + taps - 1)]
        put_back(work, c * CHUNK, weights, window)

    def make_last(c):
        window = [row(grad, c * CHUNK + i) for i in range(CHUNK)]
        put_back(work, c * CHUNK, weights, window + [row(head, i) for i in range(taps - 1)])

    skewed(steps // CHUNK, make, lambda c: gather_chunk(work, out, c), make_last)


def put_back(out, start, weights, window):
    for i in range(CHUNK):
        put(out, start + i, total([w * window[i + j] for j, w in enumerate(weights)]))


def place(group, sign):
    at = lax.axis_index("ctx")
    if sign < 0:
        at = lax.axis_size("ctx") - 1 - at
    later = (at // group) % 2
    return (at % group).astype(F32), later.astype(F32)


def exclusive(before, other, lam, span, group, sign):
    at, later = place(group, sign)
    here = later * jnp.exp(lam * (at * -float(span))) * other.astype(F32)
    return here if before is None else before + here


def inclusive(own, other, lam, span, group, sign):
    _, later = place(group, sign)
    fall = -float(span * group)
    return jnp.exp(lam * ((1.0 - later) * fall)) * own + jnp.exp(lam * (later * fall)) * other.astype(F32)


def join_kernel(span, group, sign, first, own, other, lam, *refs):
    before, ends = (None, refs[-3:]) if first else (refs[0][...], refs[-3:])
    ends[0][...] = exclusive(before, other[...], lam[...], span, group, sign)
    ends[1][...] = inclusive(own[...], other[...], lam[...], span, group, sign)
    ends[2][...] = ends[1][...].astype(BF16)


def join_four_kernel(span, sign, own, first, second, third, lam, *refs):
    before, end, sent = refs[-3:]
    at, _ = place(4, sign)
    here = lax.axis_index("ctx") if sign > 0 else lax.axis_size("ctx") - 1 - lax.axis_index("ctx")
    here, rates = here % 4, lam[...]
    total_end = jnp.exp(rates * ((3.0 - at) * -float(span))) * own[...]
    total_before = None
    for k, other in enumerate((first, second, third)):
        there = (here ^ (k + 1)).astype(F32)
        earlier = jnp.where(there < at, 1.0, 0.0)
        gap = jnp.maximum(at - 1.0 - there, 0.0)
        value = other[...]
        share = earlier * jnp.exp(rates * (gap * -float(span))) * value
        total_before = share if total_before is None else total_before + share
        total_end = total_end + jnp.exp(rates * ((3.0 - there) * -float(span))) * value
    before[...] = total_before
    end[...] = total_end
    sent[...] = total_end.astype(BF16)


def add_four_kernel(own, first, second, third, *refs):
    refs[-1][...] = (own[...] + first[...]) + (second[...] + third[...])


def add_kernel(one, other, *refs):
    refs[-1][...] = one[...] + other[...]


def pack_kernel(span, group, modes, first_rows, half, before, other, lam, early, res, rate_sum, lag_sum, faded, a_next, gmy, f1, f2, gf0, alpha, kept, sent, heads):
    alpha[...] = exclusive(before[...], other[...], lam[...], span, group, -1)
    odd = lax.axis_index("ctx") % 2
    rows = (first_rows + modes) * SUB
    for out, start in ((kept, odd * half), (sent, (1 - odd) * half)):
        for b in range(half):
            source = pl.multiple_of((start + b) * (first_rows * SUB), SUB)
            out[pl.ds(b * rows, first_rows * SUB), :] = early[pl.ds(source, first_rows * SUB), :]
            source = pl.multiple_of((start + b) * (modes * SUB), SUB)
            mine = pl.ds(source, modes * SUB)
            lagged = rate_sum[mine, :] + jnp.exp(-lam[mine, :]) * alpha[mine, :] * lag_sum[mine, :]
            out[pl.ds(b * rows + first_rows * SUB, modes * SUB), :] = -res[mine, :] * lagged
    for b in range(2 * half):
        mine = slice(b * modes * SUB, (b + 1) * modes * SUB)
        far = jnp.exp(lam[mine, :] * -float(span - SUB))
        w, fade = faded[mine, :] * (a_next[mine, :] + far * alpha[mine, :]), jnp.exp(-lam[mine, :])
        here, grads = slice(b * span * SUB, (b * span + SUB) * SUB), []
        for t in range(SUB):
            grads.append(total([w[m * SUB : (m + 1) * SUB, :] for m in range(modes)]))
            w = fade * w
        grad = gmy[here, :] + jnp.concatenate(grads[::-1], axis=0)
        for which, value in enumerate((gf0[here, :], grad * f2[here, :], grad * f1[here, :])):
            heads[which, b] = value.astype(BF16)


def finish_kernel(modes, taps, half, early_rows, mine, other, late_mine, late_other, ready, short, res, rate, skip, gain, late, early):
    del ready
    block = pl.program_id(0)
    late[...] = late_mine[...] + late_other[...]
    own = jnp.where(lax.axis_index("ctx") % 2 == block // half, 1.0, 0.0)
    early[...] = own * mine[...] + (1.0 - own) * other[...]
    for s in range(SUB):
        lanes = slice(s * LANES, (s + 1) * LANES)
        short[0, :, lanes] = early[pl.ds(s, taps, stride=SUB), :]
        short[1, :, lanes] = late[pl.ds(s, taps, stride=SUB), :]
        short[2, :, lanes] = late[pl.ds(taps * SUB + s, taps, stride=SUB), :]
        res[:, lanes] = early[pl.ds(taps * SUB + s, modes, stride=SUB), :]
        rate[:, lanes] = early[pl.ds((taps + modes + 2) * SUB + s, modes, stride=SUB), :]
    skip[...] = row(early, taps + modes)
    gain[...] = row(early, taps + modes + 1)


def ring(value, axis, distance):
    count = lax.axis_size(axis)
    return lax.ppermute(value, axis, [(i, (i + distance) % count) for i in range(count)])


def swap(value, axis, step):
    return lax.ppermute(value, axis, [(i, i ^ step) for i in range(lax.axis_size(axis))])


def small(body, ins, after, outs, name):
    near = pl.BlockSpec(memory_space=pltpu.VMEM)
    ins = [pltpu.with_memory_space_constraint(v, pltpu.VMEM) if v.size > 1 << 18 else v for v in ins]
    return pl.pallas_call(
        body,
        in_specs=[near] * len(ins) + [pl.BlockSpec(memory_space=pl.ANY)] * len(after),
        out_specs=[near] * len(outs),
        out_shape=[jax.ShapeDtypeStruct(v, F32) if isinstance(v, tuple) else v for v in outs],
        compiler_params=pltpu.CompilerParams(vmem_limit_bytes=VMEM_LIMIT),
        cost_estimate=pl.CostEstimate(flops=ins[0].size, bytes_accessed=0, transcendentals=0),
        name=name,
    )(*ins, *after)


def scan_but_last(own, lam, span, sign, under):
    count, group, before = lax.axis_size("ctx"), 1, None
    under, sent = list(under), own
    outs = [own.shape, own.shape, jax.ShapeDtypeStruct(own.shape, BF16)]
    if count >= 8:
        ins = [own, *(swap(own, "ctx", k) for k in (1, 2, 3)), lam]
        body = functools.partial(join_four_kernel, span, sign)
        before, own, sent = small(body, ins, under, outs, "join")
        group, under = 4, []
    while True:
        other = swap(sent, "ctx", group)
        if 2 * group >= count:
            return before, other, group
        body = functools.partial(join_kernel, span, group, sign, before is None)
        ins = [own, other, lam] + ([] if before is None else [before])
        after = [under.pop(0)] if under else []
        before, own, sent = small(body, ins, after, outs, "join")
        group *= 2


def shards(
    residual, query_in, key_in, value_in, short_filter, residues, decay_rate, skip_gain, norm_gain, cotangent
):
    steps, channels = residual.shape
    modes, taps = residues.shape[0], short_filter.shape[1]
    blocks = channels // WIDE
    width = channels * lax.axis_size("tp")
    skip, gain = (v.reshape(blocks * SUB, LANES) for v in (skip_gain, norm_gain))

    def pos(count):
        return jax.ShapeDtypeStruct((blocks * count * SUB, LANES), F32)

    def kept(count):
        return pltpu.VMEM((blocks * count * SUB, LANES), F32)

    def pos_spec(count):
        return pl.BlockSpec((count * SUB, LANES), lambda h: (h, 0))

    def head_spec(total_steps, start):
        return pl.BlockSpec((SUB * SUB, LANES), lambda h: (h * (total_steps // SUB) + start, 0))

    wide_spec = pl.BlockSpec((steps, WIDE), lambda h: (0, h))
    wide = jax.ShapeDtypeStruct((steps, channels), BF16)
    mode_spec, one_spec, filt_spec = pos_spec(modes), pos_spec(1), pos_spec(3 * taps)
    seq_spec, ext_spec = pos_spec(steps), pos_spec(steps + SUB)
    seq, ext, mode, one = kept(steps), kept(steps + SUB), pos(modes), pos(1)
    eights, eights_spec = kept(steps // SUB * modes), pos_spec(steps // SUB * modes)
    halo_spec = pl.BlockSpec((3, SUB, WIDE), lambda h: (0, 0, h))
    param_spec = pl.BlockSpec((modes, WIDE), lambda h: (0, h))
    short_spec = pl.BlockSpec((3, taps, WIDE), lambda h: (0, 0, h))

    def call(body, ins, in_specs, outs, out_specs, ops, name, scratch=(), aliases=None):
        elements, n_refs = steps * channels, len(ins) + len(outs)

        def with_done(*refs):
            done = refs[n_refs]
            done[...] = jnp.zeros_like(done)
            body(*refs[:n_refs], *refs[n_refs + 1 :])

        near = blocks * steps * SUB
        ins = [
            pltpu.with_memory_space_constraint(v, pltpu.VMEM) if v.shape[0] >= near and v.dtype == F32 else v
            for v in ins
        ]
        done_shape = (SUB, LANES)
        outs = [*outs, jax.ShapeDtypeStruct(done_shape, F32)]
        out_specs = [*out_specs, pl.BlockSpec(done_shape, lambda h: (0, 0))]
        return pl.pallas_call(
            with_done,
            grid=(blocks,),
            in_specs=in_specs,
            out_specs=out_specs,
            out_shape=outs,
            scratch_shapes=list(scratch),
            input_output_aliases=aliases or {},
            compiler_params=pltpu.CompilerParams(
                dimension_semantics=("arbitrary",), vmem_limit_bytes=VMEM_LIMIT
            ),
            cost_estimate=pl.CostEstimate(
                flops=ops * elements, bytes_accessed=4 * elements, transcendentals=0
            ),
            name=name,
        )(*ins)

    far = [
        pltpu.with_memory_space_constraint(v, pltpu.HBM)
        for v in (residual, query_in, key_in, value_in, cotangent, short_filter, decay_rate, residues)
    ]
    last_spec = pl.BlockSpec((2 * SUB, channels), lambda h: (steps // (2 * SUB) - 1, 0))
    trailing = pl.pallas_call(
        trailing_kernel,
        grid=(1,),
        in_specs=[last_spec] * 3,
        out_specs=pl.BlockSpec((3, SUB, channels), lambda h: (0, 0, 0)),
        out_shape=jax.ShapeDtypeStruct((3, SUB, channels), BF16),
        compiler_params=pltpu.CompilerParams(vmem_limit_bytes=VMEM_LIMIT),
        cost_estimate=pl.CostEstimate(flops=channels, bytes_accessed=channels, transcendentals=0),
        name="trailing",
    )(*far[1:4])
    halo = ring(trailing, "ctx", 1)

    k_ext, v_ext, f1, f2, u, g, lam, res, faded, filt, x_part, _ = call(
        functools.partial(features_kernel, modes, taps, steps),
        (far[2], far[3], *far[5:]),
        [wide_spec, wide_spec, short_spec, param_spec, param_spec],
        [ext, ext, seq, seq, seq, eights, mode, mode, mode, pos(3 * taps), mode],
        [ext_spec, ext_spec, seq_spec, seq_spec, seq_spec, eights_spec, mode_spec, mode_spec, mode_spec, filt_spec, mode_spec],
        64,
        "features",
    )
    any_spec = pl.BlockSpec(memory_space=pl.ANY)
    k_ext, v_ext, f1, f2, u, g, x_own, _ = call(
        functools.partial(head_kernel, modes, taps, steps),
        (halo, k_ext, v_ext, filt, lam, x_part, f1, f2, u, g),
        [halo_spec, head_spec(steps + SUB, 1), head_spec(steps + SUB, 1), filt_spec, mode_spec, mode_spec]
        + [any_spec] * 4,
        [ext, ext, seq, seq, seq, eights, mode],
        [head_spec(steps + SUB, 0)] * 2
        + [head_spec(steps, 0)] * 3
        + [pl.BlockSpec((modes * SUB, LANES), lambda h: (h * (steps // SUB), 0)), mode_spec],
        2,
        "head",
        aliases={1: 0, 2: 1, 6: 2, 7: 3, 8: 4, 9: 5},
    )
    q_ext, f0, res_pos, cot_pos, query_done = call(
        functools.partial(query_kernel, taps, steps),
        (far[1], far[0], far[4], halo, filt),
        [wide_spec, wide_spec, wide_spec, halo_spec, filt_spec],
        [ext, seq, seq, seq],
        [ext_spec, seq_spec, seq_spec, seq_spec],
        30,
        "query",
    )
    y, near_done = call(
        functools.partial(near_kernel, modes, steps),
        (u, lam, res, skip),
        [seq_spec, mode_spec, mode_spec, one_spec],
        [seq],
        [seq_spec],
        10,
        "near",
    )
    own_lag, own_lag_done = call(
        functools.partial(lags_kernel, modes, steps),
        (u, lam),
        [seq_spec, mode_spec],
        [eights],
        [eights_spec],
        32,
        "lags",
    )
    before, other, group = scan_but_last(x_own, lam, steps, 1, [query_done, near_done])
    modal, summed, x_at, sums, _ = call(
        functools.partial(summed_kernel, modes, steps, blocks, group),
        (y, f0, res_pos, cot_pos, g, before, other, lam, faded, gain, own_lag_done),
        [seq_spec] * 4 + [eights_spec] + [mode_spec] * 4 + [one_spec, any_spec],
        [seq, seq, eights, jax.ShapeDtypeStruct((2, steps), F32)],
        [seq_spec, seq_spec, eights_spec, pl.BlockSpec((2, steps), lambda h: (0, 0))],
        50,
        "summed",
        scratch=[pltpu.VMEM((steps * SUB, LANES), F32)] * 2,
    )
    all_sums = [sums, *(swap(sums, "tp", k) for k in range(1, lax.axis_size("tp")))]
    lag, lag_sum, lags_done = call(
        functools.partial(borders_kernel, modes, steps),
        (own_lag, x_at, lam),
        [eights_spec, eights_spec, mode_spec],
        [eights, mode],
        [eights_spec, mode_spec],
        8,
        "borders",
    )
    scale_spec = pl.BlockSpec((2 * steps, LANES), lambda h: (0, 0))
    scale, gm, adj, a_own, a_next, _ = call(
        functools.partial(grad_modal_kernel, modes, steps, width, len(all_sums)),
        (*all_sums, summed, cot_pos, f0, lam, gain, lags_done),
        [pl.BlockSpec((2, steps), lambda h: (0, 0))] * len(all_sums)
        + [seq_spec, seq_spec, seq_spec, mode_spec, one_spec, any_spec],
        [pltpu.VMEM((2 * steps, LANES), F32), seq, eights, mode, mode],
        [scale_spec, seq_spec, eights_spec, mode_spec, mode_spec],
        45,
        "grad_modal",
    )
    res_part, rate_part, across_done = call(
        functools.partial(across_kernel, modes, steps),
        (gm, adj, x_at, lag, lam),
        [seq_spec, eights_spec, eights_spec, eights_spec, mode_spec],
        [mode, mode],
        [mode_spec, mode_spec],
        50,
        "across",
    )
    early_rows = taps + modes + 2
    gmy, rate_sum, gf0, early, _ = call(
        functools.partial(near_adjoint_kernel, modes, taps, steps),
        (gm, u, lam, res, skip, res_part, rate_part, scale, summed, cot_pos, modal, q_ext, gain),
        [seq_spec, seq_spec, mode_spec, mode_spec, one_spec, mode_spec, mode_spec, scale_spec, seq_spec, seq_spec, seq_spec, ext_spec, one_spec],
        [seq, mode, seq, pos(early_rows)],
        [seq_spec, mode_spec, seq_spec, pos_spec(early_rows)],
        55,
        "near_adjoint",
    )
    before, other, group = scan_but_last(a_own, lam, steps, -1, [across_done])

    half = blocks // 2
    half_shape = (half * (early_rows + modes) * SUB, LANES)
    alpha, kept_half, sent_half, heads = small(
        functools.partial(pack_kernel, steps, group, modes, early_rows, half),
        [before, other, lam, early, res, rate_sum, lag_sum, faded, a_next, gmy, f1, f2, gf0],
        [],
        [lam.shape, half_shape, half_shape, jax.ShapeDtypeStruct((3, blocks, SUB * SUB, LANES), BF16)],
        "pack",
    )
    early_rows += modes
    late_rows = 2 * taps
    next_spec = pl.BlockSpec((3, 1, SUB * SUB, LANES), lambda h: (0, h, 0, 0))
    other_half = swap(sent_half, "ctx", 1)
    next_head = ring(heads, "ctx", -1)
    gf1, gf2, mixed_done = call(
        functools.partial(mixed_kernel, modes, steps),
        (gmy, f1, f2, adj, lam, faded, alpha),
        [seq_spec] * 3 + [eights_spec] + [mode_spec] * 3,
        [seq, seq],
        [seq_spec, seq_spec],
        45,
        "mixed",
    )
    late, late_done = call(
        functools.partial(filter_sums_kernel, taps, steps),
        (gf1, gf2, k_ext, v_ext),
        [seq_spec, seq_spec, ext_spec, ext_spec],
        [pos(late_rows)],
        [pos_spec(late_rows)],
        30,
        "filter_sums",
    )

    last = lax.axis_size("ctx") - 1
    back_scratch = [pltpu.VMEM((steps * SUB, LANES), F32), pltpu.VMEM((SUB * SUB, LANES), F32)]
    normed, normed_done = call(
        functools.partial(normed_kernel, steps),
        (scale, summed, gain, mixed_done),
        [scale_spec, seq_spec, one_spec, any_spec],
        [wide],
        [wide_spec],
        10,
        "normed",
        scratch=back_scratch[:1],
    )
    grad_residual, grad_query, norm_done = call(
        functools.partial(residual_kernel, taps, steps, last),
        (scale, summed, cot_pos, gain, gf0, next_head, filt, late_done),
        [scale_spec, seq_spec, seq_spec, one_spec, seq_spec, next_spec, filt_spec, any_spec],
        [wide, wide],
        [wide_spec, wide_spec],
        35,
        "residual",
        scratch=back_scratch,
    )
    grad_key, grad_value, back_done = call(
        functools.partial(back_kernel, taps, steps, last),
        (gf1, gf2, next_head, filt),
        [seq_spec, seq_spec, next_spec, filt_spec],
        [wide, wide],
        [wide_spec, wide_spec],
        40,
        "back",
        scratch=back_scratch,
    )
    count, under = lax.axis_size("ctx"), [[late_done, normed_done], [norm_done]]
    mine = small(add_kernel, [kept_half, other_half], [mixed_done, next_head], [half_shape], "add")[0]
    step = 2
    while step < count:
        after = under.pop(0) if under else [norm_done]
        mine = small(add_kernel, [mine, swap(mine, "ctx", step)], after, [half_shape], "add")[0]
        step *= 2
    other = swap(mine, "ctx", 1)
    step = 1
    if count >= 8:
        ins = [late, *(swap(late, "ctx", k) for k in (1, 2, 3))]
        late = small(add_four_kernel, ins, [norm_done], [late.shape], "add")[0]
        step = 4
    late_other = swap(late, "ctx", step)
    while 2 * step < count:
        late = small(add_kernel, [late, late_other], [norm_done], [late.shape], "add")[0]
        step *= 2
        late_other = swap(late, "ctx", step)
    half_spec = pl.BlockSpec((early_rows * SUB, LANES), lambda h: (h % half, 0))
    late_spec = pos_spec(late_rows)
    grad_short, grad_residues, grad_rate, grad_skip, grad_gain, _ = call(
        functools.partial(finish_kernel, modes, taps, half, early_rows),
        (mine, other, late, late_other, back_done),
        [half_spec, half_spec, late_spec, late_spec, any_spec],
        [
            jax.ShapeDtypeStruct(short_filter.shape, F32),
            jax.ShapeDtypeStruct(residues.shape, F32),
            jax.ShapeDtypeStruct(residues.shape, F32),
            one,
            one,
        ],
        [short_spec, param_spec, param_spec, one_spec, one_spec],
        1,
        "finish",
        scratch=[
            pltpu.VMEM((late_rows * SUB, LANES), F32),
            pltpu.VMEM((early_rows * SUB, LANES), F32),
        ],
    )
    return (
        normed,
        grad_residual,
        grad_query,
        grad_key,
        grad_value,
        grad_short,
        grad_residues,
        grad_rate,
        grad_skip.reshape(channels),
        grad_gain.reshape(channels),
    )


def solution(mesh):
    both, modes, vector = P("ctx", "tp"), P(None, "tp"), P("tp")
    return jax.shard_map(
        shards,
        mesh=mesh,
        in_specs=(both, both, both, both, P(None, None, "tp"), modes, modes, vector, vector, both),
        out_specs=(both,) * 5 + (P(None, None, "tp"), modes, modes, vector, vector),
        check_vma=False,
    )
```
